128 devices in a mesh: ty: 8 (over y, core), tx: 16 (over x, z).
Axes of the slice: x: 4, y: 4, z: 4, core: 2. Of those that a mesh axis runs over, the one named last changes fastest.
Arguments:
- locations: float32 [8, 16, 3, 65536], P('ty', 'tx'), may hold values from -2.5 to 2.5
- solution: float32 [8, 16, 65536], P('ty', 'tx'), may hold values from -0.5 to 0.5
- cotangent: float32 [8, 16, 65536], P('ty', 'tx'), may hold values from -6 to 6
- block_fill: int32 [8, 16, 256], P('ty', 'tx'), may hold values from 64 to 256
- pair_own: int32 [8, 16, 192], P('ty', 'tx'), may hold values from 0 to 255
- pair_offset: int32 [8, 16, 192], P('ty', 'tx'), may hold values from 0 to 8, as said below
- pair_block: int32 [8, 16, 192], P('ty', 'tx'), may hold values from 0 to 255
- pair_count: int32 [8, 16], P('ty', 'tx'), may hold values from 24 to 192, as said below
Outputs:
- location_gradient: float32 [8, 16, 3, 65536], P('ty', 'tx')
The draws below stay inside these ranges and needn't reach their ends.
Inputs may be any that keep to these rules, and one draw needn't show every extreme that they name: `pair_offset`: the partner tile always lies inside the grid of 8 x 16 tiles. `pair_count`: slots at and past a tile's count carry no pair. Some tile fills all 192 slots.
All inputs are finite; a program needn't handle non-finite values.
Results may differ from the reference program's by a relative error of at most 0.0003.
Values sent between devices are 32-bit elements; how exact they have to be, the bound alone decides.
No kernel may reach another device: no remote copies, remote signals or barrier semaphores. Data moves between devices by JAX's collectives and lax.ppermute only.
A program may use at most 128 MiB of HBM per device.

```python
import jax
import jax.numpy as jnp
from jax import lax

BLOCKS_DEV = 256
PAIRS = 192
BLOCK_SIZE = 256
TILE_ROWS = 8
TILE_COLS = 16
POINTS_DEV = 65536


def draw_pair_offset(key, part):
    key = jax.random.fold_in(key, 23)
    row_key, col_key = jax.random.split(key)
    shape = (TILE_ROWS, TILE_COLS, PAIRS)
    row_step = jax.random.randint(row_key, shape, 0, 3, dtype=jnp.int32)
    col_step = jax.random.randint(col_key, shape, 0, 3, dtype=jnp.int32)
    tile_row = jnp.arange(TILE_ROWS, dtype=jnp.int32)[:, None, None]
    tile_col = jnp.arange(TILE_COLS, dtype=jnp.int32)[None, :, None]
    row_step = jnp.where(tile_row + row_step - 1 < 0, 1, row_step)
    row_step = jnp.where(tile_row + row_step - 1 >= TILE_ROWS, 1, row_step)
    col_step = jnp.where(tile_col + col_step - 1 < 0, 1, col_step)
    col_step = jnp.where(tile_col + col_step - 1 >= TILE_COLS, 1, col_step)
    return (row_step * 3 + col_step).astype(jnp.int32)


def draw_pair_count(key, part):
    key = jax.random.fold_in(key, 37)
    load_key, pick_key = jax.random.split(key)
    raw = jax.random.randint(load_key, (TILE_ROWS * TILE_COLS,), 0, PAIRS + 1, dtype=jnp.int32)
    counts = PAIRS // 8 + raw * raw // PAIRS * 7 // 8
    busiest = jax.random.randint(pick_key, (), 0, TILE_ROWS * TILE_COLS, dtype=jnp.int32)
    counts = counts.at[busiest].set(PAIRS)
    return counts.reshape(TILE_ROWS, TILE_COLS).astype(jnp.int32)


def touch_ends(values, rng, least, high):
    shape = values.shape
    index_at = [jax.random.randint(jax.random.fold_in(rng, axis), (), 0, shape[axis]) for axis in range(len(shape))]
    values = values.at[tuple(index_at)].set(least)
    longest = shape.index(max(shape))
    index_at[longest] = (index_at[longest] + 1) % shape[longest]
    return values.at[tuple(index_at)].set(high)


def levels(rng, dims, cuts, smallest, top_value):
    factor_of = 1.0
    for dim, shards_of in cuts:
        heights = jax.random.uniform(jax.random.fold_in(jax.random.fold_in(rng, 6), dim), (shards_of,), jnp.float32, smallest / len(cuts), top_value / len(cuts))
        factor_of = factor_of * jnp.repeat(jnp.exp(heights), dims[dim] // shards_of).reshape((-1,) + (1,) * (len(dims) - 1 - dim))
    return factor_of


def noise(stream_key, extent, spread, bound, cuts=(), held_as=jnp.bfloat16):
    entries = spread * jax.random.normal(stream_key, extent, jnp.float32)
    if cuts:
        entries = entries * levels(stream_key, extent, cuts, -0.22, 0.18)
    return jnp.clip(entries, -bound, bound).astype(held_as)


def setup_inputs(seed: int = 0) -> dict:
    key_of = jax.random.split(jax.random.key(seed), 9)
    return {
        "locations": noise(key_of[0], (TILE_ROWS, TILE_COLS, 3, POINTS_DEV), 0.35, 2.5, ((0, 8), (1, 16)), jnp.float32),
        "solution": noise(key_of[1], (TILE_ROWS, TILE_COLS, POINTS_DEV), 0.0625, 0.5, ((0, 8), (1, 16)), jnp.float32),
        "cotangent": noise(key_of[2], (TILE_ROWS, TILE_COLS, POINTS_DEV), 1.0, 6.0, ((0, 8), (1, 16)), jnp.float32),
        "block_fill": touch_ends(jax.random.randint(key_of[3], (TILE_ROWS, TILE_COLS, BLOCKS_DEV), 64, BLOCK_SIZE + 1), jax.random.fold_in(key_of[3], 1), 64, BLOCK_SIZE).astype(jnp.int32),
        "pair_own": touch_ends(jax.random.randint(key_of[4], (TILE_ROWS, TILE_COLS, PAIRS), 0, BLOCKS_DEV), jax.random.fold_in(key_of[4], 1), 0, BLOCKS_DEV - 1).astype(jnp.int32),
        "pair_offset": draw_pair_offset(jax.random.fold_in(key_of[8], 71), 0),
        "pair_block": touch_ends(jax.random.randint(key_of[6], (TILE_ROWS, TILE_COLS, PAIRS), 0, BLOCKS_DEV), jax.random.fold_in(key_of[6], 1), 0, BLOCKS_DEV - 1).astype(jnp.int32),
        "pair_count": draw_pair_count(jax.random.fold_in(key_of[8], 71), 0),
    }


def pair_terms(own_xyz, own_sol, own_cot, far_xyz, far_sol, far_cot, live_slot):
    offset = own_xyz[:, :, :, None] - far_xyz[:, :, None, :]
    distance = jnp.sqrt(lax.optimization_barrier(jnp.sum(offset * offset, axis=1)))
    reach = jnp.maximum(1.0 - distance, 0.0)
    coupling = own_cot[:, :, None] * far_sol[:, None, :] + own_sol[:, :, None] * far_cot[:, None, :]
    weight = -20.0 * reach * reach * reach * coupling * live_slot[:, None, None]
    own_push = own_xyz * lax.optimization_barrier(jnp.sum(weight, axis=2))[:, None, :] - jnp.einsum('gcj,gij->gci', far_xyz, weight, precision=lax.Precision.HIGHEST)
    far_push = far_xyz * lax.optimization_barrier(jnp.sum(weight, axis=1))[:, None, :] - jnp.einsum('gci,gij->gcj', own_xyz, weight, precision=lax.Precision.HIGHEST)
    return (own_push, far_push)

def reference(locations, solution, cotangent, block_fill, pair_own, pair_offset, pair_block, pair_count):
    position = jnp.arange(BLOCK_SIZE, dtype=jnp.int32)
    filled = (position[None, None, None, :] < block_fill[:, :, :, None]).astype(jnp.float32)
    filled = filled.reshape(TILE_ROWS, TILE_COLS, POINTS_DEV)
    packed = jnp.concatenate([locations, (solution * filled)[:, :, None], (cotangent * filled)[:, :, None]], axis=2)
    packed = packed.reshape(TILE_ROWS, TILE_COLS, 5, BLOCKS_DEV, BLOCK_SIZE)
    padded = jnp.pad(packed, ((1, 1), (1, 1), (0, 0), (0, 0), (0, 0)))
    tile_row = jnp.repeat(jnp.arange(TILE_ROWS, dtype=jnp.int32), TILE_COLS)
    tile_col = jnp.tile(jnp.arange(TILE_COLS, dtype=jnp.int32), TILE_ROWS)
    own_list = pair_own.reshape(TILE_ROWS * TILE_COLS, PAIRS)
    offset_list = pair_offset.reshape(TILE_ROWS * TILE_COLS, PAIRS)
    block_list = pair_block.reshape(TILE_ROWS * TILE_COLS, PAIRS)
    live_pairs = pair_count.reshape(TILE_ROWS * TILE_COLS)
    gradient = jnp.zeros((TILE_ROWS + 2, TILE_COLS + 2, 3, BLOCKS_DEV, BLOCK_SIZE), jnp.float32)

    def advance(gradient, slot):
        own_slot = own_list[:, slot]
        heading = offset_list[:, slot]
        far_slot = block_list[:, slot]
        live_slot = (slot < live_pairs).astype(jnp.float32)
        own_row = tile_row + 1
        own_col = tile_col + 1
        far_row = tile_row + heading // 3
        far_col = tile_col + heading % 3
        owned = padded[own_row, own_col, :, own_slot]
        partner = padded[far_row, far_col, :, far_slot]
        own_push, far_push = pair_terms(owned[:, :3], owned[:, 3], owned[:, 4], partner[:, :3], partner[:, 3], partner[:, 4], live_slot)
        gradient = gradient.at[own_row, own_col, :, own_slot].add(own_push)
        gradient = gradient.at[far_row, far_col, :, far_slot].add(far_push)
        return (gradient, None)
    gradient, _ = lax.scan(advance, gradient, jnp.arange(PAIRS, dtype=jnp.int32))
    return gradient[1:-1, 1:-1].reshape(TILE_ROWS, TILE_COLS, 3, POINTS_DEV)
```

```python
import jax
import jax.numpy as jnp
from jax import lax
from jax.experimental import pallas as pl
from jax.experimental.pallas import tpu as pltpu
from jax.sharding import PartitionSpec as P

lanes = 128
halves = 2
fields = 5
axes = 3
meta_rows = 8
bf16 = jnp.bfloat16
f32 = jnp.float32


def pack_kernel(slots, rows, own_ref, offset_ref, block_ref, count_ref, fill_ref, loc_ref, sol_ref, cot_ref,
                tile_ref, east_ref, west_ref, east_meta, west_meta, fill_meta, sem):
    tile_ref[0 : axes * rows, :] = loc_ref[...]
    tile_ref[axes * rows : (axes + 1) * rows, :] = sol_ref[...]
    tile_ref[(axes + 1) * rows : fields * rows, :] = cot_ref[...]
    slot_rows = halves * slots
    blocks = rows // halves

    def note_fill(b, carry):
        fill_meta[b // lanes, lax.rem(b, lanes)] = fill_ref[b].astype(f32)
        return carry

    lax.fori_loop(0, blocks, note_fill, 0)

    def place(out_ref, meta, at, s):
        a = own_ref[s]
        for h in range(halves):
            out_ref[pl.ds(halves * at + h, fields, stride=slot_rows), :] = tile_ref[
                pl.ds(halves * a + h, fields, stride=rows), :
            ]
        row, lane = at // lanes, lax.rem(at, lanes)
        meta[row, lane] = block_ref[s].astype(f32)
        meta[2 + row, lane] = fill_ref[a].astype(f32)
        meta[4 + row, lane] = (offset_ref[s] // 3).astype(f32)

    def step(s, carry):
        east_at, west_at = carry
        heading = lax.rem(offset_ref[s], 3)
        is_east = heading == 2
        is_west = heading == 0

        @pl.when(is_east)
        def _():
            place(east_ref, east_meta, east_at, s)

        @pl.when(is_west)
        def _():
            place(west_ref, west_meta, west_at, s)

        return east_at + is_east.astype(jnp.int32), west_at + is_west.astype(jnp.int32)

    east_n, west_n = lax.fori_loop(0, count_ref[0], step, (0, 0))
    east_meta[6, 0] = east_n.astype(f32)
    west_meta[6, 0] = west_n.astype(f32)
    copies = (
        pltpu.make_async_copy(east_meta, east_ref.at[pl.ds(fields * slot_rows, meta_rows)], sem.at[0]),
        pltpu.make_async_copy(west_meta, west_ref.at[pl.ds(fields * slot_rows, meta_rows)], sem.at[1]),
        pltpu.make_async_copy(fill_meta, tile_ref.at[pl.ds(fields * rows, meta_rows)], sem.at[2]),
    )
    for c in copies:
        c.start()
    for c in copies:
        c.wait()


def split3(x):
    high = x.astype(bf16).astype(f32)
    rest = x - high
    mid = rest.astype(bf16).astype(f32)
    low = (rest - mid).astype(bf16).astype(f32)
    return high, mid, low


def pair_kernel(slots, rows, own_ref, offset_ref, block_ref, count_ref, fill_ref,
                tile_ref, north_ref, south_ref, east_ref, west_ref,
                g_tile, g_north, g_south, g_east, g_west,
                src, grad, east_meta, west_meta, north_fill, south_fill,
                list_a, list_b, fill_a, fill_b, sem):
    slot_rows = halves * slots
    total = 3 * rows + 2 * slot_rows
    blocks = rows // halves
    east_base, west_base = 3 * blocks, 3 * blocks + slots
    copies = (
        pltpu.make_async_copy(east_ref.at[pl.ds(fields * slot_rows, meta_rows)], east_meta, sem.at[0]),
        pltpu.make_async_copy(west_ref.at[pl.ds(fields * slot_rows, meta_rows)], west_meta, sem.at[1]),
        pltpu.make_async_copy(north_ref.at[pl.ds(fields * rows, meta_rows)], north_fill, sem.at[2]),
        pltpu.make_async_copy(south_ref.at[pl.ds(fields * rows, meta_rows)], south_fill, sem.at[3]),
    )
    for c in copies:
        c.start()
    sections = ((north_ref, 0, rows), (tile_ref, rows, rows), (south_ref, 2 * rows, rows),
                (east_ref, 3 * rows, slot_rows), (west_ref, 3 * rows + slot_rows, slot_rows))
    for ref, base, size in sections:
        for f in range(fields):
            src[f * total + base : f * total + base + size, :] = ref[f * size : (f + 1) * size, :]
    grad[...] = jnp.zeros_like(grad)
    for c in copies:
        c.wait()

    def partner_fill(dr, block):
        row, lane = block // lanes, lax.rem(block, lanes)
        return jnp.where(
            dr == 1,
            fill_ref[block],
            jnp.where(dr == 0, north_fill[row, lane], south_fill[row, lane]).astype(jnp.int32),
        )

    def note(at, a, fa, dr, block):
        list_a[at] = a
        fill_a[at] = fa
        list_b[at] = dr * blocks + block
        fill_b[at] = partner_fill(dr, block)

    def own_step(s, at):
        heading = offset_ref[s]
        a = own_ref[s]
        note(at, blocks + a, fill_ref[a], heading // 3, block_ref[s])
        return at + (lax.rem(heading, 3) == 1).astype(jnp.int32)

    at = lax.fori_loop(0, count_ref[0], own_step, 0)
    for meta, base in ((east_meta, east_base), (west_meta, west_base)):
        n = meta[6, 0].astype(jnp.int32)

        def slot_step(k, at, meta=meta, base=base):
            row, lane = k // lanes, lax.rem(k, lanes)
            note(at, base + k, meta[2 + row, lane].astype(jnp.int32),
                 meta[4 + row, lane].astype(jnp.int32), meta[row, lane].astype(jnp.int32))
            return at + 1

        at = lax.fori_loop(0, n, slot_step, at)
    list_a[at] = blocks
    list_b[at] = blocks
    fill_a[at] = 0
    fill_b[at] = 0

    size = halves * lanes
    row_id = lax.broadcasted_iota(jnp.int32, (8, size), 0)
    lane_id = lax.broadcasted_iota(jnp.int32, (8, size), 1)
    is_xyz = row_id < axes
    is_one = row_id == fields
    unit = [(row_id == k).astype(f32) for k in range(axes)]
    zero8 = jnp.zeros((8, size), f32)
    one8 = jnp.ones((8, size), f32)

    def load(index, fill):
        parts = []
        for h in range(halves):
            got = src[pl.ds(halves * index + h, fields, stride=total), :]
            parts.append(jnp.concatenate([got, jnp.zeros((8 - fields, lanes), f32)], axis=0))
        x = jnp.concatenate(parts, axis=1)
        x = jnp.where(is_xyz | (lane_id < fill), x, 0.0)
        return jnp.where(is_one, 1.0, x)

    def weights(a, b):
        ah, am, al = split3(a)
        bh, bm, bl = split3(b)
        swapped = jnp.where(row_id == 3, jnp.roll(b, -1, axis=0), jnp.where(row_id == 4, jnp.roll(b, 1, axis=0), 0.0)) * -20.0
        sh, sm, sl = split3(swapped)
        left = jnp.concatenate([ah, am, al, one8, one8, one8, ah, ah, am, zero8], axis=0).astype(bf16)
        right = []
        for k in range(axes):
            u = unit[k]
            right.append(jnp.concatenate([u, u, u, -(u * bh), -(u * bm), -(u * bl), zero8, zero8, zero8, zero8], axis=0))
        right.append(jnp.concatenate([sh, sh, sh, zero8, zero8, zero8, sm, sl, sm, zero8], axis=0))
        outs = [
            lax.dot_general(left, r.astype(bf16), (((0,), (0,)), ((), ())), preferred_element_type=f32) for r in right
        ]
        square = outs[0] * outs[0] + outs[1] * outs[1] + outs[2] * outs[2]
        square = jnp.maximum(square, 1e-30)
        reach = jnp.maximum(1.0 - square * lax.rsqrt(square), 0.0)
        w = reach * reach * reach * outs[3]
        high = w.astype(bf16)
        low = (w - high.astype(f32)).astype(bf16)
        left_b = jnp.concatenate([bh, bm, bl, zero8], axis=0).astype(bf16)
        left_a = jnp.concatenate([ah, am, al, zero8], axis=0).astype(bf16)
        nt = (((1,), (1,)), ((), ()))
        nn = (((1,), (0,)), ((), ()))
        own = lax.dot_general(left_b, high, nt, preferred_element_type=f32) + lax.dot_general(
            left_b, low, nt, preferred_element_type=f32)
        far = lax.dot_general(left_a, high, nn, preferred_element_type=f32) + lax.dot_general(
            left_a, low, nn, preferred_element_type=f32)
        own = own[0:8] + own[8:16] + own[16:24]
        far = far[0:8] + far[8:16] + far[16:24]
        own = a[0:axes] * own[fields : fields + 1] - own[0:axes]
        far = b[0:axes] * far[fields : fields + 1] - far[0:axes]
        return own, far

    def add(index, push):
        for h in range(halves):
            at = pl.ds(halves * index + h, axes, stride=total)
            grad[at, :] = grad[at, :] + push[:, h * lanes : (h + 1) * lanes]

    def turn(t, carry):
        picks = []
        for u in range(2):
            k = 2 * t + u
            ia, ib = list_a[k], list_b[k]
            picks.append((ia, ib, load(ia, fill_a[k]), load(ib, fill_b[k])))
        pushes = [weights(a, b) for _, _, a, b in picks]
        for (ia, ib, _, _), (own, far) in zip(picks, pushes):
            add(ia, own)
            add(ib, far)
        return carry

    lax.fori_loop(0, (at + 1) // 2, turn, 0)
    outs = ((g_north, 0, rows), (g_tile, rows, rows), (g_south, 2 * rows, rows),
            (g_east, 3 * rows, slot_rows), (g_west, 3 * rows + slot_rows, slot_rows))
    for ref, base, n in outs:
        for f in range(axes):
            ref[f * n : (f + 1) * n, :] = grad[f * total + base : f * total + base + n, :]


def final_kernel(slots, rows, own_ref, offset_ref, count_ref, g_tile, g_north, g_south, g_east, g_west, out_ref):
    slot_rows = halves * slots
    out_ref[...] = g_tile[...] + g_north[...] + g_south[...]

    def merge(ref, at, s):
        for h in range(halves):
            place = pl.ds(halves * own_ref[s] + h, axes, stride=rows)
            out_ref[place, :] = out_ref[place, :] + ref[pl.ds(halves * at + h, axes, stride=slot_rows), :]

    def step(s, carry):
        east_at, west_at = carry
        heading = lax.rem(offset_ref[s], 3)
        is_east = heading == 2
        is_west = heading == 0

        @pl.when(is_east)
        def _():
            merge(g_east, east_at, s)

        @pl.when(is_west)
        def _():
            merge(g_west, west_at, s)

        return east_at + is_east.astype(jnp.int32), west_at + is_west.astype(jnp.int32)

    lax.fori_loop(0, count_ref[0], step, (0, 0))


def shifted(x, axis, by):
    devices = lax.axis_size(axis)
    pairs = [(i, i + by) for i in range(devices) if 0 <= i + by < devices]
    return lax.ppermute(x, axis, pairs)


def body(locations, solution, cotangent, block_fill, pair_own, pair_offset, pair_block, pair_count):
    points = solution.shape[2]
    slots = pair_own.shape[2]
    rows = points // lanes
    slot_rows = halves * slots
    total = 3 * rows + 2 * slot_rows
    loc = locations.reshape(axes * rows, lanes)
    sol = solution.reshape(rows, lanes)
    cot = cotangent.reshape(rows, lanes)
    own = pair_own.reshape(slots)
    offset = pair_offset.reshape(slots)
    block = pair_block.reshape(slots)
    count = pair_count.reshape(1)
    fill = block_fill.reshape(-1)
    vmem = pl.BlockSpec(memory_space=pltpu.VMEM)
    smem = pl.BlockSpec(memory_space=pltpu.SMEM)

    def sds(n):
        return jax.ShapeDtypeStruct((n, lanes), f32)

    meta = pltpu.SMEM((meta_rows, lanes), f32)
    tile, to_east, to_west = pl.pallas_call(
        lambda *refs: pack_kernel(slots, rows, *refs),
        out_shape=(sds(fields * rows + meta_rows), sds(fields * slot_rows + meta_rows), sds(fields * slot_rows + meta_rows)),
        in_specs=[smem] * 5 + [vmem] * 3,
        out_specs=(vmem,) * 3,
        scratch_shapes=[meta, meta, meta, pltpu.SemaphoreType.DMA((3,))],
        compiler_params=pltpu.CompilerParams(vmem_limit_bytes=16 << 20),
        name="pack",
    )(own, offset, block, count, fill, loc, sol, cot)
    from_west = shifted(to_east, "tx", 1)
    from_east = shifted(to_west, "tx", -1)
    north = shifted(tile, "ty", 1)
    south = shifted(tile, "ty", -1)
    listing = pltpu.SMEM((3 * slots + 8,), jnp.int32)
    g_tile, g_north, g_south, g_west, g_east = pl.pallas_call(
        lambda *refs: pair_kernel(slots, rows, *refs),
        out_shape=(sds(axes * rows),) * 3 + (sds(axes * slot_rows),) * 2,
        in_specs=[smem] * 5 + [vmem] * 5,
        out_specs=(vmem,) * 5,
        scratch_shapes=[pltpu.VMEM((fields * total, lanes), f32), pltpu.VMEM((axes * total, lanes), f32),
                        meta, meta, meta, meta, listing, listing, listing, listing, pltpu.SemaphoreType.DMA((4,))],
        compiler_params=pltpu.CompilerParams(vmem_limit_bytes=32 << 20),
        name="pairs",
    )(own, offset, block, count, fill, tile, north, south, from_west, from_east)
    back_east = shifted(g_west, "tx", -1)
    back_west = shifted(g_east, "tx", 1)
    back_south = shifted(g_north, "ty", -1)
    back_north = shifted(g_south, "ty", 1)
    out = pl.pallas_call(
        lambda *refs: final_kernel(slots, rows, *refs),
        out_shape=sds(axes * rows),
        in_specs=[smem] * 3 + [vmem] * 5,
        out_specs=vmem,
        compiler_params=pltpu.CompilerParams(vmem_limit_bytes=16 << 20),
        name="merge",
    )(own, offset, count, g_tile, back_north, back_south, back_east, back_west)
    return out.reshape(locations.shape)


def solution(mesh):
    placed = (
        P("ty", "tx", None, None),
        P("ty", "tx", None),
        P("ty", "tx", None),
        P("ty", "tx", None),
        P("ty", "tx", None),
        P("ty", "tx", None),
        P("ty", "tx", None),
        P("ty", "tx"),
    )
    return jax.shard_map(
        body, mesh=mesh, in_specs=placed, out_specs=P("ty", "tx", None, None), check_vma=False
    )
```

```python
import jax
import jax.numpy as jnp
from jax import lax
from jax.experimental import pallas as pl
from jax.experimental.pallas import tpu as pltpu
from jax.sharding import PartitionSpec as P

lanes = 128
halves = 2
fields = 5
axes = 3
meta_rows = 8
kinds = 6
group = (2, 2, 2, 2, 2, 2)
bf16 = jnp.bfloat16
f32 = jnp.float32
i32 = jnp.int32


def third(heading):
    return (heading * 11) >> 5


def tile_kernel(rows, fill_ref, loc_ref, sol_ref, cot_ref, tile_ref, sem):
    copies = (
        pltpu.make_async_copy(loc_ref, tile_ref.at[pl.ds(0, axes * rows)], sem.at[0]),
        pltpu.make_async_copy(sol_ref, tile_ref.at[pl.ds(axes * rows, rows)], sem.at[1]),
        pltpu.make_async_copy(cot_ref, tile_ref.at[pl.ds((axes + 1) * rows, rows)], sem.at[2]),
    )
    for c in copies:
        c.start()
    fill = fill_ref[...].astype(f32)
    tile_ref[fields * rows : fields * rows + meta_rows, :] = jnp.concatenate(
        [fill, jnp.zeros((meta_rows - halves, lanes), f32)], axis=0
    )
    for c in copies:
        c.wait()


def pack_kernel(slots, blocks, own_ref, offset_ref, block_ref, count_ref, fill_ref, tile_ref,
                east_ref, west_ref, east_meta, west_meta, sem):
    def place(out_ref, meta, at, s, dr):
        a = own_ref[s]
        for f in range(fields):
            out_ref[f * slots + at] = tile_ref[f * blocks + a]
        row, lane = at >> 7, at & 127
        meta[0, row, lane] = block_ref[s].astype(f32)
        meta[1, row, lane] = fill_ref[a].astype(f32)
        meta[2, row, lane] = dr.astype(f32)

    def step(s, carry):
        east_front, east_back, west_front, west_back = carry
        heading = offset_ref[s]
        dr = third(heading)
        dc = heading - 3 * dr
        level = dr == 1
        is_east = dc == 2
        is_west = dc == 0

        @pl.when(is_east)
        def _():
            place(east_ref, east_meta, jnp.where(level, slots - 1 - east_back, east_front), s, dr)

        @pl.when(is_west)
        def _():
            place(west_ref, west_meta, jnp.where(level, slots - 1 - west_back, west_front), s, dr)

        east, west = is_east.astype(i32), is_west.astype(i32)
        back = level.astype(i32)
        return (east_front + east * (1 - back), east_back + east * back,
                west_front + west * (1 - back), west_back + west * back)

    ends = lax.fori_loop(0, count_ref[0], step, (0, 0, 0, 0))
    east_meta[3, 0, 0] = ends[0].astype(f32)
    east_meta[3, 0, 1] = ends[1].astype(f32)
    west_meta[3, 0, 0] = ends[2].astype(f32)
    west_meta[3, 0, 1] = ends[3].astype(f32)
    copies = (
        pltpu.make_async_copy(east_meta, east_ref.at[pl.ds(fields * slots, meta_rows // halves)], sem.at[0]),
        pltpu.make_async_copy(west_meta, west_ref.at[pl.ds(fields * slots, meta_rows // halves)], sem.at[1]),
    )
    for c in copies:
        c.start()
    for c in copies:
        c.wait()


def sort_class(size_a, size_b):
    swap = size_a * (1 + size_b // 3) > size_b * (1 + size_a // 3)
    if swap:
        size_a, size_b = size_b, size_a
    return max(size_a - 2, 0) + (3 if size_b > 2 else 0), swap


def pair_loops(total, list_ref, table, ends, src, grad):
    def load(index, fill, parts):
        size = parts * lanes
        row_id = lax.broadcasted_iota(i32, (8, size), 0)
        lane_id = lax.broadcasted_iota(i32, (8, size), 1)
        pieces = []
        for h in range(parts):
            got = src[pl.ds(halves * index + h, fields, stride=total), :]
            pieces.append(jnp.concatenate([got, jnp.zeros((8 - fields, lanes), f32)], axis=0))
        x = jnp.concatenate(pieces, axis=1)
        return jnp.where((row_id < axes) | (lane_id < fill), x, 0.0)

    def split3(x):
        high = x.astype(bf16).astype(f32)
        rest = x - high
        mid = rest.astype(bf16).astype(f32)
        return high, mid, rest - mid

    def weights(a, b, steps):
        parts_a, parts_b = a.shape[1] // lanes, b.shape[1] // lanes
        zero = jnp.zeros((8, lanes), f32)
        row_b = lax.broadcasted_iota(jnp.int32, b.shape, 0)
        ah, am, al = split3(a)
        left = jnp.concatenate([ah, am, al, ah, ah, am], axis=0).astype(bf16)
        swapped = jnp.where(row_b == 3, jnp.roll(b, -1, axis=0), jnp.where(row_b == 4, jnp.roll(b, 1, axis=0), 0.0))
        sh, sm, sl = split3(swapped * -20.0)
        right = jnp.concatenate([sh, sh, sh, sm, sl, sm], axis=0).astype(bf16)
        row_id = lax.broadcasted_iota(jnp.int32, (8, lanes), 0)
        units = [(row_id == f).astype(f32) for f in range(axes)]
        spread = jnp.concatenate([jnp.concatenate([u, u, u, zero, zero, zero], axis=0) for u in units], axis=1).astype(bf16)
        mixed = lax.dot_general(left, jnp.concatenate([spread, right], axis=1), (((0,), (0,)), ((), ())),
                                preferred_element_type=f32)
        b_rows = [
            [jnp.broadcast_to(b[f : f + 1, h * lanes : (h + 1) * lanes], (8, lanes)) for f in range(axes)]
            for h in range(parts_b)
        ]
        far = [[None] * axes for _ in range(parts_b)]
        own = [[] for _ in range(axes)]
        for g in range(steps):
            tile = mixed[8 * g : 8 * g + 8]
            a_cols = [tile[:, f * lanes : (f + 1) * lanes] for f in range(axes)]
            mine = [None] * axes
            for p in range(parts_b):
                diff = [a_cols[f] - b_rows[p][f] for f in range(axes)]
                square = diff[0] * diff[0] + diff[1] * diff[1] + diff[2] * diff[2]
                square = jnp.maximum(square, 1e-30)
                reach = jnp.maximum(1.0 - square * lax.rsqrt(square), 0.0)
                w = (reach * reach) * (reach * tile[:, (axes + p) * lanes : (axes + p + 1) * lanes])
                for f in range(axes):
                    push = w * diff[f]
                    mine[f] = push if p == 0 else mine[f] + push
                    far[p][f] = push if g == 0 else far[p][f] + push
            for f in range(axes):
                own[f].append(mine[f])
        own_rows = []
        for f in range(axes):
            halves_out = []
            for h in range(parts_a):
                tiles = own[f][16 * h : 16 * h + 16]
                tiles = tiles + [jnp.zeros((8, lanes), f32)] * (16 - len(tiles))
                turned = jnp.concatenate(tiles, axis=0).T
                halves_out.append(jnp.sum(turned, axis=0, keepdims=True))
            own_rows.append(jnp.concatenate(halves_out, axis=1))
        far_rows = [
            jnp.concatenate([jnp.sum(far[p][f], axis=0, keepdims=True) for p in range(parts_b)], axis=1)
            for f in range(axes)
        ]
        return jnp.concatenate(own_rows, axis=0), -jnp.concatenate(far_rows, axis=0)

    def add(index, push):
        for h in range(push.shape[1] // lanes):
            at = pl.ds(halves * index + h, axes, stride=total)
            grad[at, :] = grad[at, :] + push[:, h * lanes : (h + 1) * lanes]

    for k in range(kinds):
        steps = 16 + 8 * (k % 3)
        parts_a, parts_b = -(-steps // 16), 1 + k // 3
        end = ends[k]

        def turn(t, carry, k=k, steps=steps, parts_a=parts_a, parts_b=parts_b, end=end):
            picks = []
            for u in range(group[k]):
                at = group[k] * t + u
                word = list_ref[k, at]
                ia, ib = word & 4095, word >> 12
                fa = jnp.where(at < end, table[ia >> 7, ia & 127], 0)
                fb = jnp.where(at < end, table[ib >> 7, ib & 127], 0)
                picks.append((ia, ib, load(ia, fa, parts_a), load(ib, fb, parts_b)))
            pushes = [weights(a, b, steps) for _, _, a, b in picks]
            for (ia, ib, _, _), (own, far) in zip(picks, pushes):
                add(ia, own)
                add(ib, far)
            return carry

        lax.fori_loop(0, (end + group[k] - 1) // group[k], turn, 0)


def start_lists(classes, ends):
    for size_a in range(5):
        for size_b in range(5):
            kind, swap = sort_class(size_a, size_b)
            classes[size_a * 8 + size_b] = kind + (8 if swap else 0)
    for k in range(kinds):
        ends[k] = 0


def note(classes, ends, list_ref, table, a, b, live):
    size_a = (table[a >> 7, a & 127] + 63) >> 6
    size_b = (table[b >> 7, b & 127] + 63) >> 6
    found = classes[size_a * 8 + size_b]
    kind = found & 7
    at = ends[kind]
    list_ref[kind, at] = jnp.where(found > 7, b | (a << 12), a | (b << 12))
    ends[kind] = at + live


def close_lists(ends, list_ref, spare):
    for k in range(kinds):
        for u in range(group[k] - 1):
            list_ref[k, ends[k] + u] = spare | (spare << 12)


def as_table(pieces, table_v, table, sem):
    at = 0
    for piece in pieces:
        table_v[at : at + piece.shape[0], :] = piece
        at += piece.shape[0]
    copy = pltpu.make_async_copy(table_v, table, sem)
    copy.start()
    return copy


def own_kernel(rows, total, own_ref, offset_ref, block_ref, count_ref, fill_ref,
               tile_ref, north_ref, south_ref, g_tile, g_north, g_south,
               src, grad, table_v, table, list_ref, classes, ends, sem):
    blocks = rows // halves
    north_fill = north_ref[fields * rows : fields * rows + halves, :].astype(i32)
    south_fill = south_ref[fields * rows : fields * rows + halves, :].astype(i32)
    copy = as_table((north_fill, fill_ref[...], south_fill, jnp.zeros((10, lanes), i32)), table_v, table, sem)
    start_lists(classes, ends)
    for ref, base in ((north_ref, 0), (tile_ref, rows), (south_ref, 2 * rows)):
        for f in range(fields):
            src[f * total + base : f * total + base + rows, :] = ref[f * rows : (f + 1) * rows, :]
    for f in range(axes):
        grad[f * total : f * total + 3 * rows, :] = jnp.zeros((3 * rows, lanes), f32)
    copy.wait()

    def step(s, carry):
        heading = offset_ref[s]
        dr = third(heading)
        live = (heading - 3 * dr == 1).astype(i32)
        note(classes, ends, list_ref, table, blocks + own_ref[s], dr * blocks + block_ref[s], live)
        return carry

    lax.fori_loop(0, count_ref[0], step, 0)
    close_lists(ends, list_ref, blocks)
    pair_loops(total, list_ref, table, ends, src, grad)
    for ref, base in ((g_north, 0), (g_tile, rows), (g_south, 2 * rows)):
        for f in range(axes):
            ref[f * rows : (f + 1) * rows, :] = grad[f * total + base : f * total + base + rows, :]


def side_kernel(slots, rows, total, level, fill_ref, tiles, east_ref, west_ref, g_tiles, g_east, g_west,
                o_tiles, o_east, o_west, src, grad, table_v, table, list_ref, classes, ends, sem):
    blocks = rows // halves
    slot_rows = halves * slots
    bases = (rows,) if level else (0, 2 * rows)
    fills = [jnp.zeros((halves, lanes), i32)] * 3
    if level:
        fills[1] = fill_ref[...]
    else:
        fills[0], fills[2] = (t[fields * rows : fields * rows + halves, :].astype(i32) for t in tiles)
    metas = [ref[fields * slot_rows : fields * slot_rows + meta_rows, :] for ref in (east_ref, west_ref)]
    partners = [(m[4:6] * blocks + m[0:2]).astype(i32) for m in metas]
    counts = jnp.concatenate([m[6:7].astype(i32) for m in metas], axis=0)
    copy = as_table((*fills, metas[0][2:4].astype(i32), metas[1][2:4].astype(i32), *partners, counts), table_v, table, sem)
    start_lists(classes, ends)
    east_base, west_base = 6 * lanes, 8 * lanes
    slot_places = ((east_ref, halves * east_base), (west_ref, halves * west_base))
    for ref, base in zip(tiles, bases):
        for f in range(fields):
            src[f * total + base : f * total + base + rows, :] = ref[f * rows : (f + 1) * rows, :]
    for ref, base in slot_places:
        for f in range(fields):
            src[f * total + base : f * total + base + slot_rows, :] = ref[f * slot_rows : (f + 1) * slot_rows, :]
    for ref, base in zip(g_tiles, bases):
        for f in range(axes):
            grad[f * total + base : f * total + base + rows, :] = ref[f * rows : (f + 1) * rows, :]
    for ref, (_, base) in zip((g_east, g_west), slot_places):
        for f in range(axes):
            init = jnp.zeros((slot_rows, lanes), f32) if ref is None else ref[f * slot_rows : (f + 1) * slot_rows, :]
            grad[f * total + base : f * total + base + slot_rows, :] = init
    copy.wait()
    for side, base in ((0, east_base), (1, west_base)):
        if level:
            first, last = slots - table[14 + side, 1], slots
        else:
            first, last = 0, table[14 + side, 0]

        def step(k, carry, side=side, base=base):
            b = table[10 + 2 * side + (k >> 7), k & 127]
            note(classes, ends, list_ref, table, base + k, b, 1)
            return carry

        lax.fori_loop(first, last, step, 0)
    close_lists(ends, list_ref, bases[0] // halves)
    pair_loops(total, list_ref, table, ends, src, grad)
    for ref, base in zip(o_tiles, bases):
        for f in range(axes):
            ref[f * rows : (f + 1) * rows, :] = grad[f * total + base : f * total + base + rows, :]
    for ref, (_, base) in zip((o_east, o_west), slot_places):
        for f in range(axes):
            ref[f * slot_rows : (f + 1) * slot_rows, :] = grad[f * total + base : f * total + base + slot_rows, :]


def merge_kernel(slots, blocks, own_ref, offset_ref, count_ref, g_tile, g_north, g_south, g_east, g_west, out_ref):
    out_ref[...] = g_tile[...] + g_north[...] + g_south[...]

    def merge(ref, at, s):
        a = own_ref[s]
        for f in range(axes):
            out_ref[f * blocks + a] = out_ref[f * blocks + a] + ref[f * slots + at]

    def step(s, carry):
        east_front, east_back, west_front, west_back = carry
        heading = offset_ref[s]
        dr = third(heading)
        dc = heading - 3 * dr
        level = dr == 1
        is_east = dc == 2
        is_west = dc == 0

        @pl.when(is_east)
        def _():
            merge(g_east, jnp.where(level, slots - 1 - east_back, east_front), s)

        @pl.when(is_west)
        def _():
            merge(g_west, jnp.where(level, slots - 1 - west_back, west_front), s)

        east, west = is_east.astype(i32), is_west.astype(i32)
        back = level.astype(i32)
        return (east_front + east * (1 - back), east_back + east * back,
                west_front + west * (1 - back), west_back + west * back)

    lax.fori_loop(0, count_ref[0], step, (0, 0, 0, 0))


def shifted(x, axis, by):
    devices = lax.axis_size(axis)
    pairs = [(i, i + by) for i in range(devices) if 0 <= i + by < devices]
    return lax.ppermute(x, axis, pairs)


vmem = pl.BlockSpec(memory_space=pltpu.VMEM)
smem = pl.BlockSpec(memory_space=pltpu.SMEM)
anywhere = pl.BlockSpec(memory_space=pl.ANY)


def sds(n):
    return jax.ShapeDtypeStruct((n, lanes), f32)


def params(mib):
    return pltpu.CompilerParams(vmem_limit_bytes=mib << 20)


def pair_scratch(total, length):
    return [
        pltpu.VMEM((fields * total, lanes), f32),
        pltpu.VMEM((axes * total, lanes), f32),
        pltpu.VMEM((16, lanes), i32),
        pltpu.SMEM((16, lanes), i32),
        pltpu.SMEM((kinds, length), i32),
        pltpu.SMEM((64,), i32),
        pltpu.SMEM((8,), i32),
        pltpu.SemaphoreType.DMA,
    ]


def own_call(slots, rows, own, offset, block, count, fill2, tile, north, south):
    total = 3 * rows
    return pl.pallas_call(
        lambda *refs: own_kernel(rows, total, *refs),
        out_shape=(sds(axes * rows),) * 3,
        in_specs=[smem] * 4 + [vmem] * 4,
        out_specs=(vmem,) * 3,
        scratch_shapes=pair_scratch(total, slots + 8),
        compiler_params=params(24),
        name="pairs_own",
    )(own, offset, block, count, fill2, tile, north, south)


def side_call(slots, rows, level, fill2, tiles, east, west, g_tiles, g_slots):
    total = 3 * rows + 4 * halves * lanes
    n, m = len(tiles), len(g_slots)

    def run(*refs):
        refs = list(refs)
        take = lambda k: [refs.pop(0) for _ in range(k)]
        (fill_ref,), t = take(1), take(n)
        e, w = take(2)
        g = take(n)
        ge, gw = take(2) if m else (None, None)
        o = take(n)
        oe, ow = take(2)
        side_kernel(slots, rows, total, level, fill_ref, t, e, w, g, ge, gw, o, oe, ow, *refs)

    return pl.pallas_call(
        run,
        out_shape=(sds(axes * rows),) * n + (sds(axes * halves * slots),) * 2,
        in_specs=[vmem] * (1 + n + 2 + n + m),
        out_specs=(vmem,) * (n + 2),
        scratch_shapes=pair_scratch(total, 2 * slots + 8),
        compiler_params=params(32),
        name="pairs_level" if level else "pairs_cross",
    )(fill2, *tiles, east, west, *g_tiles, *g_slots)


def body(locations, solution, cotangent, block_fill, pair_own, pair_offset, pair_block, pair_count):
    points = solution.shape[2]
    slots = pair_own.shape[2]
    rows = points // lanes
    blocks = rows // halves
    own = pair_own.reshape(slots)
    offset = pair_offset.reshape(slots)
    block = pair_block.reshape(slots)
    count = pair_count.reshape(1)
    fill = block_fill.reshape(blocks)
    fill2 = block_fill.reshape(halves, lanes)
    tile_rows = fields * rows + meta_rows
    slot_rows = fields * halves * slots + meta_rows

    def paired(n):
        return jax.ShapeDtypeStruct((n // halves, halves, lanes), f32)

    tile = pl.pallas_call(
        lambda *refs: tile_kernel(rows, *refs),
        out_shape=sds(tile_rows),
        in_specs=[vmem] + [anywhere] * 3,
        out_specs=vmem,
        scratch_shapes=[pltpu.SemaphoreType.DMA((3,))],
        compiler_params=params(8),
        name="tile",
    )(fill2, locations.reshape(axes * rows, lanes), solution.reshape(rows, lanes), cotangent.reshape(rows, lanes))
    north = shifted(tile, "ty", 1)
    south = shifted(tile, "ty", -1)
    meta = pltpu.SMEM((meta_rows // halves, halves, lanes), f32)
    to_east, to_west = pl.pallas_call(
        lambda *refs: pack_kernel(slots, blocks, *refs),
        out_shape=(paired(slot_rows),) * 2,
        in_specs=[smem] * 5 + [vmem],
        out_specs=(vmem,) * 2,
        scratch_shapes=[meta, meta, pltpu.SemaphoreType.DMA((2,))],
        compiler_params=params(16),
        name="pack",
    )(own, offset, block, count, fill, tile.reshape(tile_rows // halves, halves, lanes))
    from_west = shifted(to_east, "tx", 1).reshape(slot_rows, lanes)
    from_east = shifted(to_west, "tx", -1).reshape(slot_rows, lanes)
    g_tile, g_north, g_south = own_call(slots, rows, own, offset, block, count, fill2, tile, north, south)
    g_north, g_south, g_west, g_east = side_call(
        slots, rows, False, fill2, (north, south), from_west, from_east, (g_north, g_south), ())
    back_south = shifted(g_north, "ty", -1)
    back_north = shifted(g_south, "ty", 1)
    g_tile, g_west, g_east = side_call(
        slots, rows, True, fill2, (tile,), from_west, from_east, (g_tile,), (g_west, g_east))
    back_east = shifted(g_west, "tx", -1)
    back_west = shifted(g_east, "tx", 1)
    views = [x.reshape(-1, halves, lanes) for x in (g_tile, back_north, back_south, back_east, back_west)]
    out = pl.pallas_call(
        lambda *refs: merge_kernel(slots, blocks, *refs),
        out_shape=paired(axes * rows),
        in_specs=[smem] * 3 + [vmem] * 5,
        out_specs=vmem,
        compiler_params=params(16),
        name="merge",
    )(own, offset, count, *views)
    return out.reshape(locations.shape)


def solution(mesh):
    placed = (
        P("ty", "tx", None, None),
        P("ty", "tx", None),
        P("ty", "tx", None),
        P("ty", "tx", None),
        P("ty", "tx", None),
        P("ty", "tx", None),
        P("ty", "tx", None),
        P("ty", "tx"),
    )
    return jax.shard_map(
        body, mesh=mesh, in_specs=placed, out_specs=P("ty", "tx", None, None), check_vma=False
    )
```

```python
import jax
import jax.numpy as jnp
from jax import lax
from jax.experimental import pallas as pl
from jax.experimental.pallas import tpu as pltpu
from jax.sharding import PartitionSpec as P

lanes = 128
halves = 2
fields = 5
axes = 3
meta_rows = 8
kinds = 5
bf16 = jnp.bfloat16
f32 = jnp.float32
i32 = jnp.int32


def third(heading):
    return (heading * 11) >> 5


def tile_kernel(rows, fill_ref, loc_ref, sol_ref, cot_ref, tile_ref, sem):
    copies = (
        pltpu.make_async_copy(loc_ref, tile_ref.at[pl.ds(0, axes * rows)], sem.at[0]),
        pltpu.make_async_copy(sol_ref, tile_ref.at[pl.ds(axes * rows, rows)], sem.at[1]),
        pltpu.make_async_copy(cot_ref, tile_ref.at[pl.ds((axes + 1) * rows, rows)], sem.at[2]),
    )
    for c in copies:
        c.start()
    fill = fill_ref[...].astype(f32)
    tile_ref[fields * rows : fields * rows + meta_rows, :] = jnp.concatenate(
        [fill, jnp.zeros((meta_rows - halves, lanes), f32)], axis=0
    )
    for c in copies:
        c.wait()


def pack_kernel(slots, blocks, own_ref, offset_ref, block_ref, count_ref, fill_ref, tile_ref,
                east_ref, west_ref, east_meta, west_meta, sem):
    def place(out_ref, meta, at, s, dr):
        a = own_ref[s]
        for f in range(fields):
            out_ref[f * slots + at] = tile_ref[f * blocks + a]
        row, lane = at >> 7, at & 127
        meta[0, row, lane] = block_ref[s].astype(f32)
        meta[1, row, lane] = fill_ref[a].astype(f32)
        meta[2, row, lane] = dr.astype(f32)

    def step(s, carry):
        east_front, east_back, west_front, west_back = carry
        heading = offset_ref[s]
        dr = third(heading)
        dc = heading - 3 * dr
        level = dr == 1
        is_east = dc == 2
        is_west = dc == 0

        @pl.when(is_east)
        def _():
            place(east_ref, east_meta, jnp.where(level, slots - 1 - east_back, east_front), s, dr)

        @pl.when(is_west)
        def _():
            place(west_ref, west_meta, jnp.where(level, slots - 1 - west_back, west_front), s, dr)

        east, west = is_east.astype(i32), is_west.astype(i32)
        back = level.astype(i32)
        return (east_front + east * (1 - back), east_back + east * back,
                west_front + west * (1 - back), west_back + west * back)

    ends = lax.fori_loop(0, count_ref[0], step, (0, 0, 0, 0))
    east_meta[3, 0, 0] = ends[0].astype(f32)
    east_meta[3, 0, 1] = ends[1].astype(f32)
    west_meta[3, 0, 0] = ends[2].astype(f32)
    west_meta[3, 0, 1] = ends[3].astype(f32)
    copies = (
        pltpu.make_async_copy(east_meta, east_ref.at[pl.ds(fields * slots, meta_rows // halves)], sem.at[0]),
        pltpu.make_async_copy(west_meta, west_ref.at[pl.ds(fields * slots, meta_rows // halves)], sem.at[1]),
    )
    for c in copies:
        c.start()
    for c in copies:
        c.wait()


def sort_class(size_a, size_b):
    swap = size_a * (1 + size_b // 3) > size_b * (1 + size_a // 3) or (size_a > 3 and size_b < 3)
    if swap:
        size_a, size_b = size_b, size_a
    return max(size_a - 2, 0) + (2 if size_b > 2 else 0), swap


def shape_of(kind):
    steps = (16, 24, 16, 24, 32)[kind]
    return steps, -(-steps // 16), (1, 1, 2, 2, 2)[kind]


def pair_loops(total, spare, list_ref, table, ends, src, grad, buffers):
    size = halves * lanes

    def load(index, fill, parts):
        size = parts * lanes
        row_id = lax.broadcasted_iota(i32, (8, size), 0)
        lane_id = lax.broadcasted_iota(i32, (8, size), 1)
        pieces = []
        for h in range(parts):
            got = src[pl.ds(halves * index + h, fields, stride=total), :]
            pieces.append(jnp.concatenate([got, jnp.zeros((8 - fields, lanes), f32)], axis=0))
        x = jnp.concatenate(pieces, axis=1)
        return jnp.where((row_id < axes) | (lane_id < fill), x, 0.0)

    def split3(x):
        high = x.astype(bf16).astype(f32)
        rest = x - high
        mid = rest.astype(bf16).astype(f32)
        return high, mid, rest - mid

    def spread(k, at, mixed, partner):
        steps, parts_a, parts_b = shape_of(k)
        word = list_ref[k, at]
        ia, ib = word & 4095, word >> 12
        live = at < ends[k]
        a = load(ia, jnp.where(live, table[ia >> 7, ia & 127], 0), parts_a)
        b = load(ib, jnp.where(live, table[ib >> 7, ib & 127], 0), parts_b)
        partner[:, : parts_b * lanes] = b
        zero = jnp.zeros((8, lanes), f32)
        row_b = lax.broadcasted_iota(i32, b.shape, 0)
        ah, am, al = split3(a)
        left = jnp.concatenate([ah, am, al, ah, ah, am], axis=0).astype(bf16)
        swapped = jnp.where(row_b == 3, jnp.roll(b, -1, axis=0), jnp.where(row_b == 4, jnp.roll(b, 1, axis=0), 0.0))
        sh, sm, sl = split3(swapped * -20.0)
        right = jnp.concatenate([sh, sh, sh, sm, sl, sm], axis=0).astype(bf16)
        row_id = lax.broadcasted_iota(i32, (8, lanes), 0)
        units = [(row_id == f).astype(f32) for f in range(axes)]
        pick = jnp.concatenate([jnp.concatenate([u, u, u, zero, zero, zero], axis=0) for u in units], axis=1).astype(bf16)
        mixed[: parts_a * lanes, : (axes + parts_b) * lanes] = lax.dot_general(
            left, jnp.concatenate([pick, right], axis=1), (((0,), (0,)), ((), ())), preferred_element_type=f32)

    def work(k, mixed, partner, own, far):
        steps, parts_a, parts_b = shape_of(k)
        b_rows = [
            [jnp.broadcast_to(partner[f : f + 1, p * lanes : (p + 1) * lanes], (8, lanes)) for f in range(axes)]
            for p in range(parts_b)
        ]
        sums = [[None] * axes for _ in range(parts_b)]
        for g in range(steps):
            rows = slice(8 * g, 8 * g + 8)
            a_cols = [mixed[rows, f * lanes : (f + 1) * lanes] for f in range(axes)]
            mine = [None] * axes
            for p in range(parts_b):
                diff = [a_cols[f] - b_rows[p][f] for f in range(axes)]
                square = diff[0] * diff[0] + diff[1] * diff[1] + diff[2] * diff[2]
                square = jnp.maximum(square, 1e-30)
                reach = jnp.maximum(1.0 - square * lax.rsqrt(square), 0.0)
                w = (reach * reach) * (reach * mixed[rows, (axes + p) * lanes : (axes + p + 1) * lanes])
                for f in range(axes):
                    push = w * diff[f]
                    mine[f] = push if p == 0 else mine[f] + push
                    sums[p][f] = push if g == 0 else sums[p][f] + push
            for f in range(axes):
                own[f * size + 8 * g : f * size + 8 * g + 8, :] = mine[f]
        for p in range(parts_b):
            for f in range(axes):
                far[8 * f : 8 * f + 8, p * lanes : (p + 1) * lanes] = sums[p][f]

    def finish(k, at, own, far):
        steps, parts_a, parts_b = shape_of(k)
        word = jnp.where(at < 0, spare | (spare << 12), list_ref[k, jnp.maximum(at, 0)])
        ia, ib = word & 4095, word >> 12
        for h in range(parts_a):
            count = min(lanes, 8 * steps - h * lanes)
            rows = []
            for f in range(axes):
                part = own[f * size + h * lanes : f * size + h * lanes + count, :]
                if count < lanes:
                    part = jnp.concatenate([part, jnp.zeros((lanes - count, lanes), f32)], axis=0)
                rows.append(jnp.sum(part.T, axis=0, keepdims=True))
            place = pl.ds(halves * ia + h, axes, stride=total)
            grad[place, :] = grad[place, :] + jnp.concatenate(rows, axis=0)
        for p in range(parts_b):
            rows = [jnp.sum(far[8 * f : 8 * f + 8, p * lanes : (p + 1) * lanes], axis=0, keepdims=True) for f in range(axes)]
            place = pl.ds(halves * ib + p, axes, stride=total)
            grad[place, :] = grad[place, :] - jnp.concatenate(rows, axis=0)

    mixed0, mixed1, partner0, partner1, own0, own1, far0, far1 = buffers
    for k in range(kinds):
        turns = (ends[k] + 1) // 2

        def turn(t, carry, k=k):
            at = 2 * t
            finish(k, at - 1, own1, far1)
            work(k, mixed0, partner0, own0, far0)
            spread(k, at + 1, mixed1, partner1)
            finish(k, at, own0, far0)
            work(k, mixed1, partner1, own1, far1)
            spread(k, at + 2, mixed0, partner0)
            return carry

        @pl.when(turns > 0)
        def _(k=k, turns=turns, turn=turn):
            spread(k, 0, mixed0, partner0)
            lax.fori_loop(0, turns, turn, 0)
            finish(k, 2 * turns - 1, own1, far1)


def start_lists(classes, ends):
    for size_a in range(5):
        for size_b in range(5):
            kind, swap = sort_class(size_a, size_b)
            classes[size_a * 8 + size_b] = kind + (8 if swap else 0)
    for k in range(kinds):
        ends[k] = 0


def note(classes, ends, list_ref, table, a, b, live):
    size_a = (table[a >> 7, a & 127] + 63) >> 6
    size_b = (table[b >> 7, b & 127] + 63) >> 6
    found = classes[size_a * 8 + size_b]
    kind = found & 7
    at = ends[kind]
    list_ref[kind, at] = jnp.where(found > 7, b | (a << 12), a | (b << 12))
    ends[kind] = at + live


def close_lists(ends, list_ref, spare):
    for k in range(kinds):
        for u in range(3):
            list_ref[k, ends[k] + u] = spare | (spare << 12)


def as_table(pieces, table_v, table, sem):
    at = 0
    for piece in pieces:
        table_v[at : at + piece.shape[0], :] = piece
        at += piece.shape[0]
    copy = pltpu.make_async_copy(table_v, table, sem)
    copy.start()
    return copy


def own_kernel(rows, total, own_ref, offset_ref, block_ref, count_ref, fill_ref,
               tile_ref, north_ref, south_ref, g_tile, g_north, g_south,
               src, grad, table_v, table, list_ref, classes, ends, sem, *buffers):
    blocks = rows // halves
    north_fill = north_ref[fields * rows : fields * rows + halves, :].astype(i32)
    south_fill = south_ref[fields * rows : fields * rows + halves, :].astype(i32)
    copy = as_table((north_fill, fill_ref[...], south_fill, jnp.zeros((10, lanes), i32)), table_v, table, sem)
    start_lists(classes, ends)
    for ref, base in ((north_ref, 0), (tile_ref, rows), (south_ref, 2 * rows)):
        for f in range(fields):
            src[f * total + base : f * total + base + rows, :] = ref[f * rows : (f + 1) * rows, :]
    for f in range(axes):
        grad[f * total : f * total + 3 * rows, :] = jnp.zeros((3 * rows, lanes), f32)
    copy.wait()

    def step(s, carry):
        heading = offset_ref[s]
        dr = third(heading)
        live = (heading - 3 * dr == 1).astype(i32)
        note(classes, ends, list_ref, table, blocks + own_ref[s], dr * blocks + block_ref[s], live)
        return carry

    lax.fori_loop(0, count_ref[0], step, 0)
    spare = 3 * blocks
    close_lists(ends, list_ref, spare)
    pair_loops(total, spare, list_ref, table, ends, src, grad, buffers)
    for ref, base in ((g_north, 0), (g_tile, rows), (g_south, 2 * rows)):
        for f in range(axes):
            ref[f * rows : (f + 1) * rows, :] = grad[f * total + base : f * total + base + rows, :]


def side_kernel(slots, rows, total, level, fill_ref, tiles, east_ref, west_ref, g_tiles, g_east, g_west,
                o_tiles, o_east, o_west, src, grad, table_v, table, list_ref, classes, ends, sem, *buffers):
    blocks = rows // halves
    slot_rows = halves * slots
    bases = (rows,) if level else (0, 2 * rows)
    fills = [jnp.zeros((halves, lanes), i32)] * 3
    if level:
        fills[1] = fill_ref[...]
    else:
        fills[0], fills[2] = (t[fields * rows : fields * rows + halves, :].astype(i32) for t in tiles)
    metas = [ref[fields * slot_rows : fields * slot_rows + meta_rows, :] for ref in (east_ref, west_ref)]
    partners = [(m[4:6] * blocks + m[0:2]).astype(i32) for m in metas]
    counts = jnp.concatenate([m[6:7].astype(i32) for m in metas], axis=0)
    copy = as_table((*fills, metas[0][2:4].astype(i32), metas[1][2:4].astype(i32), *partners, counts), table_v, table, sem)
    start_lists(classes, ends)
    east_base, west_base = 6 * lanes, 8 * lanes
    slot_places = ((east_ref, halves * east_base), (west_ref, halves * west_base))
    for ref, base in zip(tiles, bases):
        for f in range(fields):
            src[f * total + base : f * total + base + rows, :] = ref[f * rows : (f + 1) * rows, :]
    for ref, base in slot_places:
        for f in range(fields):
            src[f * total + base : f * total + base + slot_rows, :] = ref[f * slot_rows : (f + 1) * slot_rows, :]
    for ref, base in zip(g_tiles, bases):
        for f in range(axes):
            grad[f * total + base : f * total + base + rows, :] = ref[f * rows : (f + 1) * rows, :]
    for ref, (_, base) in zip((g_east, g_west), slot_places):
        for f in range(axes):
            init = jnp.zeros((slot_rows, lanes), f32) if ref is None else ref[f * slot_rows : (f + 1) * slot_rows, :]
            grad[f * total + base : f * total + base + slot_rows, :] = init
    copy.wait()
    for side, base in ((0, east_base), (1, west_base)):
        if level:
            first, last = slots - table[14 + side, 1], slots
        else:
            first, last = 0, table[14 + side, 0]

        def step(k, carry, side=side, base=base):
            b = table[10 + 2 * side + (k >> 7), k & 127]
            note(classes, ends, list_ref, table, base + k, b, 1)
            return carry

        lax.fori_loop(first, last, step, 0)
    spare = 10 * lanes
    close_lists(ends, list_ref, spare)
    pair_loops(total, spare, list_ref, table, ends, src, grad, buffers)
    for ref, base in zip(o_tiles, bases):
        for f in range(axes):
            ref[f * rows : (f + 1) * rows, :] = grad[f * total + base : f * total + base + rows, :]
    for ref, (_, base) in zip((o_east, o_west), slot_places):
        for f in range(axes):
            ref[f * slot_rows : (f + 1) * slot_rows, :] = grad[f * total + base : f * total + base + slot_rows, :]


def merge_kernel(slots, blocks, own_ref, offset_ref, count_ref, g_tile, g_north, g_south, g_east, g_west, out_ref):
    out_ref[...] = g_tile[...] + g_north[...] + g_south[...]

    def merge(ref, at, s):
        a = own_ref[s]
        for f in range(axes):
            out_ref[f * blocks + a] = out_ref[f * blocks + a] + ref[f * slots + at]

    def step(s, carry):
        east_front, east_back, west_front, west_back = carry
        heading = offset_ref[s]
        dr = third(heading)
        dc = heading - 3 * dr
        level = dr == 1
        is_east = dc == 2
        is_west = dc == 0

        @pl.when(is_east)
        def _():
            merge(g_east, jnp.where(level, slots - 1 - east_back, east_front), s)

        @pl.when(is_west)
        def _():
            merge(g_west, jnp.where(level, slots - 1 - west_back, west_front), s)

        east, west = is_east.astype(i32), is_west.astype(i32)
        back = level.astype(i32)
        return (east_front + east * (1 - back), east_back + east * back,
                west_front + west * (1 - back), west_back + west * back)

    lax.fori_loop(0, count_ref[0], step, (0, 0, 0, 0))


def shifted(x, axis, by):
    devices = lax.axis_size(axis)
    pairs = [(i, i + by) for i in range(devices) if 0 <= i + by < devices]
    return lax.ppermute(x, axis, pairs)


vmem = pl.BlockSpec(memory_space=pltpu.VMEM)
smem = pl.BlockSpec(memory_space=pltpu.SMEM)
anywhere = pl.BlockSpec(memory_space=pl.ANY)


def sds(n):
    return jax.ShapeDtypeStruct((n, lanes), f32)


def params(mib):
    return pltpu.CompilerParams(vmem_limit_bytes=mib << 20)


def pair_scratch(total, length):
    return [
        pltpu.VMEM((fields * total, lanes), f32),
        pltpu.VMEM((axes * total, lanes), f32),
        pltpu.VMEM((16, lanes), i32),
        pltpu.SMEM((16, lanes), i32),
        pltpu.SMEM((kinds, length), i32),
        pltpu.SMEM((64,), i32),
        pltpu.SMEM((8,), i32),
        pltpu.SemaphoreType.DMA,
        pltpu.VMEM((halves * lanes, fields * lanes), f32),
        pltpu.VMEM((halves * lanes, fields * lanes), f32),
        pltpu.VMEM((8, halves * lanes), f32),
        pltpu.VMEM((8, halves * lanes), f32),
        pltpu.VMEM((axes * halves * lanes, lanes), f32),
        pltpu.VMEM((axes * halves * lanes, lanes), f32),
        pltpu.VMEM((axes * 8, halves * lanes), f32),
        pltpu.VMEM((axes * 8, halves * lanes), f32),
    ]


def own_call(slots, rows, own, offset, block, count, fill2, tile, north, south):
    total = 3 * rows + 8
    return pl.pallas_call(
        lambda *refs: own_kernel(rows, total, *refs),
        out_shape=(sds(axes * rows),) * 3,
        in_specs=[smem] * 4 + [vmem] * 4,
        out_specs=(vmem,) * 3,
        scratch_shapes=pair_scratch(total, slots + 8),
        compiler_params=params(24),
        name="pairs_own",
    )(own, offset, block, count, fill2, tile, north, south)


def side_call(slots, rows, level, fill2, tiles, east, west, g_tiles, g_slots):
    total = 3 * rows + 4 * halves * lanes + 8
    n, m = len(tiles), len(g_slots)

    def run(*refs):
        refs = list(refs)
        take = lambda k: [refs.pop(0) for _ in range(k)]
        (fill_ref,), t = take(1), take(n)
        e, w = take(2)
        g = take(n)
        ge, gw = take(2) if m else (None, None)
        o = take(n)
        oe, ow = take(2)
        side_kernel(slots, rows, total, level, fill_ref, t, e, w, g, ge, gw, o, oe, ow, *refs)

    return pl.pallas_call(
        run,
        out_shape=(sds(axes * rows),) * n + (sds(axes * halves * slots),) * 2,
        in_specs=[vmem] * (1 + n + 2 + n + m),
        out_specs=(vmem,) * (n + 2),
        scratch_shapes=pair_scratch(total, 2 * slots + 8),
        compiler_params=params(32),
        name="pairs_level" if level else "pairs_cross",
    )(fill2, *tiles, east, west, *g_tiles, *g_slots)


def body(locations, solution, cotangent, block_fill, pair_own, pair_offset, pair_block, pair_count):
    points = solution.shape[2]
    slots = pair_own.shape[2]
    rows = points // lanes
    blocks = rows // halves
    own = pair_own.reshape(slots)
    offset = pair_offset.reshape(slots)
    block = pair_block.reshape(slots)
    count = pair_count.reshape(1)
    fill = block_fill.reshape(blocks)
    fill2 = block_fill.reshape(halves, lanes)
    tile_rows = fields * rows + meta_rows
    slot_rows = fields * halves * slots + meta_rows

    def paired(n):
        return jax.ShapeDtypeStruct((n // halves, halves, lanes), f32)

    tile = pl.pallas_call(
        lambda *refs: tile_kernel(rows, *refs),
        out_shape=sds(tile_rows),
        in_specs=[vmem] + [anywhere] * 3,
        out_specs=vmem,
        scratch_shapes=[pltpu.SemaphoreType.DMA((3,))],
        compiler_params=params(8),
        name="tile",
    )(fill2, locations.reshape(axes * rows, lanes), solution.reshape(rows, lanes), cotangent.reshape(rows, lanes))
    north = shifted(tile, "ty", 1)
    south = shifted(tile, "ty", -1)
    meta = pltpu.SMEM((meta_rows // halves, halves, lanes), f32)
    to_east, to_west = pl.pallas_call(
        lambda *refs: pack_kernel(slots, blocks, *refs),
        out_shape=(paired(slot_rows),) * 2,
        in_specs=[smem] * 5 + [vmem],
        out_specs=(vmem,) * 2,
        scratch_shapes=[meta, meta, pltpu.SemaphoreType.DMA((2,))],
        compiler_params=params(16),
        name="pack",
    )(own, offset, block, count, fill, tile.reshape(tile_rows // halves, halves, lanes))
    from_west = shifted(to_east, "tx", 1).reshape(slot_rows, lanes)
    from_east = shifted(to_west, "tx", -1).reshape(slot_rows, lanes)
    g_tile, g_north, g_south = own_call(slots, rows, own, offset, block, count, fill2, tile, north, south)
    g_north, g_south, g_west, g_east = side_call(
        slots, rows, False, fill2, (north, south), from_west, from_east, (g_north, g_south), ())
    back_south = shifted(g_north, "ty", -1)
    back_north = shifted(g_south, "ty", 1)
    g_tile, g_west, g_east = side_call(
        slots, rows, True, fill2, (tile,), from_west, from_east, (g_tile,), (g_west, g_east))
    back_east = shifted(g_west, "tx", -1)
    back_west = shifted(g_east, "tx", 1)
    views = [x.reshape(-1, halves, lanes) for x in (g_tile, back_north, back_south, back_east, back_west)]
    out = pl.pallas_call(
        lambda *refs: merge_kernel(slots, blocks, *refs),
        out_shape=paired(axes * rows),
        in_specs=[smem] * 3 + [vmem] * 5,
        out_specs=vmem,
        compiler_params=params(16),
        name="merge",
    )(own, offset, count, *views)
    return out.reshape(locations.shape)


def solution(mesh):
    placed = (
        P("ty", "tx", None, None),
        P("ty", "tx", None),
        P("ty", "tx", None),
        P("ty", "tx", None),
        P("ty", "tx", None),
        P("ty", "tx", None),
        P("ty", "tx", None),
        P("ty", "tx"),
    )
    return jax.shard_map(
        body, mesh=mesh, in_specs=placed, out_specs=P("ty", "tx", None, None), check_vma=False
    )
```

```python
import jax
import jax.numpy as jnp
from jax import lax
from jax.experimental import pallas as pl
from jax.experimental.pallas import tpu as pltpu
from jax.sharding import PartitionSpec as P

lanes = 128
halves = 2
fields = 5
axes = 3
meta_rows = 8
kinds = 5
bf16 = jnp.bfloat16
f32 = jnp.float32
i32 = jnp.int32


def third(heading):
    return (heading * 11) >> 5


def tile_kernel(rows, fill_ref, loc_ref, sol_ref, cot_ref, tile_ref, sem):
    copies = (
        pltpu.make_async_copy(loc_ref, tile_ref.at[pl.ds(0, axes * rows)], sem.at[0]),
        pltpu.make_async_copy(sol_ref, tile_ref.at[pl.ds(axes * rows, rows)], sem.at[1]),
        pltpu.make_async_copy(cot_ref, tile_ref.at[pl.ds((axes + 1) * rows, rows)], sem.at[2]),
    )
    for c in copies:
        c.start()
    fill = two_rows(fill_ref[...]).astype(f32)
    tile_ref[fields * rows : fields * rows + meta_rows, :] = jnp.concatenate(
        [fill, jnp.zeros((meta_rows - halves, lanes), f32)], axis=0
    )
    for c in copies:
        c.wait()


def rows_dot(x, y, contract):
    return lax.dot_general(x.astype(bf16), y.astype(bf16), (((1,), (contract,)), ((), ())), preferred_element_type=f32)


def split3(x):
    high = x.astype(bf16).astype(f32)
    rest = x - high
    mid = rest.astype(bf16).astype(f32)
    return high, mid, rest - mid


def stacked(rows, width):
    rows = [r.astype(f32) for r in rows]
    return jnp.concatenate(rows + [jnp.zeros((8 - len(rows), width), f32)], axis=0)


def wide(row):
    missing = halves * lanes - row.shape[1]
    return row if missing == 0 else jnp.concatenate([row, jnp.zeros((1, missing), row.dtype)], axis=1)


def one_row(x):
    return jnp.concatenate([x[0:1], x[1:2]], axis=1)


def two_rows(x):
    return jnp.concatenate([x[:, h * lanes : (h + 1) * lanes] for h in range(x.shape[1] // lanes)], axis=0)


def equal_rows(row, count, first=0):
    at = lax.broadcasted_iota(i32, (count, row.shape[1]), 0) + first
    return (row.astype(i32) == at).astype(f32).astype(bf16)


def running(flags):
    size = halves * lanes
    upper = lax.broadcasted_iota(i32, (size, size), 0) <= lax.broadcasted_iota(i32, (size, size), 1)
    return rows_dot(flags, upper.astype(f32), 0)


def pack_kernel(slots, rows, count_ref, own_ref, offset_ref, block_ref, fill_ref, tile_ref,
                east_ref, west_ref, origin_ref):
    blocks = rows // halves
    size = halves * lanes
    slot_rows = halves * slots
    own, offset, block = (wide(r[...]) for r in (own_ref, offset_ref, block_ref))
    live = lax.broadcasted_iota(i32, (1, size), 1) < count_ref[0]
    dr = third(offset)
    dc = offset - 3 * dr
    level = dr == 1
    marks = [live & (dc == want) & (level == back) for want in (2, 0) for back in (False, True)]
    counts = running(stacked(marks, size))
    picked = equal_rows(own, blocks)
    fill = rows_dot(stacked([fill_ref[...]], size), picked, 0)[0:1]
    values = stacked([block, fill, dr, own + 1], size)
    lane_id = lax.broadcasted_iota(i32, (1, lanes), 1)
    chosen = []
    for side, out_ref in enumerate((east_ref, west_ref)):
        front, back = marks[2 * side], marks[2 * side + 1]
        front_n, back_n = counts[2 * side : 2 * side + 1], counts[2 * side + 1 : 2 * side + 2]
        place = jnp.where(front, front_n - 1.0, jnp.where(back, slots - back_n, -1.0))
        moved = equal_rows(place, slots)
        meta = rows_dot(values, moved, 1)
        meta = jnp.concatenate([meta, jnp.zeros((8, size - slots), f32)], axis=1)
        ends = jnp.where(lane_id == 0, front_n[:, size - 1 :], jnp.where(lane_id == 1, back_n[:, size - 1 :], 0.0))
        out_ref[fields * slot_rows : fields * slot_rows + meta_rows, :] = jnp.concatenate(
            [two_rows(meta[k : k + 1]) for k in range(3)] + [ends, jnp.zeros((1, lanes), f32)], axis=0)
        origin_ref[side : side + 1, :] = meta[3:4] - 1.0
        chosen.append(rows_dot(moved, picked, 1).astype(bf16))
    for f in range(fields):
        data = jnp.concatenate([tile_ref[pl.ds(f * rows + h, blocks, stride=halves), :] for h in range(halves)], axis=1)
        parts = split3(data)
        for pick, out_ref in zip(chosen, (east_ref, west_ref)):
            got = rows_dot(pick, parts[0], 0) + rows_dot(pick, parts[1], 0) + rows_dot(pick, parts[2], 0)
            for h in range(halves):
                out_ref[pl.ds(f * slot_rows + h, slots, stride=halves), :] = got[:, h * lanes : (h + 1) * lanes]


def shape_of(kind):
    steps = (16, 24, 16, 24, 32)[kind]
    return steps, -(-steps // 16), (1, 1, 2, 2, 2)[kind]


def pair_loops(total, spare, table, src, grad, buffers):
    size = halves * lanes

    def word_at(k, at):
        place = table[11, k] + at
        return table[12 + (place >> 7), place & 127]

    def load(index, fill, parts):
        size = parts * lanes
        row_id = lax.broadcasted_iota(i32, (8, size), 0)
        lane_id = lax.broadcasted_iota(i32, (8, size), 1)
        pieces = []
        for h in range(parts):
            got = src[pl.ds(halves * index + h, fields, stride=total), :]
            pieces.append(jnp.concatenate([got, jnp.zeros((8 - fields, lanes), f32)], axis=0))
        x = jnp.concatenate(pieces, axis=1)
        return jnp.where((row_id < axes) | (lane_id < fill), x, 0.0)

    def spread(k, at, mixed, partner):
        steps, parts_a, parts_b = shape_of(k)
        word = word_at(k, at)
        ia, ib = word & 4095, word >> 12
        live = at < table[11, 8 + k]
        a = load(ia, jnp.where(live, table[ia >> 7, ia & 127], 0), parts_a)
        b = load(ib, jnp.where(live, table[ib >> 7, ib & 127], 0), parts_b)
        partner[:, : parts_b * lanes] = b
        zero = jnp.zeros((8, lanes), f32)
        row_b = lax.broadcasted_iota(i32, b.shape, 0)
        ah, am, al = split3(a)
        left = jnp.concatenate([ah, am, al, ah, ah, am], axis=0).astype(bf16)
        swapped = jnp.where(row_b == 3, jnp.roll(b, -1, axis=0), jnp.where(row_b == 4, jnp.roll(b, 1, axis=0), 0.0))
        sh, sm, sl = split3(swapped * -20.0)
        right = jnp.concatenate([sh, sh, sh, sm, sl, sm], axis=0).astype(bf16)
        row_id = lax.broadcasted_iota(i32, (8, lanes), 0)
        units = [(row_id == f).astype(f32) for f in range(axes)]
        pick = jnp.concatenate([jnp.concatenate([u, u, u, zero, zero, zero], axis=0) for u in units], axis=1).astype(bf16)
        mixed[: parts_a * lanes, : (axes + parts_b) * lanes] = lax.dot_general(
            left, jnp.concatenate([pick, right], axis=1), (((0,), (0,)), ((), ())), preferred_element_type=f32)

    def work(k, mixed, partner, own, far):
        steps, parts_a, parts_b = shape_of(k)
        b_rows = [
            [jnp.broadcast_to(partner[f : f + 1, p * lanes : (p + 1) * lanes], (8, lanes)) for f in range(axes)]
            for p in range(parts_b)
        ]
        sums = [[None] * axes for _ in range(parts_b)]
        for g in range(steps):
            rows = slice(8 * g, 8 * g + 8)
            a_cols = [mixed[rows, f * lanes : (f + 1) * lanes] for f in range(axes)]
            mine = [None] * axes
            for p in range(parts_b):
                diff = [a_cols[f] - b_rows[p][f] for f in range(axes)]
                square = diff[0] * diff[0] + diff[1] * diff[1] + diff[2] * diff[2]
                square = jnp.maximum(square, 1e-30)
                reach = jnp.maximum(1.0 - square * lax.rsqrt(square), 0.0)
                w = (reach * reach) * (reach * mixed[rows, (axes + p) * lanes : (axes + p + 1) * lanes])
                for f in range(axes):
                    push = w * diff[f]
                    mine[f] = push if p == 0 else mine[f] + push
                    sums[p][f] = push if g == 0 else sums[p][f] + push
            for f in range(axes):
                own[f * size + 8 * g : f * size + 8 * g + 8, :] = mine[f]
        for p in range(parts_b):
            for f in range(axes):
                far[8 * f : 8 * f + 8, p * lanes : (p + 1) * lanes] = sums[p][f]

    def finish(k, at, own, far):
        steps, parts_a, parts_b = shape_of(k)
        word = jnp.where(at < 0, spare | (spare << 12), word_at(k, jnp.maximum(at, 0)))
        ia, ib = word & 4095, word >> 12
        for h in range(parts_a):
            count = min(lanes, 8 * steps - h * lanes)
            rows = []
            for f in range(axes):
                part = own[f * size + h * lanes : f * size + h * lanes + count, :]
                if count < lanes:
                    part = jnp.concatenate([part, jnp.zeros((lanes - count, lanes), f32)], axis=0)
                rows.append(jnp.sum(part.T, axis=0, keepdims=True))
            place = pl.ds(halves * ia + h, axes, stride=total)
            grad[place, :] = grad[place, :] + jnp.concatenate(rows, axis=0)
        for p in range(parts_b):
            rows = [jnp.sum(far[8 * f : 8 * f + 8, p * lanes : (p + 1) * lanes], axis=0, keepdims=True) for f in range(axes)]
            place = pl.ds(halves * ib + p, axes, stride=total)
            grad[place, :] = grad[place, :] - jnp.concatenate(rows, axis=0)

    mixed0, mixed1, partner0, partner1, own0, own1, far0, far1 = buffers
    for k in range(kinds):
        turns = (table[11, 8 + k] + 1) // 2

        def turn(t, carry, k=k):
            at = 2 * t
            finish(k, at - 1, own1, far1)
            work(k, mixed0, partner0, own0, far0)
            spread(k, at + 1, mixed1, partner1)
            finish(k, at, own0, far0)
            work(k, mixed1, partner1, own1, far1)
            spread(k, at + 2, mixed0, partner0)
            return carry

        @pl.when(turns > 0)
        def _(k=k, turns=turns, turn=turn):
            spread(k, 0, mixed0, partner0)
            lax.fori_loop(0, turns, turn, 0)
            finish(k, 2 * turns - 1, own1, far1)


def sorted_pairs(entries):
    size = halves * lanes
    found = []
    for a, b, fill_a, fill_b, live in entries:
        size_a, size_b = (fill_a + 63) >> 6, (fill_b + 63) >> 6
        two_a, two_b = (size_a > 2).astype(i32), (size_b > 2).astype(i32)
        swap = (size_a * (1 + two_b) > size_b * (1 + two_a)) | ((size_a > 3) & (size_b < 3))
        a, b = jnp.where(swap, b, a), jnp.where(swap, a, b)
        size_a, size_b = jnp.where(swap, size_b, size_a), jnp.where(swap, size_a, size_b)
        kind = jnp.maximum(size_a - 2, 0) + jnp.where(size_b > 2, 2, 0)
        marks = [live & (kind == k) for k in range(kinds)]
        counts = running(stacked(marks, size))
        values = stacked([a & 255, a >> 8, b & 255, b >> 8], size)
        found.append((marks, counts, values))
    firsts, totals = [], []
    at = jnp.zeros((1, 1), f32)
    for k in range(kinds):
        firsts.append(at)
        total = sum(counts[k : k + 1, size - 1 :] for _, counts, _ in found)
        totals.append(total)
        at = at + total
    length = size * len(entries)
    ordered = jnp.zeros((8, length), f32)
    before = firsts
    for marks, counts, values in found:
        place = jnp.full((1, size), -1.0, f32)
        for k in range(kinds):
            place = jnp.where(marks[k], before[k] + counts[k : k + 1] - 1.0, place)
        before = [before[k] + counts[k : k + 1, size - 1 :] for k in range(kinds)]
        ordered = ordered + rows_dot(values, equal_rows(place, length), 1)
    ordered = ordered.astype(i32)
    words = ordered[0:1] + (ordered[1:2] << 8) + (ordered[2:3] << 12) + (ordered[3:4] << 20)
    lane_id = lax.broadcasted_iota(i32, (1, lanes), 1)
    bounds = jnp.zeros((1, lanes), i32)
    for k in range(kinds):
        bounds = jnp.where(lane_id == k, firsts[k].astype(i32), bounds)
        bounds = jnp.where(lane_id == 8 + k, totals[k].astype(i32), bounds)
    return words, bounds


def as_table(pieces, table_v, table, sem):
    at = 0
    for piece in pieces:
        table_v[at : at + piece.shape[0], :] = piece
        at += piece.shape[0]
    copy = pltpu.make_async_copy(table_v, table, sem)
    copy.start()
    return copy


def fills_of(fills, block):
    return rows_dot(stacked(fills, block.shape[1]), equal_rows(block, halves * lanes), 0).astype(i32)


def own_kernel(rows, total, count_ref, own_ref, offset_ref, block_ref, fill_ref,
               tile_ref, north_ref, south_ref, g_tile, g_north, g_south,
               src, grad, table_v, table, sem, *buffers):
    blocks = rows // halves
    size = halves * lanes
    fills = [one_row(north_ref[fields * rows : fields * rows + halves, :].astype(i32)), fill_ref[...],
             one_row(south_ref[fields * rows : fields * rows + halves, :].astype(i32))]
    own, offset, block = (wide(r[...]) for r in (own_ref, offset_ref, block_ref))
    live = lax.broadcasted_iota(i32, (1, size), 1) < count_ref[0]
    dr = third(offset)
    near = fills_of(fills, block)
    fill_b = jnp.where(dr == 0, near[0:1], jnp.where(dr == 1, near[1:2], near[2:3]))
    words, bounds = sorted_pairs([(blocks + own, dr * blocks + block, fills_of(fills[1:2], own)[0:1], fill_b,
                                   live & (offset - 3 * dr == 1))])
    copy = as_table((*map(two_rows, fills), jnp.zeros((5, lanes), i32), bounds, two_rows(words)), table_v, table, sem)
    for ref, base in ((north_ref, 0), (tile_ref, rows), (south_ref, 2 * rows)):
        for f in range(fields):
            src[f * total + base : f * total + base + rows, :] = ref[f * rows : (f + 1) * rows, :]
    for f in range(axes):
        grad[f * total : f * total + 3 * rows, :] = jnp.zeros((3 * rows, lanes), f32)
    copy.wait()
    pair_loops(total, 3 * blocks, table, src, grad, buffers)
    for ref, base in ((g_north, 0), (g_tile, rows), (g_south, 2 * rows)):
        for f in range(axes):
            ref[f * rows : (f + 1) * rows, :] = grad[f * total + base : f * total + base + rows, :]


def side_kernel(slots, rows, total, level, fill_ref, tiles, east_ref, west_ref, g_tiles, g_east, g_west,
                o_tiles, o_east, o_west, src, grad, table_v, table, sem, *buffers):
    blocks = rows // halves
    slot_rows = halves * slots
    size = halves * lanes
    bases = (rows,) if level else (0, 2 * rows)
    fills = [jnp.zeros((1, size), i32)] * 3
    if level:
        fills[1] = fill_ref[...]
    else:
        fills[0], fills[2] = (one_row(t[fields * rows : fields * rows + halves, :].astype(i32)) for t in tiles)
    east_base, west_base = 6 * lanes, 8 * lanes
    slot_id = lax.broadcasted_iota(i32, (1, size), 1)
    entries, slot_fills = [], []
    for ref, base in ((east_ref, east_base), (west_ref, west_base)):
        meta = ref[fields * slot_rows : fields * slot_rows + meta_rows, :].astype(i32)
        if level:
            live = (slot_id >= slots - meta[6:7, 1:2]) & (slot_id < slots)
        else:
            live = slot_id < meta[6:7, 0:1]
        block, fill, dr = (jnp.where(live, one_row(meta[2 * k : 2 * k + 2]), 0) for k in range(3))
        near = fills_of(fills, block)
        fill_b = near[1:2] if level else jnp.where(dr == 0, near[0:1], near[2:3])
        entries.append((base + slot_id, dr * blocks + block, fill, fill_b, live))
        slot_fills.append(fill)
    words, bounds = sorted_pairs(entries)
    copy = as_table((*map(two_rows, fills), *map(two_rows, slot_fills), jnp.zeros((1, lanes), i32), bounds, two_rows(words)),
                    table_v, table, sem)
    slot_places = ((east_ref, halves * east_base), (west_ref, halves * west_base))
    for ref, base in zip(tiles, bases):
        for f in range(fields):
            src[f * total + base : f * total + base + rows, :] = ref[f * rows : (f + 1) * rows, :]
    for ref, base in slot_places:
        for f in range(fields):
            src[f * total + base : f * total + base + slot_rows, :] = ref[f * slot_rows : (f + 1) * slot_rows, :]
    for ref, base in zip(g_tiles, bases):
        for f in range(axes):
            grad[f * total + base : f * total + base + rows, :] = ref[f * rows : (f + 1) * rows, :]
    for ref, (_, base) in zip((g_east, g_west), slot_places):
        for f in range(axes):
            init = jnp.zeros((slot_rows, lanes), f32) if ref is None else ref[f * slot_rows : (f + 1) * slot_rows, :]
            grad[f * total + base : f * total + base + slot_rows, :] = init
    copy.wait()
    pair_loops(total, 10 * lanes, table, src, grad, buffers)
    for ref, base in zip(o_tiles, bases):
        for f in range(axes):
            ref[f * rows : (f + 1) * rows, :] = grad[f * total + base : f * total + base + rows, :]
    for ref, (_, base) in zip((o_east, o_west), slot_places):
        for f in range(axes):
            ref[f * slot_rows : (f + 1) * slot_rows, :] = grad[f * total + base : f * total + base + slot_rows, :]


def merge_kernel(slots, rows, origin_ref, g_tile, g_north, g_south, g_east, g_west, out_ref):
    blocks = rows // halves
    slot_rows = halves * slots
    placed = [equal_rows(origin_ref[side : side + 1, :][:, :slots], blocks) for side in range(2)]
    out_ref[...] = g_tile[...] + g_north[...] + g_south[...]
    for f in range(axes):
        got = jnp.zeros((blocks, halves * lanes), f32)
        for place, ref in zip(placed, (g_east, g_west)):
            data = jnp.concatenate([ref[pl.ds(f * slot_rows + h, slots, stride=halves), :] for h in range(halves)], axis=1)
            for part in split3(data):
                got = got + rows_dot(place, part, 0)
        for h in range(halves):
            at = pl.ds(f * rows + h, blocks, stride=halves)
            out_ref[at, :] = out_ref[at, :] + got[:, h * lanes : (h + 1) * lanes]


def shifted(x, axis, by):
    devices = lax.axis_size(axis)
    pairs = [(i, i + by) for i in range(devices) if 0 <= i + by < devices]
    return lax.ppermute(x, axis, pairs)


vmem = pl.BlockSpec(memory_space=pltpu.VMEM)
smem = pl.BlockSpec(memory_space=pltpu.SMEM)
in_hbm = pl.BlockSpec(memory_space=pltpu.HBM)


def sds(n):
    return jax.ShapeDtypeStruct((n, lanes), f32)


def params(mib):
    return pltpu.CompilerParams(vmem_limit_bytes=mib << 20)


def pair_scratch(total, sets):
    return [
        pltpu.VMEM((fields * total, lanes), f32),
        pltpu.VMEM((axes * total, lanes), f32),
        pltpu.VMEM((12 + halves * sets, lanes), i32),
        pltpu.SMEM((12 + halves * sets, lanes), i32),
        pltpu.SemaphoreType.DMA,
        pltpu.VMEM((halves * lanes, fields * lanes), f32),
        pltpu.VMEM((halves * lanes, fields * lanes), f32),
        pltpu.VMEM((8, halves * lanes), f32),
        pltpu.VMEM((8, halves * lanes), f32),
        pltpu.VMEM((axes * halves * lanes, lanes), f32),
        pltpu.VMEM((axes * halves * lanes, lanes), f32),
        pltpu.VMEM((axes * 8, halves * lanes), f32),
        pltpu.VMEM((axes * 8, halves * lanes), f32),
    ]


def own_call(rows, count, own, offset, block, fill, tile, north, south):
    total = 3 * rows + 8
    return pl.pallas_call(
        lambda *refs: own_kernel(rows, total, *refs),
        out_shape=(sds(axes * rows),) * 3,
        in_specs=[smem] + [vmem] * 7,
        out_specs=(vmem,) * 3,
        scratch_shapes=pair_scratch(total, 1),
        compiler_params=params(24),
        name="pairs_own",
    )(count, own, offset, block, fill, tile, north, south)


def side_call(slots, rows, level, fill, tiles, east, west, g_tiles, g_slots):
    total = 3 * rows + 4 * halves * lanes + 8
    n, m = len(tiles), len(g_slots)

    def run(*refs):
        refs = list(refs)
        take = lambda k: [refs.pop(0) for _ in range(k)]
        (fill_ref,), t = take(1), take(n)
        e, w = take(2)
        g = take(n)
        ge, gw = take(2) if m else (None, None)
        o = take(n)
        oe, ow = take(2)
        side_kernel(slots, rows, total, level, fill_ref, t, e, w, g, ge, gw, o, oe, ow, *refs)

    return pl.pallas_call(
        run,
        out_shape=(sds(axes * rows),) * n + (sds(axes * halves * slots),) * 2,
        in_specs=[vmem] * (1 + n + 2 + n + m),
        out_specs=(vmem,) * (n + 2),
        scratch_shapes=pair_scratch(total, 2),
        compiler_params=params(32),
        name="pairs_level" if level else "pairs_cross",
    )(fill, *tiles, east, west, *g_tiles, *g_slots)


def body(locations, solution, cotangent, block_fill, pair_own, pair_offset, pair_block, pair_count):
    points = solution.shape[2]
    slots = pair_own.shape[2]
    rows = points // lanes
    blocks = rows // halves
    own = pair_own.reshape(1, slots)
    offset = pair_offset.reshape(1, slots)
    block = pair_block.reshape(1, slots)
    count = pair_count.reshape(1)
    fill = block_fill.reshape(1, blocks)
    slot_rows = fields * halves * slots + meta_rows
    tile = pl.pallas_call(
        lambda *refs: tile_kernel(rows, *refs),
        out_shape=sds(fields * rows + meta_rows),
        in_specs=[vmem] + [in_hbm] * 3,
        out_specs=vmem,
        scratch_shapes=[pltpu.SemaphoreType.DMA((3,))],
        compiler_params=params(8),
        name="tile",
    )(fill, locations.reshape(axes * rows, lanes), solution.reshape(rows, lanes), cotangent.reshape(rows, lanes))
    north = shifted(tile, "ty", 1)
    south = shifted(tile, "ty", -1)
    to_east, to_west, origin = pl.pallas_call(
        lambda *refs: pack_kernel(slots, rows, *refs),
        out_shape=(sds(slot_rows), sds(slot_rows), jax.ShapeDtypeStruct((8, halves * lanes), f32)),
        in_specs=[smem] + [vmem] * 5,
        out_specs=(vmem,) * 3,
        compiler_params=params(16),
        name="pack",
    )(count, own, offset, block, fill, tile)
    from_west = shifted(to_east, "tx", 1)
    from_east = shifted(to_west, "tx", -1)
    g_tile, g_north, g_south = own_call(rows, count, own, offset, block, fill, tile, north, south)
    g_north, g_south, g_west, g_east = side_call(
        slots, rows, False, fill, (north, south), from_west, from_east, (g_north, g_south), ())
    back_south = shifted(g_north, "ty", -1)
    back_north = shifted(g_south, "ty", 1)
    g_tile, g_west, g_east = side_call(
        slots, rows, True, fill, (tile,), from_west, from_east, (g_tile,), (g_west, g_east))
    back_east = shifted(g_west, "tx", -1)
    back_west = shifted(g_east, "tx", 1)
    out = pl.pallas_call(
        lambda *refs: merge_kernel(slots, rows, *refs),
        out_shape=sds(axes * rows),
        in_specs=[vmem] * 6,
        out_specs=vmem,
        compiler_params=params(16),
        name="merge",
    )(origin, g_tile, back_north, back_south, back_east, back_west)
    return out.reshape(locations.shape)


def solution(mesh):
    placed = (
        P("ty", "tx", None, None),
        P("ty", "tx", None),
        P("ty", "tx", None),
        P("ty", "tx", None),
        P("ty", "tx", None),
        P("ty", "tx", None),
        P("ty", "tx", None),
        P("ty", "tx"),
    )
    return jax.shard_map(
        body, mesh=mesh, in_specs=placed, out_specs=P("ty", "tx", None, None), check_vma=False
    )
```

```python
import jax
import jax.numpy as jnp
from jax import lax
from jax.experimental import pallas as pl
from jax.experimental.pallas import tpu as pltpu
from jax.sharding import PartitionSpec as P

lanes = 128
halves = 2
fields = 5
axes = 3
meta_rows = 8
kinds = 5
kept = 32
bf16 = jnp.bfloat16
f32 = jnp.float32
i32 = jnp.int32


def third(heading):
    return (heading * 11) >> 5


def tile_kernel(rows, slots, count_ref, fill_ref, own_ref, offset_ref, block_ref, loc_ref, sol_ref, cot_ref, tile_ref,
                count_s, fill_v, lists_v, meta_v, sem):
    small = (
        pltpu.make_async_copy(fill_ref, fill_v, sem.at[0]),
        pltpu.make_async_copy(own_ref, lists_v.at[0], sem.at[1]),
        pltpu.make_async_copy(offset_ref, lists_v.at[1], sem.at[2]),
        pltpu.make_async_copy(block_ref, lists_v.at[2], sem.at[3]),
        pltpu.make_async_copy(count_ref, count_s, sem.at[4]),
    )
    large = (
        pltpu.make_async_copy(loc_ref, tile_ref.at[pl.ds(0, axes * rows)], sem.at[5]),
        pltpu.make_async_copy(sol_ref, tile_ref.at[pl.ds(axes * rows, rows)], sem.at[6]),
        pltpu.make_async_copy(cot_ref, tile_ref.at[pl.ds((axes + 1) * rows, rows)], sem.at[7]),
    )
    for c in small + large:
        c.start()
    for c in small:
        c.wait()
    own, offset, block = (wide(lists_v[k]) for k in range(3))
    last = lax.broadcasted_iota(i32, own.shape, 1) == own.shape[1] - 1
    own = jnp.where(last, count_s[0, 0], own)
    meta_v[...] = jnp.concatenate([two_rows(x) for x in (fill_v[...], own, offset, block)], axis=0).astype(f32)
    note = pltpu.make_async_copy(meta_v, tile_ref.at[pl.ds(fields * rows, meta_rows)], sem.at[8])
    note.start()
    for c in large + (note,):
        c.wait()


def lists_of(ref, rows):
    meta = ref[fields * rows : fields * rows + meta_rows, :].astype(i32)
    parts = [one_row(meta[2 * k : 2 * k + 2]) for k in range(4)]
    return (*parts, parts[1][:, halves * lanes - 1 :])


def rows_dot(x, y, contract):
    return lax.dot_general(x.astype(bf16), y.astype(bf16), (((1,), (contract,)), ((), ())), preferred_element_type=f32)


def split3(x):
    high = x.astype(bf16).astype(f32)
    rest = x - high
    mid = rest.astype(bf16).astype(f32)
    return high, mid, rest - mid


def stacked(rows, width):
    rows = [r.astype(f32) for r in rows]
    return jnp.concatenate(rows + [jnp.zeros((8 - len(rows), width), f32)], axis=0)


def wide(row):
    missing = halves * lanes - row.shape[1]
    return row if missing == 0 else jnp.concatenate([row, jnp.zeros((1, missing), row.dtype)], axis=1)


def one_row(x):
    return jnp.concatenate([x[0:1], x[1:2]], axis=1)


def two_rows(x):
    return jnp.concatenate([x[:, h * lanes : (h + 1) * lanes] for h in range(x.shape[1] // lanes)], axis=0)


def equal_rows(row, count, first=0):
    at = lax.broadcasted_iota(i32, (count, row.shape[1]), 0) + first
    return (row.astype(i32) == at).astype(f32).astype(bf16)


def running(flags):
    size = halves * lanes
    upper = lax.broadcasted_iota(i32, (size, size), 0) <= lax.broadcasted_iota(i32, (size, size), 1)
    return rows_dot(flags, upper.astype(f32), 0)


def pack_kernel(slots, rows, tile_ref, east_ref, west_ref, origin_ref):
    blocks = rows // halves
    size = halves * lanes
    slot_rows = halves * slots
    fill, own, offset, block, count = lists_of(tile_ref, rows)
    live = lax.broadcasted_iota(i32, (1, size), 1) < count
    dr = third(offset)
    dc = offset - 3 * dr
    level = dr == 1
    marks = [live & (dc == want) & (level == back) for want in (2, 0) for back in (False, True)]
    counts = running(stacked(marks, size))
    picked = equal_rows(own, blocks)
    fill = rows_dot(stacked([fill], size), picked, 0)[0:1]
    values = stacked([block, fill, dr, own + 1], size)
    lane_id = lax.broadcasted_iota(i32, (1, lanes), 1)
    chosen = []
    for side, out_ref in enumerate((east_ref, west_ref)):
        front, back = marks[2 * side], marks[2 * side + 1]
        front_n, back_n = counts[2 * side : 2 * side + 1], counts[2 * side + 1 : 2 * side + 2]
        place = jnp.where(front, front_n - 1.0, jnp.where(back, slots - back_n, -1.0))
        moved = equal_rows(place, slots)
        meta = rows_dot(values, moved, 1)
        meta = jnp.concatenate([meta, jnp.zeros((8, size - slots), f32)], axis=1)
        ends = jnp.where(lane_id == 0, front_n[:, size - 1 :], jnp.where(lane_id == 1, back_n[:, size - 1 :], 0.0))
        out_ref[fields * slot_rows : fields * slot_rows + meta_rows, :] = jnp.concatenate(
            [two_rows(meta[k : k + 1]) for k in range(3)] + [ends, jnp.zeros((1, lanes), f32)], axis=0)
        origin_ref[side : side + 1, :] = meta[3:4] - 1.0
        chosen.append(rows_dot(moved, picked, 1).astype(bf16))
    for f in range(fields):
        data = jnp.concatenate([tile_ref[pl.ds(f * rows + h, blocks, stride=halves), :] for h in range(halves)], axis=1)
        parts = split3(data)
        for pick, out_ref in zip(chosen, (east_ref, west_ref)):
            got = rows_dot(pick, parts[0], 0) + rows_dot(pick, parts[1], 0) + rows_dot(pick, parts[2], 0)
            for h in range(halves):
                out_ref[pl.ds(f * slot_rows + h, slots, stride=halves), :] = got[:, h * lanes : (h + 1) * lanes]


def shape_of(kind):
    steps = (16, 24, 16, 24, 32)[kind]
    return steps, -(-steps // 16), (1, 1, 2, 2, 2)[kind]


def pair_loops(total, spare, table, src, grad, buffers):
    size = halves * lanes

    def word_at(k, at):
        place = table[11, k] + at
        return table[12 + (place >> 7), place & 127]

    def load(index, fill, parts):
        size = parts * lanes
        row_id = lax.broadcasted_iota(i32, (8, size), 0)
        lane_id = lax.broadcasted_iota(i32, (8, size), 1)
        pieces = []
        for h in range(parts):
            got = src[pl.ds(halves * index + h, fields, stride=total), :]
            pieces.append(jnp.concatenate([got, jnp.zeros((8 - fields, lanes), f32)], axis=0))
        x = jnp.concatenate(pieces, axis=1)
        return jnp.where((row_id < axes) | (lane_id < fill), x, 0.0)

    def spread(k, at, mixed, partner):
        steps, parts_a, parts_b = shape_of(k)
        word = word_at(k, at)
        ia, ib = word & 4095, word >> 12
        live = at < table[11, 8 + k]
        a = load(ia, jnp.where(live, table[ia >> 7, ia & 127], 0), parts_a)
        b = load(ib, jnp.where(live, table[ib >> 7, ib & 127], 0), parts_b)
        partner[:, : parts_b * lanes] = b
        zero = jnp.zeros((8, lanes), f32)
        row_b = lax.broadcasted_iota(i32, b.shape, 0)
        ah, am, al = split3(a)
        left = jnp.concatenate([ah, am, al, ah, ah, am], axis=0).astype(bf16)
        swapped = jnp.where(row_b == 3, jnp.roll(b, -1, axis=0), jnp.where(row_b == 4, jnp.roll(b, 1, axis=0), 0.0))
        sh, sm, sl = split3(swapped * -20.0)
        right = jnp.concatenate([sh, sh, sh, sm, sl, sm], axis=0).astype(bf16)
        row_id = lax.broadcasted_iota(i32, (8, lanes), 0)
        units = [(row_id == f).astype(f32) for f in range(axes)]
        pick = jnp.concatenate([jnp.concatenate([u, u, u, zero, zero, zero], axis=0) for u in units], axis=1).astype(bf16)
        mixed[: parts_a * lanes, : (axes + parts_b) * lanes] = lax.dot_general(
            left, jnp.concatenate([pick, right], axis=1), (((0,), (0,)), ((), ())), preferred_element_type=f32)

    def work(k, mixed, partner, own, far):
        steps, parts_a, parts_b = shape_of(k)
        b_rows = [
            [jnp.broadcast_to(partner[f : f + 1, p * lanes : (p + 1) * lanes], (8, lanes)) for f in range(axes)]
            for p in range(parts_b)
        ]
        sums = [[None] * axes for _ in range(parts_b)]
        for g in range(steps):
            rows = slice(8 * g, 8 * g + 8)
            a_cols = [mixed[rows, f * lanes : (f + 1) * lanes] for f in range(axes)]
            mine = [None] * axes
            for p in range(parts_b):
                diff = [a_cols[f] - b_rows[p][f] for f in range(axes)]
                square = diff[0] * diff[0] + diff[1] * diff[1] + diff[2] * diff[2]
                square = jnp.maximum(square, 1e-30)
                reach = jnp.maximum(1.0 - square * lax.rsqrt(square), 0.0)
                w = (reach * reach) * (reach * mixed[rows, (axes + p) * lanes : (axes + p + 1) * lanes])
                for f in range(axes):
                    push = w * diff[f]
                    mine[f] = push if p == 0 else mine[f] + push
                    sums[p][f] = push if g == 0 else sums[p][f] + push
            for f in range(axes):
                own[f * size + 8 * g : f * size + 8 * g + 8, :] = mine[f]
        for p in range(parts_b):
            for f in range(axes):
                far[8 * f : 8 * f + 8, p * lanes : (p + 1) * lanes] = sums[p][f]

    def finish(k, at, own, far):
        steps, parts_a, parts_b = shape_of(k)
        word = jnp.where(at < 0, spare | (spare << 12), word_at(k, jnp.maximum(at, 0)))
        ia, ib = word & 4095, word >> 12
        for h in range(parts_a):
            count = min(lanes, 8 * steps - h * lanes)
            rows = []
            for f in range(axes):
                part = own[f * size + h * lanes : f * size + h * lanes + count, :]
                if count < lanes:
                    part = jnp.concatenate([part, jnp.zeros((lanes - count, lanes), f32)], axis=0)
                rows.append(jnp.sum(part.T, axis=0, keepdims=True))
            place = pl.ds(halves * ia + h, axes, stride=total)
            grad[place, :] = grad[place, :] + jnp.concatenate(rows, axis=0)
        for p in range(parts_b):
            rows = [jnp.sum(far[8 * f : 8 * f + 8, p * lanes : (p + 1) * lanes], axis=0, keepdims=True) for f in range(axes)]
            place = pl.ds(halves * ib + p, axes, stride=total)
            grad[place, :] = grad[place, :] - jnp.concatenate(rows, axis=0)

    mixed0, mixed1, partner0, partner1, own0, own1, far0, far1 = buffers
    for k in range(kinds):
        turns = (table[11, 8 + k] + 1) // 2

        def turn(t, carry, k=k):
            at = 2 * t
            finish(k, at - 1, own1, far1)
            work(k, mixed0, partner0, own0, far0)
            spread(k, at + 1, mixed1, partner1)
            finish(k, at, own0, far0)
            work(k, mixed1, partner1, own1, far1)
            spread(k, at + 2, mixed0, partner0)
            return carry

        @pl.when(turns > 0)
        def _(k=k, turns=turns, turn=turn):
            spread(k, 0, mixed0, partner0)
            lax.fori_loop(0, turns, turn, 0)
            finish(k, 2 * turns - 1, own1, far1)


def sorted_pairs(entries):
    size = halves * lanes
    found = []
    for a, b, fill_a, fill_b, live in entries:
        size_a, size_b = (fill_a + 63) >> 6, (fill_b + 63) >> 6
        two_a, two_b = (size_a > 2).astype(i32), (size_b > 2).astype(i32)
        swap = (size_a * (1 + two_b) > size_b * (1 + two_a)) | ((size_a > 3) & (size_b < 3))
        a, b = jnp.where(swap, b, a), jnp.where(swap, a, b)
        size_a, size_b = jnp.where(swap, size_b, size_a), jnp.where(swap, size_a, size_b)
        kind = jnp.maximum(size_a - 2, 0) + jnp.where(size_b > 2, 2, 0)
        marks = [live & (kind == k) for k in range(kinds)]
        counts = running(stacked(marks, size))
        values = stacked([a & 255, a >> 8, b & 255, b >> 8], size)
        found.append((marks, counts, values))
    firsts, totals = [], []
    at = jnp.zeros((1, 1), f32)
    for k in range(kinds):
        firsts.append(at)
        total = sum(counts[k : k + 1, size - 1 :] for _, counts, _ in found)
        totals.append(total)
        at = at + total
    length = size * len(entries)
    ordered = jnp.zeros((8, length), f32)
    before = firsts
    for marks, counts, values in found:
        place = jnp.full((1, size), -1.0, f32)
        for k in range(kinds):
            place = jnp.where(marks[k], before[k] + counts[k : k + 1] - 1.0, place)
        before = [before[k] + counts[k : k + 1, size - 1 :] for k in range(kinds)]
        ordered = ordered + rows_dot(values, equal_rows(place, length), 1)
    ordered = ordered.astype(i32)
    words = ordered[0:1] + (ordered[1:2] << 8) + (ordered[2:3] << 12) + (ordered[3:4] << 20)
    lane_id = lax.broadcasted_iota(i32, (1, lanes), 1)
    bounds = jnp.zeros((1, lanes), i32)
    for k in range(kinds):
        bounds = jnp.where(lane_id == k, firsts[k].astype(i32), bounds)
        bounds = jnp.where(lane_id == 8 + k, totals[k].astype(i32), bounds)
    return words, bounds


def as_table(pieces, table_v, table, sem):
    at = 0
    for piece in pieces:
        table_v[at : at + piece.shape[0], :] = piece
        at += piece.shape[0]
    copy = pltpu.make_async_copy(table_v, table, sem)
    copy.start()
    return copy


def fills_of(fills, block):
    return rows_dot(stacked(fills, block.shape[1]), equal_rows(block, halves * lanes), 0).astype(i32)


def column_shares(lists, row, last_row):
    fill, own, offset, block, count = lists
    size = halves * lanes
    live = lax.broadcasted_iota(i32, (1, size), 1) < count
    dr = third(offset)
    column = live & (offset - 3 * dr == 1)
    marks = [column & (dr == k) for k in range(3)]
    rank = running(stacked(marks, size)).astype(i32)
    odd = [(rank[k : k + 1] & 1) == 1 for k in range(3)]
    spare = marks[1] & (rank[1:2] > kept)
    has_north, has_south = row > 0, row < last_row
    to_north = spare & has_north & odd[1]
    to_south = spare & has_south & jnp.logical_not(odd[1])
    inside = marks[1] & jnp.logical_not(to_north | to_south)
    return (
        (marks[0] & odd[0], inside, marks[2] & odd[2]),
        ((marks[0] & jnp.logical_not(odd[0])), to_north),
        ((marks[2] & jnp.logical_not(odd[2])), to_south),
    )


def column_entries(lists, base_row, fills):
    fill, own, offset, block, count = lists
    size = halves * lanes
    a = base_row * size + own
    target = base_row + third(offset) - 1
    b = target * size + block
    near = fills_of(fills, block)
    fill_b = jnp.where(target == 0, near[0:1], jnp.where(target == 1, near[1:2], near[2:3]))
    return a, b, fills_of([fill], own)[0:1], fill_b


def level_kernel(rows, total, last_row, tile_ref, g_tile, src, grad, table_v, table, sem, *buffers):
    blocks = rows // halves
    lists = lists_of(tile_ref, rows)
    mine, _, _ = column_shares(lists, lax.axis_index("ty"), last_row)
    fills = [jnp.zeros_like(lists[0]), lists[0], jnp.zeros_like(lists[0])]
    words, bounds = sorted_pairs([(*column_entries(lists, 1, fills), mine[1])])
    copy = as_table((*map(two_rows, fills), jnp.zeros((5, lanes), i32), bounds, two_rows(words)), table_v, table, sem)
    for f in range(fields):
        src[f * total + rows : f * total + 2 * rows, :] = tile_ref[f * rows : (f + 1) * rows, :]
    for f in range(axes):
        grad[f * total + rows : f * total + 2 * rows, :] = jnp.zeros((rows, lanes), f32)
    copy.wait()
    pair_loops(total, 3 * blocks, table, src, grad, buffers)
    for f in range(axes):
        g_tile[f * rows : (f + 1) * rows, :] = grad[f * total + rows : f * total + 2 * rows, :]


def column_kernel(rows, total, last_row, tile_ref, north_ref, south_ref, start_ref, g_tile, g_north, g_south,
                  src, grad, table_v, table, sem, *buffers):
    blocks = rows // halves
    row = lax.axis_index("ty")
    lists = [lists_of(ref, rows) for ref in (north_ref, tile_ref, south_ref)]
    fills = [l[0] for l in lists]
    shares = [column_shares(l, row + k - 1, last_row) for k, l in enumerate(lists)]
    wanted = (
        shares[0][2][0] | shares[0][2][1],
        shares[1][0][0] | shares[1][0][2],
        shares[2][1][0] | shares[2][1][1],
    )
    words, bounds = sorted_pairs([(*column_entries(l, k, fills), wanted[k]) for k, l in enumerate(lists)])
    copy = as_table((*map(two_rows, fills), jnp.zeros((5, lanes), i32), bounds, two_rows(words)), table_v, table, sem)
    for ref, base in ((north_ref, 0), (tile_ref, rows), (south_ref, 2 * rows)):
        for f in range(fields):
            src[f * total + base : f * total + base + rows, :] = ref[f * rows : (f + 1) * rows, :]
    for f in range(axes):
        grad[f * total : f * total + rows, :] = jnp.zeros((rows, lanes), f32)
        grad[f * total + rows : f * total + 2 * rows, :] = start_ref[f * rows : (f + 1) * rows, :]
        grad[f * total + 2 * rows : f * total + 3 * rows, :] = jnp.zeros((rows, lanes), f32)
    copy.wait()
    pair_loops(total, 3 * blocks, table, src, grad, buffers)
    for ref, base in ((g_north, 0), (g_tile, rows), (g_south, 2 * rows)):
        for f in range(axes):
            ref[f * rows : (f + 1) * rows, :] = grad[f * total + base : f * total + base + rows, :]


def side_kernel(slots, rows, total, level, tiles, east_ref, west_ref, g_tiles, g_east, g_west,
                o_tiles, o_east, o_west, src, grad, table_v, table, sem, *buffers):
    blocks = rows // halves
    slot_rows = halves * slots
    size = halves * lanes
    bases = (rows,) if level else (0, 2 * rows)
    fills = [jnp.zeros((1, size), i32)] * 3
    if level:
        fills[1] = lists_of(tiles[0], rows)[0]
    else:
        fills[0], fills[2] = (lists_of(t, rows)[0] for t in tiles)
    east_base, west_base = 6 * lanes, 8 * lanes
    slot_id = lax.broadcasted_iota(i32, (1, size), 1)
    entries, slot_fills = [], []
    for ref, base in ((east_ref, east_base), (west_ref, west_base)):
        meta = ref[fields * slot_rows : fields * slot_rows + meta_rows, :].astype(i32)
        if level:
            live = (slot_id >= slots - meta[6:7, 1:2]) & (slot_id < slots)
        else:
            live = slot_id < meta[6:7, 0:1]
        block, fill, dr = (jnp.where(live, one_row(meta[2 * k : 2 * k + 2]), 0) for k in range(3))
        near = fills_of(fills, block)
        fill_b = near[1:2] if level else jnp.where(dr == 0, near[0:1], near[2:3])
        entries.append((base + slot_id, dr * blocks + block, fill, fill_b, live))
        slot_fills.append(fill)
    words, bounds = sorted_pairs(entries)
    copy = as_table((*map(two_rows, fills), *map(two_rows, slot_fills), jnp.zeros((1, lanes), i32), bounds, two_rows(words)),
                    table_v, table, sem)
    slot_places = ((east_ref, halves * east_base), (west_ref, halves * west_base))
    for ref, base in zip(tiles, bases):
        for f in range(fields):
            src[f * total + base : f * total + base + rows, :] = ref[f * rows : (f + 1) * rows, :]
    for ref, base in slot_places:
        for f in range(fields):
            src[f * total + base : f * total + base + slot_rows, :] = ref[f * slot_rows : (f + 1) * slot_rows, :]
    for ref, base in zip(g_tiles, bases):
        for f in range(axes):
            grad[f * total + base : f * total + base + rows, :] = ref[f * rows : (f + 1) * rows, :]
    for ref, (_, base) in zip((g_east, g_west), slot_places):
        for f in range(axes):
            init = jnp.zeros((slot_rows, lanes), f32) if ref is None else ref[f * slot_rows : (f + 1) * slot_rows, :]
            grad[f * total + base : f * total + base + slot_rows, :] = init
    copy.wait()
    pair_loops(total, 10 * lanes, table, src, grad, buffers)
    for ref, base in zip(o_tiles, bases):
        for f in range(axes):
            ref[f * rows : (f + 1) * rows, :] = grad[f * total + base : f * total + base + rows, :]
    for ref, (_, base) in zip((o_east, o_west), slot_places):
        for f in range(axes):
            ref[f * slot_rows : (f + 1) * slot_rows, :] = grad[f * total + base : f * total + base + slot_rows, :]


def merge_kernel(slots, rows, origin_ref, g_tile, g_north, g_south, g_east, g_west, out_ref):
    blocks = rows // halves
    slot_rows = halves * slots
    placed = [equal_rows(origin_ref[side : side + 1, :][:, :slots], blocks) for side in range(2)]
    out_ref[...] = g_tile[...] + g_north[...] + g_south[...]
    for f in range(axes):
        got = jnp.zeros((blocks, halves * lanes), f32)
        for place, ref in zip(placed, (g_east, g_west)):
            data = jnp.concatenate([ref[pl.ds(f * slot_rows + h, slots, stride=halves), :] for h in range(halves)], axis=1)
            for part in split3(data):
                got = got + rows_dot(place, part, 0)
        for h in range(halves):
            at = pl.ds(f * rows + h, blocks, stride=halves)
            out_ref[at, :] = out_ref[at, :] + got[:, h * lanes : (h + 1) * lanes]


def shifted(x, axis, by):
    devices = lax.axis_size(axis)
    pairs = [(i, i + by) for i in range(devices) if 0 <= i + by < devices]
    return lax.ppermute(x, axis, pairs)


vmem = pl.BlockSpec(memory_space=pltpu.VMEM)
smem = pl.BlockSpec(memory_space=pltpu.SMEM)
in_hbm = pl.BlockSpec(memory_space=pltpu.HBM)


def sds(n):
    return jax.ShapeDtypeStruct((n, lanes), f32)


def params(mib):
    return pltpu.CompilerParams(vmem_limit_bytes=mib << 20)


def pair_scratch(total, sets):
    return [
        pltpu.VMEM((fields * total, lanes), f32),
        pltpu.VMEM((axes * total, lanes), f32),
        pltpu.VMEM((12 + halves * sets, lanes), i32),
        pltpu.SMEM((12 + halves * sets, lanes), i32),
        pltpu.SemaphoreType.DMA,
        pltpu.VMEM((halves * lanes, fields * lanes), f32),
        pltpu.VMEM((halves * lanes, fields * lanes), f32),
        pltpu.VMEM((8, halves * lanes), f32),
        pltpu.VMEM((8, halves * lanes), f32),
        pltpu.VMEM((axes * halves * lanes, lanes), f32),
        pltpu.VMEM((axes * halves * lanes, lanes), f32),
        pltpu.VMEM((axes * 8, halves * lanes), f32),
        pltpu.VMEM((axes * 8, halves * lanes), f32),
    ]


def level_call(rows, last_row, tile):
    total = 3 * rows + 8
    return pl.pallas_call(
        lambda *refs: level_kernel(rows, total, last_row, *refs),
        out_shape=sds(axes * rows),
        in_specs=[vmem],
        out_specs=vmem,
        scratch_shapes=pair_scratch(total, 1),
        compiler_params=params(24),
        name="pairs_inside",
    )(tile)


def column_call(rows, last_row, tile, north, south, g_tile):
    total = 3 * rows + 8
    return pl.pallas_call(
        lambda *refs: column_kernel(rows, total, last_row, *refs),
        out_shape=(sds(axes * rows),) * 3,
        in_specs=[vmem] * 4,
        out_specs=(vmem,) * 3,
        scratch_shapes=pair_scratch(total, 3),
        compiler_params=params(24),
        name="pairs_column",
    )(tile, north, south, g_tile)


def side_call(slots, rows, level, tiles, east, west, g_tiles, g_slots):
    total = 3 * rows + 4 * halves * lanes + 8
    n, m = len(tiles), len(g_slots)

    def run(*refs):
        refs = list(refs)
        take = lambda k: [refs.pop(0) for _ in range(k)]
        t = take(n)
        e, w = take(2)
        g = take(n)
        ge, gw = take(2) if m else (None, None)
        o = take(n)
        oe, ow = take(2)
        side_kernel(slots, rows, total, level, t, e, w, g, ge, gw, o, oe, ow, *refs)

    return pl.pallas_call(
        run,
        out_shape=(sds(axes * rows),) * n + (sds(axes * halves * slots),) * 2,
        in_specs=[vmem] * (n + 2 + n + m),
        out_specs=(vmem,) * (n + 2),
        scratch_shapes=pair_scratch(total, 2),
        compiler_params=params(32),
        name="pairs_level" if level else "pairs_cross",
    )(*tiles, east, west, *g_tiles, *g_slots)


def body(locations, solution, cotangent, block_fill, pair_own, pair_offset, pair_block, pair_count):
    points = solution.shape[2]
    slots = pair_own.shape[2]
    rows = points // lanes
    blocks = rows // halves
    own = pair_own.reshape(1, slots)
    offset = pair_offset.reshape(1, slots)
    block = pair_block.reshape(1, slots)
    count = pair_count.reshape(1, 1)
    fill = block_fill.reshape(1, blocks)
    slot_rows = fields * halves * slots + meta_rows
    last_row = lax.axis_size("ty") - 1
    tile = pl.pallas_call(
        lambda *refs: tile_kernel(rows, slots, *refs),
        out_shape=sds(fields * rows + meta_rows),
        in_specs=[in_hbm] * 8,
        out_specs=in_hbm,
        scratch_shapes=[pltpu.SMEM((1, 1), i32), pltpu.VMEM((1, blocks), i32), pltpu.VMEM((3, 1, slots), i32),
                        pltpu.VMEM((meta_rows, lanes), f32), pltpu.SemaphoreType.DMA((9,))],
        compiler_params=params(60),
        name="tile",
    )(count, fill, own, offset, block, locations.reshape(axes * rows, lanes), solution.reshape(rows, lanes),
      cotangent.reshape(rows, lanes))
    north = shifted(tile, "ty", 1)
    south = shifted(tile, "ty", -1)
    to_east, to_west, origin = pl.pallas_call(
        lambda *refs: pack_kernel(slots, rows, *refs),
        out_shape=(sds(slot_rows), sds(slot_rows), jax.ShapeDtypeStruct((8, halves * lanes), f32)),
        in_specs=[vmem],
        out_specs=(vmem,) * 3,
        compiler_params=params(16),
        name="pack",
    )(tile)
    from_west = shifted(to_east, "tx", 1)
    from_east = shifted(to_west, "tx", -1)
    g_tile = level_call(rows, last_row, tile)
    g_tile, g_north, g_south = column_call(rows, last_row, tile, north, south, g_tile)
    g_north, g_south, g_west, g_east = side_call(
        slots, rows, False, (north, south), from_west, from_east, (g_north, g_south), ())
    back_south = shifted(g_north, "ty", -1)
    back_north = shifted(g_south, "ty", 1)
    g_tile, g_west, g_east = side_call(
        slots, rows, True, (tile,), from_west, from_east, (g_tile,), (g_west, g_east))
    back_east = shifted(g_west, "tx", -1)
    back_west = shifted(g_east, "tx", 1)
    out = pl.pallas_call(
        lambda *refs: merge_kernel(slots, rows, *refs),
        out_shape=sds(axes * rows),
        in_specs=[vmem] * 6,
        out_specs=vmem,
        compiler_params=params(16),
        name="merge",
    )(origin, g_tile, back_north, back_south, back_east, back_west)
    return out.reshape(locations.shape)


def solution(mesh):
    placed = (
        P("ty", "tx", None, None),
        P("ty", "tx", None),
        P("ty", "tx", None),
        P("ty", "tx", None),
        P("ty", "tx", None),
        P("ty", "tx", None),
        P("ty", "tx", None),
        P("ty", "tx"),
    )
    return jax.shard_map(
        body, mesh=mesh, in_specs=placed, out_specs=P("ty", "tx", None, None), check_vma=False
    )
```

```python
import jax
import jax.numpy as jnp
from jax import lax
from jax.experimental import pallas as pl
from jax.experimental.pallas import tpu as pltpu
from jax.sharding import PartitionSpec as P

lanes = 128
halves = 2
fields = 5
axes = 3
meta_rows = 8
kinds = 5
kept = 32
bf16 = jnp.bfloat16
f32 = jnp.float32
i32 = jnp.int32


def third(heading):
    return (heading * 11) >> 5


def note_kernel(count_ref, fill_ref, own_ref, offset_ref, block_ref, note_ref, count_s, fill_v, lists_v, sem):
    copies = (
        pltpu.make_async_copy(fill_ref, fill_v, sem.at[0]),
        pltpu.make_async_copy(own_ref, lists_v.at[0], sem.at[1]),
        pltpu.make_async_copy(offset_ref, lists_v.at[1], sem.at[2]),
        pltpu.make_async_copy(block_ref, lists_v.at[2], sem.at[3]),
        pltpu.make_async_copy(count_ref, count_s, sem.at[4]),
    )
    for c in copies:
        c.start()
    for c in copies:
        c.wait()
    own, offset, block = (wide(lists_v[k]) for k in range(3))
    last = lax.broadcasted_iota(i32, own.shape, 1) == own.shape[1] - 1
    own = jnp.where(last, count_s[0, 0], own)
    note_ref[...] = jnp.concatenate([two_rows(x) for x in (fill_v[...], own, offset, block)], axis=0).astype(f32)


def lists_of(ref, rows):
    meta = ref[fields * rows : fields * rows + meta_rows, :].astype(i32)
    parts = [one_row(meta[2 * k : 2 * k + 2]) for k in range(4)]
    return (*parts, parts[1][:, halves * lanes - 1 :])


def rows_dot(x, y, contract):
    return lax.dot_general(x.astype(bf16), y.astype(bf16), (((1,), (contract,)), ((), ())), preferred_element_type=f32)


def split3(x):
    high = x.astype(bf16).astype(f32)
    rest = x - high
    mid = rest.astype(bf16).astype(f32)
    return high, mid, rest - mid


def stacked(rows, width):
    rows = [r.astype(f32) for r in rows]
    return jnp.concatenate(rows + [jnp.zeros((8 - len(rows), width), f32)], axis=0)


def wide(row):
    missing = halves * lanes - row.shape[1]
    return row if missing == 0 else jnp.concatenate([row, jnp.zeros((1, missing), row.dtype)], axis=1)


def one_row(x):
    return jnp.concatenate([x[0:1], x[1:2]], axis=1)


def two_rows(x):
    return jnp.concatenate([x[:, h * lanes : (h + 1) * lanes] for h in range(x.shape[1] // lanes)], axis=0)


def equal_rows(row, count, first=0):
    at = lax.broadcasted_iota(i32, (count, row.shape[1]), 0) + first
    return (row.astype(i32) == at).astype(f32).astype(bf16)


def running(flags):
    size = halves * lanes
    upper = lax.broadcasted_iota(i32, (size, size), 0) <= lax.broadcasted_iota(i32, (size, size), 1)
    return rows_dot(flags, upper.astype(f32), 0)


def pack_kernel(slots, rows, tile_ref, east_ref, west_ref, origin_ref):
    blocks = rows // halves
    size = halves * lanes
    slot_rows = halves * slots
    fill, own, offset, block, count = lists_of(tile_ref, rows)
    live = lax.broadcasted_iota(i32, (1, size), 1) < count
    dr = third(offset)
    dc = offset - 3 * dr
    level = dr == 1
    marks = [live & (dc == want) & (level == back) for want in (2, 0) for back in (False, True)]
    counts = running(stacked(marks, size))
    picked = equal_rows(own, blocks)
    fill = rows_dot(stacked([fill], size), picked, 0)[0:1]
    values = stacked([block, fill, dr, own + 1], size)
    lane_id = lax.broadcasted_iota(i32, (1, lanes), 1)
    chosen = []
    for side, out_ref in enumerate((east_ref, west_ref)):
        front, back = marks[2 * side], marks[2 * side + 1]
        front_n, back_n = counts[2 * side : 2 * side + 1], counts[2 * side + 1 : 2 * side + 2]
        place = jnp.where(front, front_n - 1.0, jnp.where(back, slots - back_n, -1.0))
        moved = equal_rows(place, slots)
        meta = rows_dot(values, moved, 1)
        meta = jnp.concatenate([meta, jnp.zeros((8, size - slots), f32)], axis=1)
        ends = jnp.where(lane_id == 0, front_n[:, size - 1 :], jnp.where(lane_id == 1, back_n[:, size - 1 :], 0.0))
        out_ref[fields * slot_rows : fields * slot_rows + meta_rows, :] = jnp.concatenate(
            [two_rows(meta[k : k + 1]) for k in range(3)] + [ends, jnp.zeros((1, lanes), f32)], axis=0)
        origin_ref[side : side + 1, :] = meta[3:4] - 1.0
        chosen.append(rows_dot(moved, picked, 1).astype(bf16))
    for f in range(fields):
        data = jnp.concatenate([tile_ref[pl.ds(f * rows + h, blocks, stride=halves), :] for h in range(halves)], axis=1)
        parts = split3(data)
        for pick, out_ref in zip(chosen, (east_ref, west_ref)):
            got = rows_dot(pick, parts[0], 0) + rows_dot(pick, parts[1], 0) + rows_dot(pick, parts[2], 0)
            for h in range(halves):
                out_ref[pl.ds(f * slot_rows + h, slots, stride=halves), :] = got[:, h * lanes : (h + 1) * lanes]


def shape_of(kind):
    steps = (16, 24, 16, 24, 32)[kind]
    return steps, -(-steps // 16), (1, 1, 2, 2, 2)[kind]


def pair_loops(total, spare, table, src, grad, buffers):
    size = halves * lanes

    def word_at(k, at):
        place = table[11, k] + at
        return table[12 + (place >> 7), place & 127]

    def load(index, fill, parts):
        size = parts * lanes
        row_id = lax.broadcasted_iota(i32, (8, size), 0)
        lane_id = lax.broadcasted_iota(i32, (8, size), 1)
        pieces = []
        for h in range(parts):
            got = src[pl.ds(halves * index + h, fields, stride=total), :]
            pieces.append(jnp.concatenate([got, jnp.zeros((8 - fields, lanes), f32)], axis=0))
        x = jnp.concatenate(pieces, axis=1)
        return jnp.where((row_id < axes) | (lane_id < fill), x, 0.0)

    def spread(k, at, mixed, partner):
        steps, parts_a, parts_b = shape_of(k)
        word = word_at(k, at)
        ia, ib = word & 4095, word >> 12
        live = at < table[11, 8 + k]
        a = load(ia, jnp.where(live, table[ia >> 7, ia & 127], 0), parts_a)
        b = load(ib, jnp.where(live, table[ib >> 7, ib & 127], 0), parts_b)
        partner[:, : parts_b * lanes] = b
        zero = jnp.zeros((8, lanes), f32)
        row_b = lax.broadcasted_iota(i32, b.shape, 0)
        ah, am, al = split3(a)
        left = jnp.concatenate([ah, am, al, ah, ah, am], axis=0).astype(bf16)
        swapped = jnp.where(row_b == 3, jnp.roll(b, -1, axis=0), jnp.where(row_b == 4, jnp.roll(b, 1, axis=0), 0.0))
        sh, sm, sl = split3(swapped * -20.0)
        right = jnp.concatenate([sh, sh, sh, sm, sl, sm], axis=0).astype(bf16)
        row_id = lax.broadcasted_iota(i32, (8, lanes), 0)
        units = [(row_id == f).astype(f32) for f in range(axes)]
        pick = jnp.concatenate([jnp.concatenate([u, u, u, zero, zero, zero], axis=0) for u in units], axis=1).astype(bf16)
        mixed[: parts_a * lanes, : (axes + parts_b) * lanes] = lax.dot_general(
            left, jnp.concatenate([pick, right], axis=1), (((0,), (0,)), ((), ())), preferred_element_type=f32)

    def work(k, mixed, partner, own, far):
        steps, parts_a, parts_b = shape_of(k)
        b_rows = [
            [jnp.broadcast_to(partner[f : f + 1, p * lanes : (p + 1) * lanes], (8, lanes)) for f in range(axes)]
            for p in range(parts_b)
        ]
        sums = [[None] * axes for _ in range(parts_b)]
        for g in range(steps):
            rows = slice(8 * g, 8 * g + 8)
            a_cols = [mixed[rows, f * lanes : (f + 1) * lanes] for f in range(axes)]
            mine = [None] * axes
            for p in range(parts_b):
                diff = [a_cols[f] - b_rows[p][f] for f in range(axes)]
                square = diff[0] * diff[0] + diff[1] * diff[1] + diff[2] * diff[2]
                square = jnp.maximum(square, 1e-30)
                reach = jnp.maximum(1.0 - square * lax.rsqrt(square), 0.0)
                w = (reach * reach) * (reach * mixed[rows, (axes + p) * lanes : (axes + p + 1) * lanes])
                for f in range(axes):
                    push = w * diff[f]
                    mine[f] = push if p == 0 else mine[f] + push
                    sums[p][f] = push if g == 0 else sums[p][f] + push
            for f in range(axes):
                own[f * size + 8 * g : f * size + 8 * g + 8, :] = mine[f]
        for p in range(parts_b):
            for f in range(axes):
                far[8 * f : 8 * f + 8, p * lanes : (p + 1) * lanes] = sums[p][f]

    def finish(k, at, own, far):
        steps, parts_a, parts_b = shape_of(k)
        word = jnp.where(at < 0, spare | (spare << 12), word_at(k, jnp.maximum(at, 0)))
        ia, ib = word & 4095, word >> 12
        for h in range(parts_a):
            count = min(lanes, 8 * steps - h * lanes)
            rows = []
            for f in range(axes):
                part = own[f * size + h * lanes : f * size + h * lanes + count, :]
                if count < lanes:
                    part = jnp.concatenate([part, jnp.zeros((lanes - count, lanes), f32)], axis=0)
                rows.append(jnp.sum(part.T, axis=0, keepdims=True))
            place = pl.ds(halves * ia + h, axes, stride=total)
            grad[place, :] = grad[place, :] + jnp.concatenate(rows, axis=0)
        for p in range(parts_b):
            rows = [jnp.sum(far[8 * f : 8 * f + 8, p * lanes : (p + 1) * lanes], axis=0, keepdims=True) for f in range(axes)]
            place = pl.ds(halves * ib + p, axes, stride=total)
            grad[place, :] = grad[place, :] - jnp.concatenate(rows, axis=0)

    mixed0, mixed1, partner0, partner1, own0, own1, far0, far1 = buffers
    for k in range(kinds):
        turns = (table[11, 8 + k] + 1) // 2

        def turn(t, carry, k=k):
            at = 2 * t
            finish(k, at - 1, own1, far1)
            work(k, mixed0, partner0, own0, far0)
            spread(k, at + 1, mixed1, partner1)
            finish(k, at, own0, far0)
            work(k, mixed1, partner1, own1, far1)
            spread(k, at + 2, mixed0, partner0)
            return carry

        @pl.when(turns > 0)
        def _(k=k, turns=turns, turn=turn):
            spread(k, 0, mixed0, partner0)
            lax.fori_loop(0, turns, turn, 0)
            finish(k, 2 * turns - 1, own1, far1)


def sorted_pairs(entries):
    size = halves * lanes
    found = []
    for a, b, fill_a, fill_b, live in entries:
        size_a, size_b = (fill_a + 63) >> 6, (fill_b + 63) >> 6
        two_a, two_b = (size_a > 2).astype(i32), (size_b > 2).astype(i32)
        swap = (size_a * (1 + two_b) > size_b * (1 + two_a)) | ((size_a > 3) & (size_b < 3))
        a, b = jnp.where(swap, b, a), jnp.where(swap, a, b)
        size_a, size_b = jnp.where(swap, size_b, size_a), jnp.where(swap, size_a, size_b)
        kind = jnp.maximum(size_a - 2, 0) + jnp.where(size_b > 2, 2, 0)
        marks = [live & (kind == k) for k in range(kinds)]
        counts = running(stacked(marks, size))
        values = stacked([a & 255, a >> 8, b & 255, b >> 8], size)
        found.append((marks, counts, values))
    firsts, totals = [], []
    at = jnp.zeros((1, 1), f32)
    for k in range(kinds):
        firsts.append(at)
        total = sum(counts[k : k + 1, size - 1 :] for _, counts, _ in found)
        totals.append(total)
        at = at + total
    length = size * len(entries)
    ordered = jnp.zeros((8, length), f32)
    before = firsts
    for marks, counts, values in found:
        place = jnp.full((1, size), -1.0, f32)
        for k in range(kinds):
            place = jnp.where(marks[k], before[k] + counts[k : k + 1] - 1.0, place)
        before = [before[k] + counts[k : k + 1, size - 1 :] for k in range(kinds)]
        ordered = ordered + rows_dot(values, equal_rows(place, length), 1)
    ordered = ordered.astype(i32)
    words = ordered[0:1] + (ordered[1:2] << 8) + (ordered[2:3] << 12) + (ordered[3:4] << 20)
    lane_id = lax.broadcasted_iota(i32, (1, lanes), 1)
    bounds = jnp.zeros((1, lanes), i32)
    for k in range(kinds):
        bounds = jnp.where(lane_id == k, firsts[k].astype(i32), bounds)
        bounds = jnp.where(lane_id == 8 + k, totals[k].astype(i32), bounds)
    return words, bounds


def as_table(pieces, table_v, table, sem):
    at = 0
    for piece in pieces:
        table_v[at : at + piece.shape[0], :] = piece
        at += piece.shape[0]
    copy = pltpu.make_async_copy(table_v, table, sem)
    copy.start()
    return copy


def fills_of(fills, block):
    return rows_dot(stacked(fills, block.shape[1]), equal_rows(block, halves * lanes), 0).astype(i32)


def column_shares(lists, row, last_row):
    fill, own, offset, block, count = lists
    size = halves * lanes
    live = lax.broadcasted_iota(i32, (1, size), 1) < count
    dr = third(offset)
    column = live & (offset - 3 * dr == 1)
    marks = [column & (dr == k) for k in range(3)]
    rank = running(stacked(marks, size)).astype(i32)
    odd = [(rank[k : k + 1] & 1) == 1 for k in range(3)]
    spare = marks[1] & (rank[1:2] > kept)
    has_north, has_south = row > 0, row < last_row
    to_north = spare & has_north & odd[1]
    to_south = spare & has_south & jnp.logical_not(odd[1])
    inside = marks[1] & jnp.logical_not(to_north | to_south)
    return (
        (marks[0] & odd[0], inside, marks[2] & odd[2]),
        ((marks[0] & jnp.logical_not(odd[0])), to_north),
        ((marks[2] & jnp.logical_not(odd[2])), to_south),
    )


def column_entries(lists, base_row, fills):
    fill, own, offset, block, count = lists
    size = halves * lanes
    a = base_row * size + own
    target = base_row + third(offset) - 1
    b = target * size + block
    near = fills_of(fills, block)
    fill_b = jnp.where(target == 0, near[0:1], jnp.where(target == 1, near[1:2], near[2:3]))
    return a, b, fills_of([fill], own)[0:1], fill_b


def level_kernel(rows, total, last_row, tile_ref, g_tile, src, grad, table_v, table, sem, *buffers):
    blocks = rows // halves
    lists = lists_of(tile_ref, rows)
    mine, _, _ = column_shares(lists, lax.axis_index("ty"), last_row)
    fills = [jnp.zeros_like(lists[0]), lists[0], jnp.zeros_like(lists[0])]
    words, bounds = sorted_pairs([(*column_entries(lists, 1, fills), mine[1])])
    copy = as_table((*map(two_rows, fills), jnp.zeros((5, lanes), i32), bounds, two_rows(words)), table_v, table, sem)
    for f in range(fields):
        src[f * total + rows : f * total + 2 * rows, :] = tile_ref[f * rows : (f + 1) * rows, :]
    for f in range(axes):
        grad[f * total + rows : f * total + 2 * rows, :] = jnp.zeros((rows, lanes), f32)
    copy.wait()
    pair_loops(total, 3 * blocks, table, src, grad, buffers)
    for f in range(axes):
        g_tile[f * rows : (f + 1) * rows, :] = grad[f * total + rows : f * total + 2 * rows, :]


def column_kernel(rows, total, last_row, tile_ref, north_ref, south_ref, start_ref, g_tile, g_north, g_south,
                  src, grad, table_v, table, sem, *buffers):
    blocks = rows // halves
    row = lax.axis_index("ty")
    lists = [lists_of(ref, rows) for ref in (north_ref, tile_ref, south_ref)]
    fills = [l[0] for l in lists]
    shares = [column_shares(l, row + k - 1, last_row) for k, l in enumerate(lists)]
    wanted = (
        shares[0][2][0] | shares[0][2][1],
        shares[1][0][0] | shares[1][0][2],
        shares[2][1][0] | shares[2][1][1],
    )
    words, bounds = sorted_pairs([(*column_entries(l, k, fills), wanted[k]) for k, l in enumerate(lists)])
    copy = as_table((*map(two_rows, fills), jnp.zeros((5, lanes), i32), bounds, two_rows(words)), table_v, table, sem)
    for ref, base in ((north_ref, 0), (tile_ref, rows), (south_ref, 2 * rows)):
        for f in range(fields):
            src[f * total + base : f * total + base + rows, :] = ref[f * rows : (f + 1) * rows, :]
    for f in range(axes):
        grad[f * total : f * total + rows, :] = jnp.zeros((rows, lanes), f32)
        grad[f * total + rows : f * total + 2 * rows, :] = start_ref[f * rows : (f + 1) * rows, :]
        grad[f * total + 2 * rows : f * total + 3 * rows, :] = jnp.zeros((rows, lanes), f32)
    copy.wait()
    pair_loops(total, 3 * blocks, table, src, grad, buffers)
    for ref, base in ((g_north, 0), (g_tile, rows), (g_south, 2 * rows)):
        for f in range(axes):
            ref[f * rows : (f + 1) * rows, :] = grad[f * total + base : f * total + base + rows, :]


def side_kernel(slots, rows, total, level, tiles, east_ref, west_ref, g_tiles, g_east, g_west,
                o_tiles, o_east, o_west, src, grad, table_v, table, sem, *buffers):
    blocks = rows // halves
    slot_rows = halves * slots
    size = halves * lanes
    bases = (rows,) if level else (0, 2 * rows)
    fills = [jnp.zeros((1, size), i32)] * 3
    if level:
        fills[1] = lists_of(tiles[0], rows)[0]
    else:
        fills[0], fills[2] = (lists_of(t, rows)[0] for t in tiles)
    east_base, west_base = 6 * lanes, 8 * lanes
    slot_id = lax.broadcasted_iota(i32, (1, size), 1)
    entries, slot_fills = [], []
    for ref, base in ((east_ref, east_base), (west_ref, west_base)):
        meta = ref[fields * slot_rows : fields * slot_rows + meta_rows, :].astype(i32)
        if level:
            live = (slot_id >= slots - meta[6:7, 1:2]) & (slot_id < slots)
        else:
            live = slot_id < meta[6:7, 0:1]
        block, fill, dr = (jnp.where(live, one_row(meta[2 * k : 2 * k + 2]), 0) for k in range(3))
        near = fills_of(fills, block)
        fill_b = near[1:2] if level else jnp.where(dr == 0, near[0:1], near[2:3])
        entries.append((base + slot_id, dr * blocks + block, fill, fill_b, live))
        slot_fills.append(fill)
    words, bounds = sorted_pairs(entries)
    copy = as_table((*map(two_rows, fills), *map(two_rows, slot_fills), jnp.zeros((1, lanes), i32), bounds, two_rows(words)),
                    table_v, table, sem)
    slot_places = ((east_ref, halves * east_base), (west_ref, halves * west_base))
    for ref, base in zip(tiles, bases):
        for f in range(fields):
            src[f * total + base : f * total + base + rows, :] = ref[f * rows : (f + 1) * rows, :]
    for ref, base in slot_places:
        for f in range(fields):
            src[f * total + base : f * total + base + slot_rows, :] = ref[f * slot_rows : (f + 1) * slot_rows, :]
    for ref, base in zip(g_tiles, bases):
        for f in range(axes):
            grad[f * total + base : f * total + base + rows, :] = ref[f * rows : (f + 1) * rows, :]
    for ref, (_, base) in zip((g_east, g_west), slot_places):
        for f in range(axes):
            init = jnp.zeros((slot_rows, lanes), f32) if ref is None else ref[f * slot_rows : (f + 1) * slot_rows, :]
            grad[f * total + base : f * total + base + slot_rows, :] = init
    copy.wait()
    pair_loops(total, 10 * lanes, table, src, grad, buffers)
    for ref, base in zip(o_tiles, bases):
        for f in range(axes):
            ref[f * rows : (f + 1) * rows, :] = grad[f * total + base : f * total + base + rows, :]
    for ref, (_, base) in zip((o_east, o_west), slot_places):
        for f in range(axes):
            ref[f * slot_rows : (f + 1) * slot_rows, :] = grad[f * total + base : f * total + base + slot_rows, :]


def merge_kernel(slots, rows, origin_ref, g_tile, g_north, g_south, g_east, g_west, out_ref):
    blocks = rows // halves
    slot_rows = halves * slots
    placed = [equal_rows(origin_ref[side : side + 1, :][:, :slots], blocks) for side in range(2)]
    out_ref[...] = g_tile[...] + g_north[...] + g_south[...]
    for f in range(axes):
        got = jnp.zeros((blocks, halves * lanes), f32)
        for place, ref in zip(placed, (g_east, g_west)):
            data = jnp.concatenate([ref[pl.ds(f * slot_rows + h, slots, stride=halves), :] for h in range(halves)], axis=1)
            for part in split3(data):
                got = got + rows_dot(place, part, 0)
        for h in range(halves):
            at = pl.ds(f * rows + h, blocks, stride=halves)
            out_ref[at, :] = out_ref[at, :] + got[:, h * lanes : (h + 1) * lanes]


def shifted(x, axis, by):
    devices = lax.axis_size(axis)
    pairs = [(i, i + by) for i in range(devices) if 0 <= i + by < devices]
    return lax.ppermute(x, axis, pairs)


vmem = pl.BlockSpec(memory_space=pltpu.VMEM)
smem = pl.BlockSpec(memory_space=pltpu.SMEM)
in_hbm = pl.BlockSpec(memory_space=pltpu.HBM)


def sds(n):
    return jax.ShapeDtypeStruct((n, lanes), f32)


def params(mib):
    return pltpu.CompilerParams(vmem_limit_bytes=mib << 20)


def pair_scratch(total, sets):
    return [
        pltpu.VMEM((fields * total, lanes), f32),
        pltpu.VMEM((axes * total, lanes), f32),
        pltpu.VMEM((12 + halves * sets, lanes), i32),
        pltpu.SMEM((12 + halves * sets, lanes), i32),
        pltpu.SemaphoreType.DMA,
        pltpu.VMEM((halves * lanes, fields * lanes), f32),
        pltpu.VMEM((halves * lanes, fields * lanes), f32),
        pltpu.VMEM((8, halves * lanes), f32),
        pltpu.VMEM((8, halves * lanes), f32),
        pltpu.VMEM((axes * halves * lanes, lanes), f32),
        pltpu.VMEM((axes * halves * lanes, lanes), f32),
        pltpu.VMEM((axes * 8, halves * lanes), f32),
        pltpu.VMEM((axes * 8, halves * lanes), f32),
    ]


def level_call(rows, last_row, tile):
    total = 3 * rows + 8
    return pl.pallas_call(
        lambda *refs: level_kernel(rows, total, last_row, *refs),
        out_shape=sds(axes * rows),
        in_specs=[vmem],
        out_specs=vmem,
        scratch_shapes=pair_scratch(total, 1),
        compiler_params=params(24),
        name="pairs_inside",
    )(tile)


def column_call(rows, last_row, tile, north, south, g_tile):
    total = 3 * rows + 8
    return pl.pallas_call(
        lambda *refs: column_kernel(rows, total, last_row, *refs),
        out_shape=(sds(axes * rows),) * 3,
        in_specs=[vmem] * 4,
        out_specs=(vmem,) * 3,
        scratch_shapes=pair_scratch(total, 3),
        compiler_params=params(24),
        name="pairs_column",
    )(tile, north, south, g_tile)


def side_call(slots, rows, level, tiles, east, west, g_tiles, g_slots):
    total = 3 * rows + 4 * halves * lanes + 8
    n, m = len(tiles), len(g_slots)

    def run(*refs):
        refs = list(refs)
        take = lambda k: [refs.pop(0) for _ in range(k)]
        t = take(n)
        e, w = take(2)
        g = take(n)
        ge, gw = take(2) if m else (None, None)
        o = take(n)
        oe, ow = take(2)
        side_kernel(slots, rows, total, level, t, e, w, g, ge, gw, o, oe, ow, *refs)

    return pl.pallas_call(
        run,
        out_shape=(sds(axes * rows),) * n + (sds(axes * halves * slots),) * 2,
        in_specs=[vmem] * (n + 2 + n + m),
        out_specs=(vmem,) * (n + 2),
        scratch_shapes=pair_scratch(total, 2),
        compiler_params=params(32),
        name="pairs_level" if level else "pairs_cross",
    )(*tiles, east, west, *g_tiles, *g_slots)


def body(locations, solution, cotangent, block_fill, pair_own, pair_offset, pair_block, pair_count):
    points = solution.shape[2]
    slots = pair_own.shape[2]
    rows = points // lanes
    blocks = rows // halves
    own = pair_own.reshape(1, slots)
    offset = pair_offset.reshape(1, slots)
    block = pair_block.reshape(1, slots)
    count = pair_count.reshape(1, 1)
    fill = block_fill.reshape(1, blocks)
    slot_rows = fields * halves * slots + meta_rows
    last_row = lax.axis_size("ty") - 1
    note = pl.pallas_call(
        note_kernel,
        out_shape=sds(meta_rows),
        in_specs=[in_hbm] * 5,
        out_specs=vmem,
        scratch_shapes=[pltpu.SMEM((1, 1), i32), pltpu.VMEM((1, blocks), i32), pltpu.VMEM((3, 1, slots), i32),
                        pltpu.SemaphoreType.DMA((5,))],
        compiler_params=params(60),
        name="note",
    )(count, fill, own, offset, block)
    tile = jnp.concatenate([locations.reshape(axes * rows, lanes), solution.reshape(rows, lanes),
                            cotangent.reshape(rows, lanes), note], axis=0)
    north = shifted(tile, "ty", 1)
    south = shifted(tile, "ty", -1)
    to_east, to_west, origin = pl.pallas_call(
        lambda *refs: pack_kernel(slots, rows, *refs),
        out_shape=(sds(slot_rows), sds(slot_rows), jax.ShapeDtypeStruct((8, halves * lanes), f32)),
        in_specs=[vmem],
        out_specs=(vmem,) * 3,
        compiler_params=params(16),
        name="pack",
    )(tile)
    from_west = shifted(to_east, "tx", 1)
    from_east = shifted(to_west, "tx", -1)
    g_tile = level_call(rows, last_row, tile)
    g_tile, g_north, g_south = column_call(rows, last_row, tile, north, south, g_tile)
    g_north, g_south, g_west, g_east = side_call(
        slots, rows, False, (north, south), from_west, from_east, (g_north, g_south), ())
    back_south = shifted(g_north, "ty", -1)
    back_north = shifted(g_south, "ty", 1)
    g_tile, g_west, g_east = side_call(
        slots, rows, True, (tile,), from_west, from_east, (g_tile,), (g_west, g_east))
    back_east = shifted(g_west, "tx", -1)
    back_west = shifted(g_east, "tx", 1)
    out = pl.pallas_call(
        lambda *refs: merge_kernel(slots, rows, *refs),
        out_shape=sds(axes * rows),
        in_specs=[vmem] * 6,
        out_specs=vmem,
        compiler_params=params(16),
        name="merge",
    )(origin, g_tile, back_north, back_south, back_east, back_west)
    return out.reshape(locations.shape)


def solution(mesh):
    placed = (
        P("ty", "tx", None, None),
        P("ty", "tx", None),
        P("ty", "tx", None),
        P("ty", "tx", None),
        P("ty", "tx", None),
        P("ty", "tx", None),
        P("ty", "tx", None),
        P("ty", "tx"),
    )
    return jax.shard_map(
        body, mesh=mesh, in_specs=placed, out_specs=P("ty", "tx", None, None), check_vma=False
    )
```

```python
import jax
import jax.numpy as jnp
from jax import lax
from jax.experimental import pallas as pl
from jax.experimental.pallas import tpu as pltpu
from jax.sharding import PartitionSpec as P

lanes = 128
halves = 2
fields = 5
axes = 3
meta_rows = 8
kinds = 5
kept = 32
bf16 = jnp.bfloat16
f32 = jnp.float32
i32 = jnp.int32


def third(heading):
    return (heading * 11) >> 5


def note_kernel(count_ref, fill_ref, own_ref, offset_ref, block_ref, note_ref, count_s, fill_v, lists_v, sem):
    copies = (
        pltpu.make_async_copy(fill_ref, fill_v, sem.at[0]),
        pltpu.make_async_copy(own_ref, lists_v.at[0], sem.at[1]),
        pltpu.make_async_copy(offset_ref, lists_v.at[1], sem.at[2]),
        pltpu.make_async_copy(block_ref, lists_v.at[2], sem.at[3]),
        pltpu.make_async_copy(count_ref, count_s, sem.at[4]),
    )
    for c in copies:
        c.start()
    for c in copies:
        c.wait()
    own, offset, block = (wide(lists_v[k]) for k in range(3))
    last = lax.broadcasted_iota(i32, own.shape, 1) == own.shape[1] - 1
    own = jnp.where(last, count_s[0, 0], own)
    note_ref[...] = jnp.concatenate([two_rows(x) for x in (fill_v[...], own, offset, block)], axis=0).astype(f32)


def lists_of(ref, rows):
    meta = ref[fields * rows : fields * rows + meta_rows, :].astype(i32)
    parts = [one_row(meta[2 * k : 2 * k + 2]) for k in range(4)]
    return (*parts, parts[1][:, halves * lanes - 1 :])


def rows_dot(x, y, contract):
    return lax.dot_general(x.astype(bf16), y.astype(bf16), (((1,), (contract,)), ((), ())), preferred_element_type=f32)


def split3(x):
    high = x.astype(bf16).astype(f32)
    rest = x - high
    mid = rest.astype(bf16).astype(f32)
    return high, mid, rest - mid


def stacked(rows, width):
    rows = [r.astype(f32) for r in rows]
    return jnp.concatenate(rows + [jnp.zeros((8 - len(rows), width), f32)], axis=0)


def wide(row):
    missing = halves * lanes - row.shape[1]
    return row if missing == 0 else jnp.concatenate([row, jnp.zeros((1, missing), row.dtype)], axis=1)


def one_row(x):
    return jnp.concatenate([x[0:1], x[1:2]], axis=1)


def two_rows(x):
    return jnp.concatenate([x[:, h * lanes : (h + 1) * lanes] for h in range(x.shape[1] // lanes)], axis=0)


def equal_rows(row, count, first=0):
    at = lax.broadcasted_iota(i32, (count, row.shape[1]), 0) + first
    return (row.astype(i32) == at).astype(f32).astype(bf16)


def running(flags):
    size = halves * lanes
    upper = lax.broadcasted_iota(i32, (size, size), 0) <= lax.broadcasted_iota(i32, (size, size), 1)
    return rows_dot(flags, upper.astype(f32), 0)


def pack_kernel(slots, rows, tile_ref, east_ref, west_ref, origin_ref):
    blocks = rows // halves
    size = halves * lanes
    slot_rows = halves * slots
    fill, own, offset, block, count = lists_of(tile_ref, rows)
    live = lax.broadcasted_iota(i32, (1, size), 1) < count
    dr = third(offset)
    dc = offset - 3 * dr
    marks = [live & (dc == want) for want in (2, 0)]
    counts = running(stacked(marks, size))
    picked = equal_rows(own, blocks)
    fill = rows_dot(stacked([fill], size), picked, 0)[0:1]
    values = stacked([block, fill, dr, own + 1], size)
    lane_id = lax.broadcasted_iota(i32, (1, lanes), 1)
    chosen = []
    for side, out_ref in enumerate((east_ref, west_ref)):
        count = counts[side : side + 1]
        place = jnp.where(marks[side], count - 1.0, -1.0)
        moved = equal_rows(place, slots)
        meta = rows_dot(values, moved, 1)
        meta = jnp.concatenate([meta, jnp.zeros((8, size - slots), f32)], axis=1)
        ends = jnp.where(lane_id == 0, count[:, size - 1 :], 0.0)
        out_ref[fields * slot_rows : fields * slot_rows + meta_rows, :] = jnp.concatenate(
            [two_rows(meta[k : k + 1]) for k in range(3)] + [ends, jnp.zeros((1, lanes), f32)], axis=0)
        origin_ref[side : side + 1, :] = meta[3:4] - 1.0
        chosen.append(rows_dot(moved, picked, 1).astype(bf16))
    for f in range(fields):
        data = jnp.concatenate([tile_ref[pl.ds(f * rows + h, blocks, stride=halves), :] for h in range(halves)], axis=1)
        parts = split3(data)
        for pick, out_ref in zip(chosen, (east_ref, west_ref)):
            got = rows_dot(pick, parts[0], 0) + rows_dot(pick, parts[1], 0) + rows_dot(pick, parts[2], 0)
            for h in range(halves):
                out_ref[pl.ds(f * slot_rows + h, slots, stride=halves), :] = got[:, h * lanes : (h + 1) * lanes]


def shape_of(kind):
    steps = (16, 24, 16, 24, 32)[kind]
    return steps, -(-steps // 16), (1, 1, 2, 2, 2)[kind]


def pair_loops(total, spare, table, src, grad, buffers):
    size = halves * lanes

    def word_at(k, at):
        place = table[11, k] + at
        return table[12 + (place >> 7), place & 127]

    def load(index, fill, parts):
        size = parts * lanes
        row_id = lax.broadcasted_iota(i32, (8, size), 0)
        lane_id = lax.broadcasted_iota(i32, (8, size), 1)
        pieces = []
        for h in range(parts):
            got = src[pl.ds(halves * index + h, fields, stride=total), :]
            pieces.append(jnp.concatenate([got, jnp.zeros((8 - fields, lanes), f32)], axis=0))
        x = jnp.concatenate(pieces, axis=1)
        return jnp.where((row_id < axes) | (lane_id < fill), x, 0.0)

    def spread(k, at, mixed, partner):
        steps, parts_a, parts_b = shape_of(k)
        word = word_at(k, at)
        ia, ib = word & 4095, word >> 12
        live = at < table[11, 8 + k]
        a = load(ia, jnp.where(live, table[ia >> 7, ia & 127], 0), parts_a)
        b = load(ib, jnp.where(live, table[ib >> 7, ib & 127], 0), parts_b)
        partner[:, : parts_b * lanes] = b
        zero = jnp.zeros((8, lanes), f32)
        row_b = lax.broadcasted_iota(i32, b.shape, 0)
        ah, am, al = split3(a)
        left = jnp.concatenate([ah, am, al, ah], axis=0).astype(bf16)
        swapped = jnp.where(row_b == 3, jnp.roll(b, -1, axis=0), jnp.where(row_b == 4, jnp.roll(b, 1, axis=0), 0.0))
        swapped = swapped * -20.0
        sh = swapped.astype(bf16).astype(f32)
        sm = swapped - sh
        right = jnp.concatenate([sh, sh, jnp.zeros_like(b), sm], axis=0).astype(bf16)
        row_id = lax.broadcasted_iota(i32, (8, lanes), 0)
        units = [(row_id == f).astype(f32) for f in range(axes)]
        pick = jnp.concatenate([jnp.concatenate([u, u, u, zero], axis=0) for u in units], axis=1).astype(bf16)
        mixed[: parts_a * lanes, : (axes + parts_b) * lanes] = lax.dot_general(
            left, jnp.concatenate([pick, right], axis=1), (((0,), (0,)), ((), ())), preferred_element_type=f32)

    def work(k, mixed, partner, own, far):
        steps, parts_a, parts_b = shape_of(k)
        b_rows = [
            [jnp.broadcast_to(partner[f : f + 1, p * lanes : (p + 1) * lanes], (8, lanes)) for f in range(axes)]
            for p in range(parts_b)
        ]
        sums = [[None] * axes for _ in range(parts_b)]
        for g in range(steps):
            rows = slice(8 * g, 8 * g + 8)
            a_cols = [mixed[rows, f * lanes : (f + 1) * lanes] for f in range(axes)]
            mine = [None] * axes
            for p in range(parts_b):
                diff = [a_cols[f] - b_rows[p][f] for f in range(axes)]
                square = diff[0] * diff[0] + diff[1] * diff[1] + diff[2] * diff[2]
                square = jnp.maximum(square, 1e-30)
                reach = jnp.maximum(1.0 - square * lax.rsqrt(square), 0.0)
                w = (reach * reach) * (reach * mixed[rows, (axes + p) * lanes : (axes + p + 1) * lanes])
                for f in range(axes):
                    push = w * diff[f]
                    mine[f] = push if p == 0 else mine[f] + push
                    sums[p][f] = push if g == 0 else sums[p][f] + push
            for f in range(axes):
                own[f * size + 8 * g : f * size + 8 * g + 8, :] = mine[f]
        for p in range(parts_b):
            for f in range(axes):
                far[8 * f : 8 * f + 8, p * lanes : (p + 1) * lanes] = sums[p][f]

    def finish(k, at, own, far):
        steps, parts_a, parts_b = shape_of(k)
        word = jnp.where(at < 0, spare | (spare << 12), word_at(k, jnp.maximum(at, 0)))
        ia, ib = word & 4095, word >> 12
        for h in range(parts_a):
            count = min(lanes, 8 * steps - h * lanes)
            rows = []
            for f in range(axes):
                part = own[f * size + h * lanes : f * size + h * lanes + count, :]
                if count < lanes:
                    part = jnp.concatenate([part, jnp.zeros((lanes - count, lanes), f32)], axis=0)
                rows.append(jnp.sum(part.T, axis=0, keepdims=True))
            place = pl.ds(halves * ia + h, axes, stride=total)
            grad[place, :] = grad[place, :] + jnp.concatenate(rows, axis=0)
        for p in range(parts_b):
            rows = [jnp.sum(far[8 * f : 8 * f + 8, p * lanes : (p + 1) * lanes], axis=0, keepdims=True) for f in range(axes)]
            place = pl.ds(halves * ib + p, axes, stride=total)
            grad[place, :] = grad[place, :] - jnp.concatenate(rows, axis=0)

    mixed0, mixed1, partner0, partner1, own0, own1, far0, far1 = buffers
    for k in range(kinds):
        turns = (table[11, 8 + k] + 1) // 2

        def turn(t, carry, k=k):
            at = 2 * t
            finish(k, at - 1, own1, far1)
            work(k, mixed0, partner0, own0, far0)
            spread(k, at + 1, mixed1, partner1)
            finish(k, at, own0, far0)
            work(k, mixed1, partner1, own1, far1)
            spread(k, at + 2, mixed0, partner0)
            return carry

        @pl.when(turns > 0)
        def _(k=k, turns=turns, turn=turn):
            spread(k, 0, mixed0, partner0)
            lax.fori_loop(0, turns, turn, 0)
            finish(k, 2 * turns - 1, own1, far1)


def sorted_pairs(entries):
    size = halves * lanes
    found = []
    for a, b, fill_a, fill_b, live in entries:
        size_a, size_b = (fill_a + 63) >> 6, (fill_b + 63) >> 6
        two_a, two_b = (size_a > 2).astype(i32), (size_b > 2).astype(i32)
        swap = (size_a * (1 + two_b) > size_b * (1 + two_a)) | ((size_a > 3) & (size_b < 3))
        a, b = jnp.where(swap, b, a), jnp.where(swap, a, b)
        size_a, size_b = jnp.where(swap, size_b, size_a), jnp.where(swap, size_a, size_b)
        kind = jnp.maximum(size_a - 2, 0) + jnp.where(size_b > 2, 2, 0)
        marks = [live & (kind == k) for k in range(kinds)]
        counts = running(stacked(marks, size))
        values = stacked([a & 255, a >> 8, b & 255, b >> 8], size)
        found.append((marks, counts, values))
    firsts, totals = [], []
    at = jnp.zeros((1, 1), f32)
    for k in range(kinds):
        firsts.append(at)
        total = sum(counts[k : k + 1, size - 1 :] for _, counts, _ in found)
        totals.append(total)
        at = at + total
    length = size * len(entries)
    ordered = jnp.zeros((8, length), f32)
    before = firsts
    for marks, counts, values in found:
        place = jnp.full((1, size), -1.0, f32)
        for k in range(kinds):
            place = jnp.where(marks[k], before[k] + counts[k : k + 1] - 1.0, place)
        before = [before[k] + counts[k : k + 1, size - 1 :] for k in range(kinds)]
        ordered = ordered + rows_dot(values, equal_rows(place, length), 1)
    ordered = ordered.astype(i32)
    words = ordered[0:1] + (ordered[1:2] << 8) + (ordered[2:3] << 12) + (ordered[3:4] << 20)
    lane_id = lax.broadcasted_iota(i32, (1, lanes), 1)
    bounds = jnp.zeros((1, lanes), i32)
    firsts, totals = [f.astype(i32) for f in firsts], [t.astype(i32) for t in totals]
    for k in (0, 2, 3):
        odd = totals[k] & 1
        totals[k], firsts[k + 1], totals[k + 1] = totals[k] - odd, firsts[k + 1] - odd, totals[k + 1] + odd
    for k in range(kinds):
        bounds = jnp.where(lane_id == k, firsts[k], bounds)
        bounds = jnp.where(lane_id == 8 + k, totals[k], bounds)
    return words, bounds


def as_table(pieces, table_v, table, sem):
    at = 0
    for piece in pieces:
        table_v[at : at + piece.shape[0], :] = piece
        at += piece.shape[0]
    copy = pltpu.make_async_copy(table_v, table, sem)
    copy.start()
    return copy


def fills_of(fills, block):
    return rows_dot(stacked(fills, block.shape[1]), equal_rows(block, halves * lanes), 0).astype(i32)


def column_shares(lists, row, last_row):
    fill, own, offset, block, count = lists
    size = halves * lanes
    live = lax.broadcasted_iota(i32, (1, size), 1) < count
    dr = third(offset)
    column = live & (offset - 3 * dr == 1)
    marks = [column & (dr == k) for k in range(3)]
    rank = running(stacked(marks, size)).astype(i32)
    odd = [(rank[k : k + 1] & 1) == 1 for k in range(3)]
    spare = marks[1] & (rank[1:2] > kept)
    has_north, has_south = row > 0, row < last_row
    to_north = spare & has_north & odd[1]
    to_south = spare & has_south & jnp.logical_not(odd[1])
    inside = marks[1] & jnp.logical_not(to_north | to_south)
    return (
        (marks[0] & odd[0], inside, marks[2] & odd[2]),
        ((marks[0] & jnp.logical_not(odd[0])), to_north),
        ((marks[2] & jnp.logical_not(odd[2])), to_south),
    )


def column_entries(lists, base_row, fills):
    fill, own, offset, block, count = lists
    size = halves * lanes
    a = base_row * size + own
    target = base_row + third(offset) - 1
    b = target * size + block
    near = fills_of(fills, block)
    fill_b = jnp.where(target == 0, near[0:1], jnp.where(target == 1, near[1:2], near[2:3]))
    return a, b, fills_of([fill], own)[0:1], fill_b


def level_kernel(rows, total, last_row, tile_ref, g_tile, src, grad, table_v, table, sem, *buffers):
    blocks = rows // halves
    lists = lists_of(tile_ref, rows)
    mine, _, _ = column_shares(lists, lax.axis_index("ty"), last_row)
    fills = [jnp.zeros_like(lists[0]), lists[0], jnp.zeros_like(lists[0])]
    words, bounds = sorted_pairs([(*column_entries(lists, 1, fills), mine[1])])
    copy = as_table((*map(two_rows, fills), jnp.zeros((5, lanes), i32), bounds, two_rows(words)), table_v, table, sem)
    for f in range(fields):
        src[f * total + rows : f * total + 2 * rows, :] = tile_ref[f * rows : (f + 1) * rows, :]
    for f in range(axes):
        grad[f * total + rows : f * total + 2 * rows, :] = jnp.zeros((rows, lanes), f32)
    copy.wait()
    pair_loops(total, 3 * blocks, table, src, grad, buffers)
    for f in range(axes):
        g_tile[f * rows : (f + 1) * rows, :] = grad[f * total + rows : f * total + 2 * rows, :]


def column_kernel(rows, total, last_row, tile_ref, north_ref, south_ref, start_ref, g_tile, g_north, g_south,
                  src, grad, table_v, table, sem, *buffers):
    blocks = rows // halves
    row = lax.axis_index("ty")
    lists = [lists_of(ref, rows) for ref in (north_ref, tile_ref, south_ref)]
    fills = [l[0] for l in lists]
    shares = [column_shares(l, row + k - 1, last_row) for k, l in enumerate(lists)]
    wanted = (
        shares[0][2][0] | shares[0][2][1],
        shares[1][0][0] | shares[1][0][2],
        shares[2][1][0] | shares[2][1][1],
    )
    words, bounds = sorted_pairs([(*column_entries(l, k, fills), wanted[k]) for k, l in enumerate(lists)])
    copy = as_table((*map(two_rows, fills), jnp.zeros((5, lanes), i32), bounds, two_rows(words)), table_v, table, sem)
    for ref, base in ((north_ref, 0), (tile_ref, rows), (south_ref, 2 * rows)):
        for f in range(fields):
            src[f * total + base : f * total + base + rows, :] = ref[f * rows : (f + 1) * rows, :]
    for f in range(axes):
        grad[f * total : f * total + rows, :] = jnp.zeros((rows, lanes), f32)
        grad[f * total + rows : f * total + 2 * rows, :] = start_ref[f * rows : (f + 1) * rows, :]
        grad[f * total + 2 * rows : f * total + 3 * rows, :] = jnp.zeros((rows, lanes), f32)
    copy.wait()
    pair_loops(total, 3 * blocks, table, src, grad, buffers)
    for ref, base in ((g_north, 0), (g_tile, rows), (g_south, 2 * rows)):
        for f in range(axes):
            ref[f * rows : (f + 1) * rows, :] = grad[f * total + base : f * total + base + rows, :]


def side_kernel(slots, rows, total, tiles, east_ref, west_ref, g_tiles, o_tiles, o_east, o_west,
                src, grad, table_v, table, sem, *buffers):
    blocks = rows // halves
    slot_rows = halves * slots
    size = halves * lanes
    bases = (0, rows, 2 * rows)
    fills = [lists_of(t, rows)[0] for t in tiles]
    east_base, west_base = 6 * lanes, 8 * lanes
    slot_id = lax.broadcasted_iota(i32, (1, size), 1)
    entries, slot_fills = [], []
    for ref, base in ((east_ref, east_base), (west_ref, west_base)):
        meta = ref[fields * slot_rows : fields * slot_rows + meta_rows, :].astype(i32)
        live = slot_id < meta[6:7, 0:1]
        block, fill, dr = (jnp.where(live, one_row(meta[2 * k : 2 * k + 2]), 0) for k in range(3))
        near = fills_of(fills, block)
        fill_b = jnp.where(dr == 0, near[0:1], jnp.where(dr == 1, near[1:2], near[2:3]))
        entries.append((base + slot_id, dr * blocks + block, fill, fill_b, live))
        slot_fills.append(fill)
    words, bounds = sorted_pairs(entries)
    copy = as_table((*map(two_rows, fills), *map(two_rows, slot_fills), jnp.zeros((1, lanes), i32), bounds, two_rows(words)),
                    table_v, table, sem)
    slot_places = ((east_ref, halves * east_base), (west_ref, halves * west_base))
    for ref, base in zip(tiles, bases):
        for f in range(fields):
            src[f * total + base : f * total + base + rows, :] = ref[f * rows : (f + 1) * rows, :]
    for ref, base in slot_places:
        for f in range(fields):
            src[f * total + base : f * total + base + slot_rows, :] = ref[f * slot_rows : (f + 1) * slot_rows, :]
    for ref, base in zip(g_tiles, bases):
        for f in range(axes):
            grad[f * total + base : f * total + base + rows, :] = ref[f * rows : (f + 1) * rows, :]
    for _, base in slot_places:
        for f in range(axes):
            grad[f * total + base : f * total + base + slot_rows, :] = jnp.zeros((slot_rows, lanes), f32)
    copy.wait()
    pair_loops(total, 10 * lanes, table, src, grad, buffers)
    for ref, base in zip(o_tiles, bases):
        for f in range(axes):
            ref[f * rows : (f + 1) * rows, :] = grad[f * total + base : f * total + base + rows, :]
    for ref, (_, base) in zip((o_east, o_west), slot_places):
        for f in range(axes):
            ref[f * slot_rows : (f + 1) * slot_rows, :] = grad[f * total + base : f * total + base + slot_rows, :]


def merge_kernel(slots, rows, origin_ref, g_tile, g_north, g_south, g_east, g_west, out_ref):
    blocks = rows // halves
    slot_rows = halves * slots
    placed = [equal_rows(origin_ref[side : side + 1, :][:, :slots], blocks) for side in range(2)]
    out_ref[...] = g_tile[...] + g_north[...] + g_south[...]
    for f in range(axes):
        got = jnp.zeros((blocks, halves * lanes), f32)
        for place, ref in zip(placed, (g_east, g_west)):
            data = jnp.concatenate([ref[pl.ds(f * slot_rows + h, slots, stride=halves), :] for h in range(halves)], axis=1)
            for part in split3(data):
                got = got + rows_dot(place, part, 0)
        for h in range(halves):
            at = pl.ds(f * rows + h, blocks, stride=halves)
            out_ref[at, :] = out_ref[at, :] + got[:, h * lanes : (h + 1) * lanes]


def shifted(x, axis, by):
    devices = lax.axis_size(axis)
    pairs = [(i, i + by) for i in range(devices) if 0 <= i + by < devices]
    return lax.ppermute(x, axis, pairs)


vmem = pl.BlockSpec(memory_space=pltpu.VMEM)
smem = pl.BlockSpec(memory_space=pltpu.SMEM)
in_hbm = pl.BlockSpec(memory_space=pltpu.HBM)


def sds(n):
    return jax.ShapeDtypeStruct((n, lanes), f32)


def params(mib):
    return pltpu.CompilerParams(vmem_limit_bytes=mib << 20)


def pair_scratch(total, sets):
    return [
        pltpu.VMEM((fields * total, lanes), f32),
        pltpu.VMEM((axes * total, lanes), f32),
        pltpu.VMEM((12 + halves * sets, lanes), i32),
        pltpu.SMEM((12 + halves * sets, lanes), i32),
        pltpu.SemaphoreType.DMA,
        pltpu.VMEM((halves * lanes, fields * lanes), f32),
        pltpu.VMEM((halves * lanes, fields * lanes), f32),
        pltpu.VMEM((8, halves * lanes), f32),
        pltpu.VMEM((8, halves * lanes), f32),
        pltpu.VMEM((axes * halves * lanes, lanes), f32),
        pltpu.VMEM((axes * halves * lanes, lanes), f32),
        pltpu.VMEM((axes * 8, halves * lanes), f32),
        pltpu.VMEM((axes * 8, halves * lanes), f32),
    ]


def level_call(rows, last_row, tile):
    total = 3 * rows + 8
    return pl.pallas_call(
        lambda *refs: level_kernel(rows, total, last_row, *refs),
        out_shape=sds(axes * rows),
        in_specs=[vmem],
        out_specs=vmem,
        scratch_shapes=pair_scratch(total, 1),
        compiler_params=params(24),
        name="pairs_inside",
    )(tile)


def column_call(rows, last_row, tile, north, south, g_tile):
    total = 3 * rows + 8
    return pl.pallas_call(
        lambda *refs: column_kernel(rows, total, last_row, *refs),
        out_shape=(sds(axes * rows),) * 3,
        in_specs=[vmem] * 4,
        out_specs=(vmem,) * 3,
        scratch_shapes=pair_scratch(total, 3),
        compiler_params=params(24),
        name="pairs_column",
    )(tile, north, south, g_tile)


def side_call(slots, rows, tiles, east, west, g_tiles):
    total = 3 * rows + 4 * halves * lanes + 8

    def run(*refs):
        side_kernel(slots, rows, total, refs[:3], *refs[3:5], refs[5:8], refs[8:11], *refs[11:])

    return pl.pallas_call(
        run,
        out_shape=(sds(axes * rows),) * 3 + (sds(axes * halves * slots),) * 2,
        in_specs=[vmem] * 8,
        out_specs=(vmem,) * 5,
        scratch_shapes=pair_scratch(total, 2),
        compiler_params=params(32),
        name="pairs_side",
    )(*tiles, east, west, *g_tiles)


def body(locations, solution, cotangent, block_fill, pair_own, pair_offset, pair_block, pair_count):
    points = solution.shape[2]
    slots = pair_own.shape[2]
    rows = points // lanes
    blocks = rows // halves
    own = pair_own.reshape(1, slots)
    offset = pair_offset.reshape(1, slots)
    block = pair_block.reshape(1, slots)
    count = pair_count.reshape(1, 1)
    fill = block_fill.reshape(1, blocks)
    slot_rows = fields * halves * slots + meta_rows
    last_row = lax.axis_size("ty") - 1
    note = pl.pallas_call(
        note_kernel,
        out_shape=sds(meta_rows),
        in_specs=[in_hbm] * 5,
        out_specs=vmem,
        scratch_shapes=[pltpu.SMEM((1, 1), i32), pltpu.VMEM((1, blocks), i32), pltpu.VMEM((3, 1, slots), i32),
                        pltpu.SemaphoreType.DMA((5,))],
        compiler_params=params(60),
        name="note",
    )(count, fill, own, offset, block)
    tile = jnp.concatenate([locations.reshape(axes * rows, lanes), solution.reshape(rows, lanes),
                            cotangent.reshape(rows, lanes), note], axis=0)
    north = shifted(tile, "ty", 1)
    south = shifted(tile, "ty", -1)
    to_east, to_west, origin = pl.pallas_call(
        lambda *refs: pack_kernel(slots, rows, *refs),
        out_shape=(sds(slot_rows), sds(slot_rows), jax.ShapeDtypeStruct((8, halves * lanes), f32)),
        in_specs=[vmem],
        out_specs=(vmem,) * 3,
        compiler_params=params(16),
        name="pack",
    )(tile)
    from_west = shifted(to_east, "tx", 1)
    from_east = shifted(to_west, "tx", -1)
    g_tile = level_call(rows, last_row, tile)
    g_tile, g_north, g_south = column_call(rows, last_row, tile, north, south, g_tile)
    g_north, g_tile, g_south, g_west, g_east = side_call(
        slots, rows, (north, tile, south), from_west, from_east, (g_north, g_tile, g_south))
    back_east = shifted(g_west, "tx", -1)
    back_west = shifted(g_east, "tx", 1)
    back_south = shifted(g_north, "ty", -1)
    back_north = shifted(g_south, "ty", 1)
    out = pl.pallas_call(
        lambda *refs: merge_kernel(slots, rows, *refs),
        out_shape=sds(axes * rows),
        in_specs=[vmem] * 6,
        out_specs=vmem,
        compiler_params=params(16),
        name="merge",
    )(origin, g_tile, back_north, back_south, back_east, back_west)
    return out.reshape(locations.shape)


def solution(mesh):
    placed = (
        P("ty", "tx", None, None),
        P("ty", "tx", None),
        P("ty", "tx", None),
        P("ty", "tx", None),
        P("ty", "tx", None),
        P("ty", "tx", None),
        P("ty", "tx", None),
        P("ty", "tx"),
    )
    return jax.shard_map(
        body, mesh=mesh, in_specs=placed, out_specs=P("ty", "tx", None, None), check_vma=False
    )
```

```python
import jax
import jax.numpy as jnp
from jax import lax
from jax.experimental import pallas as pl
from jax.experimental.pallas import tpu as pltpu
from jax.sharding import PartitionSpec as P

lanes = 128
halves = 2
fields = 5
axes = 3
meta_rows = 8
kinds = 4
kept = 16
bf16 = jnp.bfloat16
f32 = jnp.float32
i32 = jnp.int32


def third(heading):
    return (heading * 11) >> 5


def note_kernel(count_ref, fill_ref, own_ref, offset_ref, block_ref, note_ref, count_s, fill_v, lists_v, sem):
    copies = (
        pltpu.make_async_copy(fill_ref, fill_v, sem.at[0]),
        pltpu.make_async_copy(own_ref, lists_v.at[0], sem.at[1]),
        pltpu.make_async_copy(offset_ref, lists_v.at[1], sem.at[2]),
        pltpu.make_async_copy(block_ref, lists_v.at[2], sem.at[3]),
        pltpu.make_async_copy(count_ref, count_s, sem.at[4]),
    )
    for c in copies:
        c.start()
    for c in copies:
        c.wait()
    own, offset, block = (wide(lists_v[k]) for k in range(3))
    last = lax.broadcasted_iota(i32, own.shape, 1) == own.shape[1] - 1
    own = jnp.where(last, count_s[0, 0], own)
    note_ref[...] = jnp.concatenate([two_rows(x) for x in (fill_v[...], own, offset, block)], axis=0).astype(f32)


def lists_of(ref, rows):
    meta = ref[fields * rows : fields * rows + meta_rows, :].astype(i32)
    parts = [one_row(meta[2 * k : 2 * k + 2]) for k in range(4)]
    return (*parts, parts[1][:, halves * lanes - 1 :])


def rows_dot(x, y, contract):
    return lax.dot_general(x.astype(bf16), y.astype(bf16), (((1,), (contract,)), ((), ())), preferred_element_type=f32)


def split3(x):
    high = x.astype(bf16).astype(f32)
    rest = x - high
    mid = rest.astype(bf16).astype(f32)
    return high, mid, rest - mid


def stacked(rows, width):
    rows = [r.astype(f32) for r in rows]
    return jnp.concatenate(rows + [jnp.zeros((8 - len(rows), width), f32)], axis=0)


def wide(row):
    missing = halves * lanes - row.shape[1]
    return row if missing == 0 else jnp.concatenate([row, jnp.zeros((1, missing), row.dtype)], axis=1)


def one_row(x):
    return jnp.concatenate([x[0:1], x[1:2]], axis=1)


def two_rows(x):
    return jnp.concatenate([x[:, h * lanes : (h + 1) * lanes] for h in range(x.shape[1] // lanes)], axis=0)


def equal_rows(row, count, first=0):
    at = lax.broadcasted_iota(i32, (count, row.shape[1]), 0) + first
    return (row.astype(i32) == at).astype(f32).astype(bf16)


def running(flags):
    size = halves * lanes
    upper = lax.broadcasted_iota(i32, (size, size), 0) <= lax.broadcasted_iota(i32, (size, size), 1)
    return rows_dot(flags, upper.astype(f32), 0)


def pack_kernel(slots, rows, tile_ref, east_ref, west_ref, origin_ref):
    blocks = rows // halves
    size = halves * lanes
    slot_rows = halves * slots
    fill, own, offset, block, count = lists_of(tile_ref, rows)
    live = lax.broadcasted_iota(i32, (1, size), 1) < count
    dr = third(offset)
    dc = offset - 3 * dr
    marks = [live & (dc == want) for want in (2, 0)]
    counts = running(stacked(marks, size))
    picked = equal_rows(own, blocks)
    fill = rows_dot(stacked([fill], size), picked, 0)[0:1]
    values = stacked([block, fill, dr, own + 1], size)
    lane_id = lax.broadcasted_iota(i32, (1, lanes), 1)
    chosen = []
    for side, out_ref in enumerate((east_ref, west_ref)):
        count = counts[side : side + 1]
        place = jnp.where(marks[side], count - 1.0, -1.0)
        moved = equal_rows(place, slots)
        meta = rows_dot(values, moved, 1)
        meta = jnp.concatenate([meta, jnp.zeros((8, size - slots), f32)], axis=1)
        ends = jnp.where(lane_id == 0, count[:, size - 1 :], 0.0)
        out_ref[fields * slot_rows : fields * slot_rows + meta_rows, :] = jnp.concatenate(
            [two_rows(meta[k : k + 1]) for k in range(3)] + [ends, jnp.zeros((1, lanes), f32)], axis=0)
        origin_ref[side : side + 1, :] = meta[3:4] - 1.0
        chosen.append(rows_dot(moved, picked, 1).astype(bf16))
    for f in range(fields):
        data = jnp.concatenate([tile_ref[pl.ds(f * rows + h, blocks, stride=halves), :] for h in range(halves)], axis=1)
        parts = split3(data)
        for pick, out_ref in zip(chosen, (east_ref, west_ref)):
            got = rows_dot(pick, parts[0], 0) + rows_dot(pick, parts[1], 0) + rows_dot(pick, parts[2], 0)
            for h in range(halves):
                out_ref[pl.ds(f * slot_rows + h, slots, stride=halves), :] = got[:, h * lanes : (h + 1) * lanes]


def shape_of(kind):
    steps = (16, 16, 24, 32)[kind]
    return steps, -(-steps // 16), (1, 2, 2, 2)[kind]


def pair_loops(total, spare, table, src, grad, buffers):
    size = halves * lanes

    def word_at(k, at):
        place = table[11, k] + at
        return table[12 + (place >> 7), place & 127]

    def load(index, fill, parts):
        size = parts * lanes
        row_id = lax.broadcasted_iota(i32, (8, size), 0)
        lane_id = lax.broadcasted_iota(i32, (8, size), 1)
        pieces = []
        for h in range(parts):
            got = src[pl.ds(halves * index + h, fields, stride=total), :]
            pieces.append(jnp.concatenate([got, jnp.zeros((8 - fields, lanes), f32)], axis=0))
        x = jnp.concatenate(pieces, axis=1)
        return jnp.where((row_id < axes) | (lane_id < fill), x, 0.0)

    def spread(k, at, mixed, partner):
        steps, parts_a, parts_b = shape_of(k)
        word = word_at(k, at)
        ia, ib = word & 4095, word >> 12
        live = at < table[11, 8 + k]
        a = load(ia, jnp.where(live, table[ia >> 7, ia & 127], 0), parts_a)
        b = load(ib, jnp.where(live, table[ib >> 7, ib & 127], 0), parts_b)
        partner[:, : parts_b * lanes] = b
        zero = jnp.zeros((8, lanes), f32)
        row_b = lax.broadcasted_iota(i32, b.shape, 0)
        ah, am, al = split3(a)
        left = jnp.concatenate([ah, am, al, ah], axis=0).astype(bf16)
        swapped = jnp.where(row_b == 3, jnp.roll(b, -1, axis=0), jnp.where(row_b == 4, jnp.roll(b, 1, axis=0), 0.0))
        swapped = swapped * -20.0
        sh = swapped.astype(bf16).astype(f32)
        sm = swapped - sh
        right = jnp.concatenate([sh, sh, jnp.zeros_like(b), sm], axis=0).astype(bf16)
        row_id = lax.broadcasted_iota(i32, (8, lanes), 0)
        units = [(row_id == f).astype(f32) for f in range(axes)]
        pick = jnp.concatenate([jnp.concatenate([u, u, u, zero], axis=0) for u in units], axis=1).astype(bf16)
        mixed[: parts_a * lanes, : (axes + parts_b) * lanes] = lax.dot_general(
            left, jnp.concatenate([pick, right], axis=1), (((0,), (0,)), ((), ())), preferred_element_type=f32)

    def work(k, mixed, partner, own, far):
        steps, parts_a, parts_b = shape_of(k)
        b_rows = [
            [jnp.broadcast_to(partner[f : f + 1, p * lanes : (p + 1) * lanes], (8, lanes)) for f in range(axes)]
            for p in range(parts_b)
        ]
        sums = [[None] * axes for _ in range(parts_b)]
        for g in range(steps):
            rows = slice(8 * g, 8 * g + 8)
            a_cols = [mixed[rows, f * lanes : (f + 1) * lanes] for f in range(axes)]
            mine = [None] * axes
            for p in range(parts_b):
                diff = [a_cols[f] - b_rows[p][f] for f in range(axes)]
                square = diff[0] * diff[0] + diff[1] * diff[1] + diff[2] * diff[2]
                square = jnp.maximum(square, 1e-30)
                reach = jnp.maximum(1.0 - square * lax.rsqrt(square), 0.0)
                w = (reach * reach) * (reach * mixed[rows, (axes + p) * lanes : (axes + p + 1) * lanes])
                for f in range(axes):
                    push = w * diff[f]
                    mine[f] = push if p == 0 else mine[f] + push
                    sums[p][f] = push if g == 0 else sums[p][f] + push
            for f in range(axes):
                own[f * size + 8 * g : f * size + 8 * g + 8, :] = mine[f]
        for p in range(parts_b):
            for f in range(axes):
                far[8 * f : 8 * f + 8, p * lanes : (p + 1) * lanes] = sums[p][f]

    def finish(k, at, own, far):
        steps, parts_a, parts_b = shape_of(k)
        word = jnp.where(at < 0, spare | (spare << 12), word_at(k, jnp.maximum(at, 0)))
        ia, ib = word & 4095, word >> 12
        for h in range(parts_a):
            count = min(lanes, 8 * steps - h * lanes)
            rows = []
            for f in range(axes):
                part = own[f * size + h * lanes : f * size + h * lanes + count, :]
                if count < lanes:
                    part = jnp.concatenate([part, jnp.zeros((lanes - count, lanes), f32)], axis=0)
                rows.append(jnp.sum(part.T, axis=0, keepdims=True))
            place = pl.ds(halves * ia + h, axes, stride=total)
            grad[place, :] = grad[place, :] + jnp.concatenate(rows, axis=0)
        for p in range(parts_b):
            rows = [jnp.sum(far[8 * f : 8 * f + 8, p * lanes : (p + 1) * lanes], axis=0, keepdims=True) for f in range(axes)]
            place = pl.ds(halves * ib + p, axes, stride=total)
            grad[place, :] = grad[place, :] - jnp.concatenate(rows, axis=0)

    mixed0, mixed1, partner0, partner1, own0, own1, far0, far1 = buffers
    for k in range(kinds):
        turns = (table[11, 8 + k] + 1) // 2

        def turn(t, carry, k=k):
            at = 2 * t
            finish(k, at - 1, own1, far1)
            work(k, mixed0, partner0, own0, far0)
            spread(k, at + 1, mixed1, partner1)
            finish(k, at, own0, far0)
            work(k, mixed1, partner1, own1, far1)
            spread(k, at + 2, mixed0, partner0)
            return carry

        @pl.when(turns > 0)
        def _(k=k, turns=turns, turn=turn):
            spread(k, 0, mixed0, partner0)
            lax.fori_loop(0, turns >> 1, lambda t, c: turn(2 * t + 1, turn(2 * t, c)), 0)
            lax.fori_loop(turns & ~1, turns, turn, 0)
            finish(k, 2 * turns - 1, own1, far1)


def sorted_pairs(entries):
    size = halves * lanes
    found = []
    for a, b, fill_a, fill_b, live in entries:
        size_a, size_b = (fill_a + 63) >> 6, (fill_b + 63) >> 6
        swap = size_a > size_b
        a, b = jnp.where(swap, b, a), jnp.where(swap, a, b)
        size_a, size_b = jnp.where(swap, size_b, size_a), jnp.where(swap, size_a, size_b)
        kind = jnp.maximum(size_a - 2, 0) + jnp.where(size_b > 2, 1, 0)
        marks = [live & (kind == k) for k in range(kinds)]
        counts = running(stacked(marks, size))
        values = stacked([a & 255, a >> 8, b & 255, b >> 8], size)
        found.append((marks, counts, values))
    firsts, totals = [], []
    at = jnp.zeros((1, 1), f32)
    for k in range(kinds):
        firsts.append(at)
        total = sum(counts[k : k + 1, size - 1 :] for _, counts, _ in found)
        totals.append(total)
        at = at + total
    length = size * len(entries)
    ordered = jnp.zeros((8, length), f32)
    before = firsts
    for marks, counts, values in found:
        place = jnp.full((1, size), -1.0, f32)
        for k in range(kinds):
            place = jnp.where(marks[k], before[k] + counts[k : k + 1] - 1.0, place)
        before = [before[k] + counts[k : k + 1, size - 1 :] for k in range(kinds)]
        ordered = ordered + rows_dot(values, equal_rows(place, length), 1)
    ordered = ordered.astype(i32)
    words = ordered[0:1] + (ordered[1:2] << 8) + (ordered[2:3] << 12) + (ordered[3:4] << 20)
    lane_id = lax.broadcasted_iota(i32, (1, lanes), 1)
    bounds = jnp.zeros((1, lanes), i32)
    firsts, totals = [f.astype(i32) for f in firsts], [t.astype(i32) for t in totals]
    for k in range(kinds - 1):
        odd = totals[k] & 1
        totals[k], firsts[k + 1], totals[k + 1] = totals[k] - odd, firsts[k + 1] - odd, totals[k + 1] + odd
    for k in range(kinds):
        bounds = jnp.where(lane_id == k, firsts[k], bounds)
        bounds = jnp.where(lane_id == 8 + k, totals[k], bounds)
    return words, bounds


def as_table(pieces, table_v, table, sem):
    at = 0
    for piece in pieces:
        table_v[at : at + piece.shape[0], :] = piece
        at += piece.shape[0]
    copy = pltpu.make_async_copy(table_v, table, sem)
    copy.start()
    return copy


def fills_of(fills, block):
    return rows_dot(stacked(fills, block.shape[1]), equal_rows(block, halves * lanes), 0).astype(i32)


def column_shares(lists, row, last_row):
    fill, own, offset, block, count = lists
    size = halves * lanes
    live = lax.broadcasted_iota(i32, (1, size), 1) < count
    dr = third(offset)
    column = live & (offset - 3 * dr == 1)
    marks = [column & (dr == k) for k in range(3)]
    rank = running(stacked(marks, size)).astype(i32)
    odd = [(rank[k : k + 1] & 1) == 1 for k in range(3)]
    spare = marks[1] & (rank[1:2] > kept)
    has_north, has_south = row > 0, row < last_row
    to_north = spare & has_north & odd[1]
    to_south = spare & has_south & jnp.logical_not(odd[1])
    inside = marks[1] & jnp.logical_not(to_north | to_south)
    return (
        (marks[0] & odd[0], inside, marks[2] & odd[2]),
        ((marks[0] & jnp.logical_not(odd[0])), to_north),
        ((marks[2] & jnp.logical_not(odd[2])), to_south),
    )


def column_entries(lists, base_row, fills):
    fill, own, offset, block, count = lists
    size = halves * lanes
    a = base_row * size + own
    target = base_row + third(offset) - 1
    b = target * size + block
    near = fills_of(fills, block)
    fill_b = jnp.where(target == 0, near[0:1], jnp.where(target == 1, near[1:2], near[2:3]))
    return a, b, fills_of([fill], own)[0:1], fill_b


def level_kernel(rows, total, last_row, tile_ref, g_tile, src, grad, table_v, table, sem, *buffers):
    blocks = rows // halves
    lists = lists_of(tile_ref, rows)
    mine, _, _ = column_shares(lists, lax.axis_index("ty"), last_row)
    fills = [jnp.zeros_like(lists[0]), lists[0], jnp.zeros_like(lists[0])]
    words, bounds = sorted_pairs([(*column_entries(lists, 1, fills), mine[1])])
    copy = as_table((*map(two_rows, fills), jnp.zeros((5, lanes), i32), bounds, two_rows(words)), table_v, table, sem)
    for f in range(fields):
        src[f * total + rows : f * total + 2 * rows, :] = tile_ref[f * rows : (f + 1) * rows, :]
    for f in range(axes):
        grad[f * total + rows : f * total + 2 * rows, :] = jnp.zeros((rows, lanes), f32)
    copy.wait()
    pair_loops(total, 3 * blocks, table, src, grad, buffers)
    for f in range(axes):
        g_tile[f * rows : (f + 1) * rows, :] = grad[f * total + rows : f * total + 2 * rows, :]


def column_kernel(rows, total, last_row, tile_ref, north_ref, south_ref, start_ref, g_tile, g_north, g_south,
                  src, grad, table_v, table, sem, *buffers):
    blocks = rows // halves
    row = lax.axis_index("ty")
    lists = [lists_of(ref, rows) for ref in (north_ref, tile_ref, south_ref)]
    fills = [l[0] for l in lists]
    shares = [column_shares(l, row + k - 1, last_row) for k, l in enumerate(lists)]
    wanted = (
        shares[0][2][0] | shares[0][2][1],
        shares[1][0][0] | shares[1][0][2],
        shares[2][1][0] | shares[2][1][1],
    )
    words, bounds = sorted_pairs([(*column_entries(l, k, fills), wanted[k]) for k, l in enumerate(lists)])
    copy = as_table((*map(two_rows, fills), jnp.zeros((5, lanes), i32), bounds, two_rows(words)), table_v, table, sem)
    for ref, base in ((north_ref, 0), (tile_ref, rows), (south_ref, 2 * rows)):
        for f in range(fields):
            src[f * total + base : f * total + base + rows, :] = ref[f * rows : (f + 1) * rows, :]
    for f in range(axes):
        grad[f * total : f * total + rows, :] = jnp.zeros((rows, lanes), f32)
        grad[f * total + rows : f * total + 2 * rows, :] = start_ref[f * rows : (f + 1) * rows, :]
        grad[f * total + 2 * rows : f * total + 3 * rows, :] = jnp.zeros((rows, lanes), f32)
    copy.wait()
    pair_loops(total, 3 * blocks, table, src, grad, buffers)
    for ref, base in ((g_north, 0), (g_tile, rows), (g_south, 2 * rows)):
        for f in range(axes):
            ref[f * rows : (f + 1) * rows, :] = grad[f * total + base : f * total + base + rows, :]


def side_kernel(slots, rows, total, tiles, east_ref, west_ref, g_tiles, o_tiles, o_east, o_west,
                src, grad, table_v, table, sem, *buffers):
    blocks = rows // halves
    slot_rows = halves * slots
    size = halves * lanes
    bases = (0, rows, 2 * rows)
    fills = [lists_of(t, rows)[0] for t in tiles]
    east_base, west_base = 6 * lanes, 8 * lanes
    slot_id = lax.broadcasted_iota(i32, (1, size), 1)
    entries, slot_fills = [], []
    for ref, base in ((east_ref, east_base), (west_ref, west_base)):
        meta = ref[fields * slot_rows : fields * slot_rows + meta_rows, :].astype(i32)
        live = slot_id < meta[6:7, 0:1]
        block, fill, dr = (jnp.where(live, one_row(meta[2 * k : 2 * k + 2]), 0) for k in range(3))
        near = fills_of(fills, block)
        fill_b = jnp.where(dr == 0, near[0:1], jnp.where(dr == 1, near[1:2], near[2:3]))
        entries.append((base + slot_id, dr * blocks + block, fill, fill_b, live))
        slot_fills.append(fill)
    words, bounds = sorted_pairs(entries)
    copy = as_table((*map(two_rows, fills), *map(two_rows, slot_fills), jnp.zeros((1, lanes), i32), bounds, two_rows(words)),
                    table_v, table, sem)
    slot_places = ((east_ref, halves * east_base), (west_ref, halves * west_base))
    for ref, base in zip(tiles, bases):
        for f in range(fields):
            src[f * total + base : f * total + base + rows, :] = ref[f * rows : (f + 1) * rows, :]
    for ref, base in slot_places:
        for f in range(fields):
            src[f * total + base : f * total + base + slot_rows, :] = ref[f * slot_rows : (f + 1) * slot_rows, :]
    for ref, base in zip(g_tiles, bases):
        for f in range(axes):
            grad[f * total + base : f * total + base + rows, :] = ref[f * rows : (f + 1) * rows, :]
    for _, base in slot_places:
        for f in range(axes):
            grad[f * total + base : f * total + base + slot_rows, :] = jnp.zeros((slot_rows, lanes), f32)
    copy.wait()
    pair_loops(total, 10 * lanes, table, src, grad, buffers)
    for ref, base in zip(o_tiles, bases):
        for f in range(axes):
            ref[f * rows : (f + 1) * rows, :] = grad[f * total + base : f * total + base + rows, :]
    for ref, (_, base) in zip((o_east, o_west), slot_places):
        for f in range(axes):
            ref[f * slot_rows : (f + 1) * slot_rows, :] = grad[f * total + base : f * total + base + slot_rows, :]


def merge_kernel(slots, rows, origin_ref, g_tile, g_north, g_south, g_east, g_west, out_ref):
    blocks = rows // halves
    slot_rows = halves * slots
    placed = [equal_rows(origin_ref[side : side + 1, :][:, :slots], blocks) for side in range(2)]
    out_ref[...] = g_tile[...] + g_north[...] + g_south[...]
    for f in range(axes):
        got = jnp.zeros((blocks, halves * lanes), f32)
        for place, ref in zip(placed, (g_east, g_west)):
            data = jnp.concatenate([ref[pl.ds(f * slot_rows + h, slots, stride=halves), :] for h in range(halves)], axis=1)
            for part in split3(data):
                got = got + rows_dot(place, part, 0)
        for h in range(halves):
            at = pl.ds(f * rows + h, blocks, stride=halves)
            out_ref[at, :] = out_ref[at, :] + got[:, h * lanes : (h + 1) * lanes]


def shifted(x, axis, by):
    devices = lax.axis_size(axis)
    pairs = [(i, i + by) for i in range(devices) if 0 <= i + by < devices]
    return lax.ppermute(x, axis, pairs)


vmem = pl.BlockSpec(memory_space=pltpu.VMEM)
smem = pl.BlockSpec(memory_space=pltpu.SMEM)
in_hbm = pl.BlockSpec(memory_space=pltpu.HBM)


def sds(n):
    return jax.ShapeDtypeStruct((n, lanes), f32)


def params(mib):
    return pltpu.CompilerParams(vmem_limit_bytes=mib << 20)


def pair_scratch(total, sets):
    return [
        pltpu.VMEM((fields * total, lanes), f32),
        pltpu.VMEM((axes * total, lanes), f32),
        pltpu.VMEM((12 + halves * sets, lanes), i32),
        pltpu.SMEM((12 + halves * sets, lanes), i32),
        pltpu.SemaphoreType.DMA,
        pltpu.VMEM((halves * lanes, fields * lanes), f32),
        pltpu.VMEM((halves * lanes, fields * lanes), f32),
        pltpu.VMEM((8, halves * lanes), f32),
        pltpu.VMEM((8, halves * lanes), f32),
        pltpu.VMEM((axes * halves * lanes, lanes), f32),
        pltpu.VMEM((axes * halves * lanes, lanes), f32),
        pltpu.VMEM((axes * 8, halves * lanes), f32),
        pltpu.VMEM((axes * 8, halves * lanes), f32),
    ]


def level_call(rows, last_row, tile):
    total = 3 * rows + 8
    return pl.pallas_call(
        lambda *refs: level_kernel(rows, total, last_row, *refs),
        out_shape=sds(axes * rows),
        in_specs=[vmem],
        out_specs=vmem,
        scratch_shapes=pair_scratch(total, 1),
        compiler_params=params(24),
        name="pairs_inside",
    )(tile)


def column_call(rows, last_row, tile, north, south, g_tile):
    total = 3 * rows + 8
    return pl.pallas_call(
        lambda *refs: column_kernel(rows, total, last_row, *refs),
        out_shape=(sds(axes * rows),) * 3,
        in_specs=[vmem] * 4,
        out_specs=(vmem,) * 3,
        scratch_shapes=pair_scratch(total, 3),
        compiler_params=params(24),
        name="pairs_column",
    )(tile, north, south, g_tile)


def side_call(slots, rows, tiles, east, west, g_tiles):
    total = 3 * rows + 4 * halves * lanes + 8

    def run(*refs):
        side_kernel(slots, rows, total, refs[:3], *refs[3:5], refs[5:8], refs[8:11], *refs[11:])

    return pl.pallas_call(
        run,
        out_shape=(sds(axes * rows),) * 3 + (sds(axes * halves * slots),) * 2,
        in_specs=[vmem] * 8,
        out_specs=(vmem,) * 5,
        scratch_shapes=pair_scratch(total, 2),
        compiler_params=params(32),
        name="pairs_side",
    )(*tiles, east, west, *g_tiles)


def body(locations, solution, cotangent, block_fill, pair_own, pair_offset, pair_block, pair_count):
    points = solution.shape[2]
    slots = pair_own.shape[2]
    rows = points // lanes
    blocks = rows // halves
    own = pair_own.reshape(1, slots)
    offset = pair_offset.reshape(1, slots)
    block = pair_block.reshape(1, slots)
    count = pair_count.reshape(1, 1)
    fill = block_fill.reshape(1, blocks)
    slot_rows = fields * halves * slots + meta_rows
    last_row = lax.axis_size("ty") - 1
    note = pl.pallas_call(
        note_kernel,
        out_shape=sds(meta_rows),
        in_specs=[in_hbm] * 5,
        out_specs=vmem,
        scratch_shapes=[pltpu.SMEM((1, 1), i32), pltpu.VMEM((1, blocks), i32), pltpu.VMEM((3, 1, slots), i32),
                        pltpu.SemaphoreType.DMA((5,))],
        compiler_params=params(60),
        name="note",
    )(count, fill, own, offset, block)
    tile = jnp.concatenate([locations.reshape(axes * rows, lanes), solution.reshape(rows, lanes),
                            cotangent.reshape(rows, lanes), note], axis=0)
    north = shifted(tile, "ty", 1)
    south = shifted(tile, "ty", -1)
    to_east, to_west, origin = pl.pallas_call(
        lambda *refs: pack_kernel(slots, rows, *refs),
        out_shape=(sds(slot_rows), sds(slot_rows), jax.ShapeDtypeStruct((8, halves * lanes), f32)),
        in_specs=[vmem],
        out_specs=(vmem,) * 3,
        compiler_params=params(16),
        name="pack",
    )(tile)
    from_west = shifted(to_east, "tx", 1)
    from_east = shifted(to_west, "tx", -1)
    g_tile = level_call(rows, last_row, tile)
    g_tile, g_north, g_south = column_call(rows, last_row, tile, north, south, g_tile)
    g_north, g_tile, g_south, g_west, g_east = side_call(
        slots, rows, (north, tile, south), from_west, from_east, (g_north, g_tile, g_south))
    back_east = shifted(g_west, "tx", -1)
    back_west = shifted(g_east, "tx", 1)
    back_south = shifted(g_north, "ty", -1)
    back_north = shifted(g_south, "ty", 1)
    out = pl.pallas_call(
        lambda *refs: merge_kernel(slots, rows, *refs),
        out_shape=sds(axes * rows),
        in_specs=[vmem] * 6,
        out_specs=vmem,
        compiler_params=params(16),
        name="merge",
    )(origin, g_tile, back_north, back_south, back_east, back_west)
    return out.reshape(locations.shape)


def solution(mesh):
    placed = (
        P("ty", "tx", None, None),
        P("ty", "tx", None),
        P("ty", "tx", None),
        P("ty", "tx", None),
        P("ty", "tx", None),
        P("ty", "tx", None),
        P("ty", "tx", None),
        P("ty", "tx"),
    )
    return jax.shard_map(
        body, mesh=mesh, in_specs=placed, out_specs=P("ty", "tx", None, None), check_vma=False
    )
```

```python
import jax
import jax.numpy as jnp
from jax import lax
from jax.experimental import pallas as pl
from jax.experimental.pallas import tpu as pltpu
from jax.sharding import PartitionSpec as P

lanes = 128
halves = 2
fields = 5
axes = 3
meta_rows = 8
kinds = 4
kept = 16
bf16 = jnp.bfloat16
f32 = jnp.float32
i32 = jnp.int32


def third(heading):
    return (heading * 11) >> 5


def note_kernel(count_ref, fill_ref, own_ref, offset_ref, block_ref, note_ref, count_s, fill_v, lists_v, sem):
    copies = (
        pltpu.make_async_copy(fill_ref, fill_v, sem.at[0]),
        pltpu.make_async_copy(own_ref, lists_v.at[0], sem.at[1]),
        pltpu.make_async_copy(offset_ref, lists_v.at[1], sem.at[2]),
        pltpu.make_async_copy(block_ref, lists_v.at[2], sem.at[3]),
        pltpu.make_async_copy(count_ref, count_s, sem.at[4]),
    )
    for c in copies:
        c.start()
    for c in copies:
        c.wait()
    own, offset, block = (wide(lists_v[k]) for k in range(3))
    last = lax.broadcasted_iota(i32, own.shape, 1) == own.shape[1] - 1
    own = jnp.where(last, count_s[0, 0], own)
    note_ref[...] = jnp.concatenate([two_rows(x) for x in (fill_v[...], own, offset, block)], axis=0).astype(f32)


def lists_of(ref, rows):
    meta = ref[fields * rows : fields * rows + meta_rows, :].astype(i32)
    parts = [one_row(meta[2 * k : 2 * k + 2]) for k in range(4)]
    return (*parts, parts[1][:, halves * lanes - 1 :])


def rows_dot(x, y, contract):
    return lax.dot_general(x.astype(bf16), y.astype(bf16), (((1,), (contract,)), ((), ())), preferred_element_type=f32)


def split3(x):
    high = x.astype(bf16).astype(f32)
    rest = x - high
    mid = rest.astype(bf16).astype(f32)
    return high, mid, rest - mid


def stacked(rows, width):
    rows = [r.astype(f32) for r in rows]
    return jnp.concatenate(rows + [jnp.zeros((8 - len(rows), width), f32)], axis=0)


def wide(row):
    missing = halves * lanes - row.shape[1]
    return row if missing == 0 else jnp.concatenate([row, jnp.zeros((1, missing), row.dtype)], axis=1)


def one_row(x):
    return jnp.concatenate([x[0:1], x[1:2]], axis=1)


def two_rows(x):
    return jnp.concatenate([x[:, h * lanes : (h + 1) * lanes] for h in range(x.shape[1] // lanes)], axis=0)


def equal_rows(row, count, first=0):
    at = lax.broadcasted_iota(i32, (count, row.shape[1]), 0) + first
    return (row.astype(i32) == at).astype(f32).astype(bf16)


def running(flags):
    size = halves * lanes
    upper = lax.broadcasted_iota(i32, (size, size), 0) <= lax.broadcasted_iota(i32, (size, size), 1)
    return rows_dot(flags, upper.astype(f32), 0)


def pack_kernel(slots, rows, tile_ref, east_ref, west_ref, origin_ref):
    blocks = rows // halves
    size = halves * lanes
    slot_rows = halves * slots
    fill, own, offset, block, count = lists_of(tile_ref, rows)
    live = lax.broadcasted_iota(i32, (1, size), 1) < count
    dr = third(offset)
    dc = offset - 3 * dr
    marks = [live & (dc == want) for want in (2, 0)]
    counts = running(stacked(marks, size))
    picked = equal_rows(own, blocks)
    fill = rows_dot(stacked([fill], size), picked, 0)[0:1]
    values = stacked([block, fill, dr, own + 1], size)
    lane_id = lax.broadcasted_iota(i32, (1, lanes), 1)
    chosen = []
    for side, out_ref in enumerate((east_ref, west_ref)):
        count = counts[side : side + 1]
        place = jnp.where(marks[side], count - 1.0, -1.0)
        moved = equal_rows(place, slots)
        meta = rows_dot(values, moved, 1)
        meta = jnp.concatenate([meta, jnp.zeros((8, size - slots), f32)], axis=1)
        ends = jnp.where(lane_id == 0, count[:, size - 1 :], 0.0)
        out_ref[fields * slot_rows : fields * slot_rows + meta_rows, :] = jnp.concatenate(
            [two_rows(meta[k : k + 1]) for k in range(3)] + [ends, jnp.zeros((1, lanes), f32)], axis=0)
        origin_ref[side : side + 1, :] = meta[3:4] - 1.0
        chosen.append(rows_dot(moved, picked, 1).astype(bf16))
    for f in range(fields):
        data = jnp.concatenate([tile_ref[pl.ds(f * rows + h, blocks, stride=halves), :] for h in range(halves)], axis=1)
        parts = split3(data)
        for pick, out_ref in zip(chosen, (east_ref, west_ref)):
            got = rows_dot(pick, parts[0], 0) + rows_dot(pick, parts[1], 0) + rows_dot(pick, parts[2], 0)
            for h in range(halves):
                out_ref[pl.ds(f * slot_rows + h, slots, stride=halves), :] = got[:, h * lanes : (h + 1) * lanes]


def shape_of(kind):
    steps = (16, 16, 24, 32)[kind]
    return steps, -(-steps // 16), (1, 2, 2, 2)[kind]


def pair_loops(total, spare, table, src, grad, buffers):
    size = halves * lanes

    def word_at(k, at):
        place = table[11, k] + at
        return table[12 + (place >> 7), place & 127]

    def load(index, fill, parts):
        size = parts * lanes
        row_id = lax.broadcasted_iota(i32, (8, size), 0)
        lane_id = lax.broadcasted_iota(i32, (8, size), 1)
        pieces = []
        for h in range(parts):
            got = src[pl.ds(halves * index + h, fields, stride=total), :]
            pieces.append(jnp.concatenate([got, jnp.zeros((8 - fields, lanes), f32)], axis=0))
        x = jnp.concatenate(pieces, axis=1)
        return jnp.where((row_id < axes) | (lane_id < fill), x, 0.0)

    def spread(k, at, mixed, partner):
        steps, parts_a, parts_b = shape_of(k)
        word = word_at(k, at)
        ia, ib = word & 4095, word >> 12
        live = at < table[11, 8 + k]
        a = load(ia, jnp.where(live, table[ia >> 7, ia & 127], 0), parts_a)
        b = load(ib, jnp.where(live, table[ib >> 7, ib & 127], 0), parts_b)
        partner[:, : parts_b * lanes] = b
        zero = jnp.zeros((8, lanes), f32)
        row_b = lax.broadcasted_iota(i32, b.shape, 0)
        ah, am, al = split3(a)
        left = jnp.concatenate([ah, am, al, ah], axis=0).astype(bf16)
        swapped = jnp.where(row_b == 3, jnp.roll(b, -1, axis=0), jnp.where(row_b == 4, jnp.roll(b, 1, axis=0), 0.0))
        swapped = swapped * -20.0
        sh = swapped.astype(bf16).astype(f32)
        sm = swapped - sh
        right = jnp.concatenate([sh, sh, jnp.zeros_like(b), sm], axis=0).astype(bf16)
        row_id = lax.broadcasted_iota(i32, (8, lanes), 0)
        units = [(row_id == f).astype(f32) for f in range(axes)]
        pick = jnp.concatenate([jnp.concatenate([u, u, u, zero], axis=0) for u in units], axis=1).astype(bf16)
        mixed[: parts_a * lanes, : (axes + parts_b) * lanes] = lax.dot_general(
            left, jnp.concatenate([pick, right], axis=1), (((0,), (0,)), ((), ())), preferred_element_type=f32)

    def work(k, mixed, partner, own, far):
        steps, parts_a, parts_b = shape_of(k)
        b_rows = [
            [jnp.broadcast_to(partner[f : f + 1, p * lanes : (p + 1) * lanes], (8, lanes)) for f in range(axes)]
            for p in range(parts_b)
        ]
        sums = [[None] * axes for _ in range(parts_b)]
        for g in range(steps):
            rows = slice(8 * g, 8 * g + 8)
            a_cols = [mixed[rows, f * lanes : (f + 1) * lanes] for f in range(axes)]
            mine = [None] * axes
            for p in range(parts_b):
                diff = [a_cols[f] - b_rows[p][f] for f in range(axes)]
                square = diff[0] * diff[0] + diff[1] * diff[1] + diff[2] * diff[2]
                square = jnp.maximum(square, 1e-30)
                reach = jnp.maximum(1.0 - square * lax.rsqrt(square), 0.0)
                w = (reach * reach) * (reach * mixed[rows, (axes + p) * lanes : (axes + p + 1) * lanes])
                for f in range(axes):
                    push = w * diff[f]
                    mine[f] = push if p == 0 else mine[f] + push
                    sums[p][f] = push if g == 0 else sums[p][f] + push
            for f in range(axes):
                own[f * size + 8 * g : f * size + 8 * g + 8, :] = mine[f]
        for p in range(parts_b):
            for f in range(axes):
                far[8 * f : 8 * f + 8, p * lanes : (p + 1) * lanes] = sums[p][f]

    def finish(k, at, own, far):
        steps, parts_a, parts_b = shape_of(k)
        word = jnp.where(at < 0, spare | (spare << 12), word_at(k, jnp.maximum(at, 0)))
        ia, ib = word & 4095, word >> 12
        for h in range(parts_a):
            count = min(lanes, 8 * steps - h * lanes)
            rows = []
            for f in range(axes):
                part = own[f * size + h * lanes : f * size + h * lanes + count, :]
                if count < lanes:
                    part = jnp.concatenate([part, jnp.zeros((lanes - count, lanes), f32)], axis=0)
                rows.append(jnp.sum(part.T, axis=0, keepdims=True))
            place = pl.ds(halves * ia + h, axes, stride=total)
            grad[place, :] = grad[place, :] + jnp.concatenate(rows, axis=0)
        for p in range(parts_b):
            rows = [jnp.sum(far[8 * f : 8 * f + 8, p * lanes : (p + 1) * lanes], axis=0, keepdims=True) for f in range(axes)]
            place = pl.ds(halves * ib + p, axes, stride=total)
            grad[place, :] = grad[place, :] - jnp.concatenate(rows, axis=0)

    mixed0, mixed1, partner0, partner1, own0, own1, far0, far1 = buffers
    for k in range(kinds):
        turns = (table[11, 8 + k] + 1) // 2

        def turn(t, carry, k=k):
            at = 2 * t
            finish(k, at - 1, own1, far1)
            work(k, mixed0, partner0, own0, far0)
            spread(k, at + 1, mixed1, partner1)
            finish(k, at, own0, far0)
            work(k, mixed1, partner1, own1, far1)
            spread(k, at + 2, mixed0, partner0)
            return carry

        @pl.when(turns > 0)
        def _(k=k, turns=turns, turn=turn):
            spread(k, 0, mixed0, partner0)
            lax.fori_loop(0, turns >> 1, lambda t, c: turn(2 * t + 1, turn(2 * t, c)), 0)
            lax.fori_loop(turns & ~1, turns, turn, 0)
            finish(k, 2 * turns - 1, own1, far1)


def sorted_pairs(entries):
    size = halves * lanes
    found = []
    for a, b, fill_a, fill_b, live in entries:
        size_a, size_b = (fill_a + 63) >> 6, (fill_b + 63) >> 6
        swap = size_a > size_b
        a, b = jnp.where(swap, b, a), jnp.where(swap, a, b)
        size_a, size_b = jnp.where(swap, size_b, size_a), jnp.where(swap, size_a, size_b)
        kind = jnp.maximum(size_a - 2, 0) + jnp.where(size_b > 2, 1, 0)
        marks = [live & (kind == k) for k in range(kinds)]
        counts = running(stacked(marks, size))
        values = stacked([a & 255, a >> 8, b & 255, b >> 8], size)
        found.append((marks, counts, values))
    firsts, totals = [], []
    at = jnp.zeros((1, 1), f32)
    for k in range(kinds):
        firsts.append(at)
        total = sum(counts[k : k + 1, size - 1 :] for _, counts, _ in found)
        totals.append(total)
        at = at + total
    length = size * len(entries)
    ordered = jnp.zeros((8, length), f32)
    before = firsts
    for marks, counts, values in found:
        place = jnp.full((1, size), -1.0, f32)
        for k in range(kinds):
            place = jnp.where(marks[k], before[k] + counts[k : k + 1] - 1.0, place)
        before = [before[k] + counts[k : k + 1, size - 1 :] for k in range(kinds)]
        ordered = ordered + rows_dot(values, equal_rows(place, length), 1)
    ordered = ordered.astype(i32)
    words = ordered[0:1] + (ordered[1:2] << 8) + (ordered[2:3] << 12) + (ordered[3:4] << 20)
    lane_id = lax.broadcasted_iota(i32, (1, lanes), 1)
    bounds = jnp.zeros((1, lanes), i32)
    firsts, totals = [f.astype(i32) for f in firsts], [t.astype(i32) for t in totals]
    for k in range(kinds - 1):
        odd = totals[k] & 1
        totals[k], firsts[k + 1], totals[k + 1] = totals[k] - odd, firsts[k + 1] - odd, totals[k + 1] + odd
    for k in range(kinds):
        bounds = jnp.where(lane_id == k, firsts[k], bounds)
        bounds = jnp.where(lane_id == 8 + k, totals[k], bounds)
    return words, bounds


def as_table(pieces, table_v, table, sem):
    at = 0
    for piece in pieces:
        table_v[at : at + piece.shape[0], :] = piece
        at += piece.shape[0]
    copy = pltpu.make_async_copy(table_v, table, sem)
    copy.start()
    return copy


def fills_of(fills, block):
    return rows_dot(stacked(fills, block.shape[1]), equal_rows(block, halves * lanes), 0).astype(i32)


def column_shares(lists, row, last_row):
    fill, own, offset, block, count = lists
    size = halves * lanes
    live = lax.broadcasted_iota(i32, (1, size), 1) < count
    dr = third(offset)
    column = live & (offset - 3 * dr == 1)
    marks = [column & (dr == k) for k in range(3)]
    rank = running(stacked(marks, size)).astype(i32)
    odd = [(rank[k : k + 1] & 1) == 1 for k in range(3)]
    spare = marks[1] & (rank[1:2] > kept)
    has_north, has_south = row > 0, row < last_row
    to_north = spare & has_north & odd[1]
    to_south = spare & has_south & jnp.logical_not(odd[1])
    inside = marks[1] & jnp.logical_not(to_north | to_south)
    return (
        (marks[0] & odd[0], inside, marks[2] & odd[2]),
        ((marks[0] & jnp.logical_not(odd[0])), to_north),
        ((marks[2] & jnp.logical_not(odd[2])), to_south),
    )


def column_entries(lists, base_row, fills):
    fill, own, offset, block, count = lists
    size = halves * lanes
    a = base_row * size + own
    target = base_row + third(offset) - 1
    b = target * size + block
    near = fills_of(fills, block)
    fill_b = jnp.where(target == 0, near[0:1], jnp.where(target == 1, near[1:2], near[2:3]))
    return a, b, fills_of([fill], own)[0:1], fill_b


def level_kernel(rows, total, last_row, tile_ref, g_tile, src, grad, table_v, table, sem, *buffers):
    blocks = rows // halves
    lists = lists_of(tile_ref, rows)
    mine, _, _ = column_shares(lists, lax.axis_index("ty"), last_row)
    fills = [jnp.zeros_like(lists[0]), lists[0], jnp.zeros_like(lists[0])]
    words, bounds = sorted_pairs([(*column_entries(lists, 1, fills), mine[1])])
    copy = as_table((*map(two_rows, fills), jnp.zeros((5, lanes), i32), bounds, two_rows(words)), table_v, table, sem)
    for f in range(fields):
        src[f * total + rows : f * total + 2 * rows, :] = tile_ref[f * rows : (f + 1) * rows, :]
    for f in range(axes):
        grad[f * total + rows : f * total + 2 * rows, :] = jnp.zeros((rows, lanes), f32)
    copy.wait()
    pair_loops(total, 3 * blocks, table, src, grad, buffers)
    for f in range(axes):
        g_tile[f * rows : (f + 1) * rows, :] = grad[f * total + rows : f * total + 2 * rows, :]


def column_kernel(rows, total, last_row, tile_ref, north_ref, south_ref, start_ref, g_tile, g_north, g_south,
                  src, grad, table_v, table, sem, *buffers):
    blocks = rows // halves
    row = lax.axis_index("ty")
    lists = [lists_of(ref, rows) for ref in (north_ref, tile_ref, south_ref)]
    fills = [l[0] for l in lists]
    shares = [column_shares(l, row + k - 1, last_row) for k, l in enumerate(lists)]
    wanted = (
        shares[0][2][0] | shares[0][2][1],
        shares[1][0][0] | shares[1][0][2],
        shares[2][1][0] | shares[2][1][1],
    )
    words, bounds = sorted_pairs([(*column_entries(l, k, fills), wanted[k]) for k, l in enumerate(lists)])
    copy = as_table((*map(two_rows, fills), jnp.zeros((5, lanes), i32), bounds, two_rows(words)), table_v, table, sem)
    for ref, base in ((north_ref, 0), (tile_ref, rows), (south_ref, 2 * rows)):
        for f in range(fields):
            src[f * total + base : f * total + base + rows, :] = ref[f * rows : (f + 1) * rows, :]
    for f in range(axes):
        grad[f * total : f * total + rows, :] = jnp.zeros((rows, lanes), f32)
        grad[f * total + rows : f * total + 2 * rows, :] = start_ref[f * rows : (f + 1) * rows, :]
        grad[f * total + 2 * rows : f * total + 3 * rows, :] = jnp.zeros((rows, lanes), f32)
    copy.wait()
    pair_loops(total, 3 * blocks, table, src, grad, buffers)
    for ref, base in ((g_north, 0), (g_tile, rows), (g_south, 2 * rows)):
        for f in range(axes):
            ref[f * rows : (f + 1) * rows, :] = grad[f * total + base : f * total + base + rows, :]


def side_kernel(slots, rows, total, tiles, east_ref, west_ref, g_tiles, o_tiles, o_east, o_west,
                src, grad, table_v, table, sem, *buffers):
    blocks = rows // halves
    slot_rows = halves * slots
    size = halves * lanes
    bases = (0, rows, 2 * rows)
    fills = [lists_of(t, rows)[0] for t in tiles]
    east_base, west_base = 6 * lanes, 8 * lanes
    slot_id = lax.broadcasted_iota(i32, (1, size), 1)
    entries, slot_fills = [], []
    for ref, base in ((east_ref, east_base), (west_ref, west_base)):
        meta = ref[fields * slot_rows : fields * slot_rows + meta_rows, :].astype(i32)
        live = slot_id < meta[6:7, 0:1]
        block, fill, dr = (jnp.where(live, one_row(meta[2 * k : 2 * k + 2]), 0) for k in range(3))
        near = fills_of(fills, block)
        fill_b = jnp.where(dr == 0, near[0:1], jnp.where(dr == 1, near[1:2], near[2:3]))
        entries.append((base + slot_id, dr * blocks + block, fill, fill_b, live))
        slot_fills.append(fill)
    words, bounds = sorted_pairs(entries)
    copy = as_table((*map(two_rows, fills), *map(two_rows, slot_fills), jnp.zeros((1, lanes), i32), bounds, two_rows(words)),
                    table_v, table, sem)
    slot_places = ((east_ref, halves * east_base), (west_ref, halves * west_base))
    for ref, base in zip(tiles, bases):
        for f in range(fields):
            src[f * total + base : f * total + base + rows, :] = ref[f * rows : (f + 1) * rows, :]
    for ref, base in slot_places:
        for f in range(fields):
            src[f * total + base : f * total + base + slot_rows, :] = ref[f * slot_rows : (f + 1) * slot_rows, :]
    for ref, base in zip(g_tiles, bases):
        for f in range(axes):
            grad[f * total + base : f * total + base + rows, :] = ref[f * rows : (f + 1) * rows, :]
    for _, base in slot_places:
        for f in range(axes):
            grad[f * total + base : f * total + base + slot_rows, :] = jnp.zeros((slot_rows, lanes), f32)
    copy.wait()
    pair_loops(total, 10 * lanes, table, src, grad, buffers)
    outs = (o_tiles[:2], o_tiles[2:3], o_tiles[3:])
    for refs, base in zip(outs, bases):
        for f in range(axes):
            ref, at = (refs[1], 0) if len(refs) > 1 and f == axes - 1 else (refs[0], f)
            ref[at * rows : (at + 1) * rows, :] = grad[f * total + base : f * total + base + rows, :]
    for ref, (_, base) in zip((o_east, o_west), slot_places):
        for f in range(axes):
            ref[f * slot_rows : (f + 1) * slot_rows, :] = grad[f * total + base : f * total + base + slot_rows, :]


def merge_kernel(slots, rows, origin_ref, g_tile, g_north, g_north_z, g_south, g_south_z, g_east, g_west, out_ref):
    blocks = rows // halves
    slot_rows = halves * slots
    placed = [equal_rows(origin_ref[side : side + 1, :][:, :slots], blocks) for side in range(2)]
    plane = (axes - 1) * rows
    out_ref[:plane, :] = g_tile[:plane, :] + g_north[...] + g_south[...]
    out_ref[plane:, :] = g_tile[plane:, :] + g_north_z[...] + g_south_z[...]
    for f in range(axes):
        got = jnp.zeros((blocks, halves * lanes), f32)
        for place, ref in zip(placed, (g_east, g_west)):
            data = jnp.concatenate([ref[pl.ds(f * slot_rows + h, slots, stride=halves), :] for h in range(halves)], axis=1)
            for part in split3(data):
                got = got + rows_dot(place, part, 0)
        for h in range(halves):
            at = pl.ds(f * rows + h, blocks, stride=halves)
            out_ref[at, :] = out_ref[at, :] + got[:, h * lanes : (h + 1) * lanes]


def shifted(x, axis, by):
    devices = lax.axis_size(axis)
    pairs = [(i, i + by) for i in range(devices) if 0 <= i + by < devices]
    return lax.ppermute(x, axis, pairs)


vmem = pl.BlockSpec(memory_space=pltpu.VMEM)
smem = pl.BlockSpec(memory_space=pltpu.SMEM)
in_hbm = pl.BlockSpec(memory_space=pltpu.HBM)


def sds(n):
    return jax.ShapeDtypeStruct((n, lanes), f32)


def params(mib):
    return pltpu.CompilerParams(vmem_limit_bytes=mib << 20)


def pair_scratch(total, sets):
    return [
        pltpu.VMEM((fields * total, lanes), f32),
        pltpu.VMEM((axes * total, lanes), f32),
        pltpu.VMEM((12 + halves * sets, lanes), i32),
        pltpu.SMEM((12 + halves * sets, lanes), i32),
        pltpu.SemaphoreType.DMA,
        pltpu.VMEM((halves * lanes, fields * lanes), f32),
        pltpu.VMEM((halves * lanes, fields * lanes), f32),
        pltpu.VMEM((8, halves * lanes), f32),
        pltpu.VMEM((8, halves * lanes), f32),
        pltpu.VMEM((axes * halves * lanes, lanes), f32),
        pltpu.VMEM((axes * halves * lanes, lanes), f32),
        pltpu.VMEM((axes * 8, halves * lanes), f32),
        pltpu.VMEM((axes * 8, halves * lanes), f32),
    ]


def level_call(rows, last_row, tile):
    total = 3 * rows + 8
    return pl.pallas_call(
        lambda *refs: level_kernel(rows, total, last_row, *refs),
        out_shape=sds(axes * rows),
        in_specs=[vmem],
        out_specs=vmem,
        scratch_shapes=pair_scratch(total, 1),
        compiler_params=params(24),
        name="pairs_inside",
    )(tile)


def column_call(rows, last_row, tile, north, south, g_tile):
    total = 3 * rows + 8
    return pl.pallas_call(
        lambda *refs: column_kernel(rows, total, last_row, *refs),
        out_shape=(sds(axes * rows),) * 3,
        in_specs=[vmem] * 4,
        out_specs=(vmem,) * 3,
        scratch_shapes=pair_scratch(total, 3),
        compiler_params=params(24),
        name="pairs_column",
    )(tile, north, south, g_tile)


def side_call(slots, rows, tiles, east, west, g_tiles):
    total = 3 * rows + 4 * halves * lanes + 8

    def run(*refs):
        side_kernel(slots, rows, total, refs[:3], *refs[3:5], refs[5:8], refs[8:13], *refs[13:])

    return pl.pallas_call(
        run,
        out_shape=(sds((axes - 1) * rows), sds(rows), sds(axes * rows), sds((axes - 1) * rows), sds(rows))
        + (sds(axes * halves * slots),) * 2,
        in_specs=[vmem] * 8,
        out_specs=(vmem,) * 7,
        scratch_shapes=pair_scratch(total, 2),
        compiler_params=params(32),
        name="pairs_side",
    )(*tiles, east, west, *g_tiles)


def body(locations, solution, cotangent, block_fill, pair_own, pair_offset, pair_block, pair_count):
    points = solution.shape[2]
    slots = pair_own.shape[2]
    rows = points // lanes
    blocks = rows // halves
    own = pair_own.reshape(1, slots)
    offset = pair_offset.reshape(1, slots)
    block = pair_block.reshape(1, slots)
    count = pair_count.reshape(1, 1)
    fill = block_fill.reshape(1, blocks)
    slot_rows = fields * halves * slots + meta_rows
    last_row = lax.axis_size("ty") - 1
    note = pl.pallas_call(
        note_kernel,
        out_shape=sds(meta_rows),
        in_specs=[in_hbm] * 5,
        out_specs=vmem,
        scratch_shapes=[pltpu.SMEM((1, 1), i32), pltpu.VMEM((1, blocks), i32), pltpu.VMEM((3, 1, slots), i32),
                        pltpu.SemaphoreType.DMA((5,))],
        compiler_params=params(60),
        name="note",
    )(count, fill, own, offset, block)
    tile = jnp.concatenate([locations.reshape(axes * rows, lanes), solution.reshape(rows, lanes),
                            cotangent.reshape(rows, lanes), note], axis=0)
    north = shifted(tile, "ty", 1)
    south = shifted(tile, "ty", -1)
    to_east, to_west, origin = pl.pallas_call(
        lambda *refs: pack_kernel(slots, rows, *refs),
        out_shape=(sds(slot_rows), sds(slot_rows), jax.ShapeDtypeStruct((8, halves * lanes), f32)),
        in_specs=[vmem],
        out_specs=(vmem,) * 3,
        compiler_params=params(16),
        name="pack",
    )(tile)
    from_west = shifted(to_east, "tx", 1)
    from_east = shifted(to_west, "tx", -1)
    g_tile = level_call(rows, last_row, tile)
    g_tile, g_north, g_south = column_call(rows, last_row, tile, north, south, g_tile)
    *g_north, g_tile, g_south, g_south_z, g_west, g_east = side_call(
        slots, rows, (north, tile, south), from_west, from_east, (g_north, g_tile, g_south))
    back_east = shifted(g_west, "tx", -1)
    back_west = shifted(g_east, "tx", 1)
    back_south = [shifted(g, "ty", -1) for g in g_north]
    back_north = [shifted(g, "ty", 1) for g in (g_south, g_south_z)]
    out = pl.pallas_call(
        lambda *refs: merge_kernel(slots, rows, *refs),
        out_shape=sds(axes * rows),
        in_specs=[vmem] * 8,
        out_specs=vmem,
        compiler_params=params(16),
        name="merge",
    )(origin, g_tile, *back_north, *back_south, back_east, back_west)
    return out.reshape(locations.shape)


def solution(mesh):
    placed = (
        P("ty", "tx", None, None),
        P("ty", "tx", None),
        P("ty", "tx", None),
        P("ty", "tx", None),
        P("ty", "tx", None),
        P("ty", "tx", None),
        P("ty", "tx", None),
        P("ty", "tx"),
    )
    return jax.shard_map(
        body, mesh=mesh, in_specs=placed, out_specs=P("ty", "tx", None, None), check_vma=False
    )
```

```python
import jax
import jax.numpy as jnp
from jax import lax
from jax.experimental import pallas as pl
from jax.experimental.pallas import tpu as pltpu
from jax.sharding import PartitionSpec as P

lanes = 128
halves = 2
fields = 5
axes = 3
meta_rows = 8
kinds = 4
kept = 28
bf16 = jnp.bfloat16
f32 = jnp.float32
i32 = jnp.int32


def third(heading):
    return (heading * 11) >> 5


def note_kernel(count_ref, fill_ref, own_ref, offset_ref, block_ref, note_ref, count_s, fill_v, lists_v, sem):
    copies = (
        pltpu.make_async_copy(fill_ref, fill_v, sem.at[0]),
        pltpu.make_async_copy(own_ref, lists_v.at[0], sem.at[1]),
        pltpu.make_async_copy(offset_ref, lists_v.at[1], sem.at[2]),
        pltpu.make_async_copy(block_ref, lists_v.at[2], sem.at[3]),
        pltpu.make_async_copy(count_ref, count_s, sem.at[4]),
    )
    for c in copies:
        c.start()
    for c in copies:
        c.wait()
    own, offset, block = (wide(lists_v[k]) for k in range(3))
    last = lax.broadcasted_iota(i32, own.shape, 1) == own.shape[1] - 1
    own = jnp.where(last, count_s[0, 0], own)
    note_ref[...] = jnp.concatenate([two_rows(x) for x in (fill_v[...], own, offset, block)], axis=0).astype(f32)


def lists_of(ref, rows):
    meta = ref[fields * rows : fields * rows + meta_rows, :].astype(i32)
    parts = [one_row(meta[2 * k : 2 * k + 2]) for k in range(4)]
    return (*parts, parts[1][:, halves * lanes - 1 :])


def rows_dot(x, y, contract):
    return lax.dot_general(x.astype(bf16), y.astype(bf16), (((1,), (contract,)), ((), ())), preferred_element_type=f32)


def split3(x):
    high = x.astype(bf16).astype(f32)
    rest = x - high
    mid = rest.astype(bf16).astype(f32)
    return high, mid, rest - mid


def stacked(rows, width):
    rows = [r.astype(f32) for r in rows]
    return jnp.concatenate(rows + [jnp.zeros((8 - len(rows), width), f32)], axis=0)


def wide(row):
    missing = halves * lanes - row.shape[1]
    return row if missing == 0 else jnp.concatenate([row, jnp.zeros((1, missing), row.dtype)], axis=1)


def one_row(x):
    return jnp.concatenate([x[0:1], x[1:2]], axis=1)


def two_rows(x):
    return jnp.concatenate([x[:, h * lanes : (h + 1) * lanes] for h in range(x.shape[1] // lanes)], axis=0)


def equal_rows(row, count, first=0):
    at = lax.broadcasted_iota(i32, (count, row.shape[1]), 0) + first
    return (row.astype(i32) == at).astype(f32).astype(bf16)


def running(flags):
    size = halves * lanes
    upper = lax.broadcasted_iota(i32, (size, size), 0) <= lax.broadcasted_iota(i32, (size, size), 1)
    return rows_dot(flags, upper.astype(f32), 0)


def pack_kernel(slots, rows, tile_ref, east_ref, west_ref, origin_ref):
    blocks = rows // halves
    size = halves * lanes
    slot_rows = halves * slots
    fill, own, offset, block, count = lists_of(tile_ref, rows)
    live = lax.broadcasted_iota(i32, (1, size), 1) < count
    dr = third(offset)
    dc = offset - 3 * dr
    marks = [live & (dc == want) for want in (2, 0)]
    counts = running(stacked(marks, size))
    picked = equal_rows(own, blocks)
    fill = rows_dot(stacked([fill], size), picked, 0)[0:1]
    values = stacked([block, fill, dr, own + 1], size)
    lane_id = lax.broadcasted_iota(i32, (1, lanes), 1)
    chosen = []
    for side, out_ref in enumerate((east_ref, west_ref)):
        count = counts[side : side + 1]
        place = jnp.where(marks[side], count - 1.0, -1.0)
        moved = equal_rows(place, slots)
        meta = rows_dot(values, moved, 1)
        meta = jnp.concatenate([meta, jnp.zeros((8, size - slots), f32)], axis=1)
        ends = jnp.where(lane_id == 0, count[:, size - 1 :], 0.0)
        out_ref[fields * slot_rows : fields * slot_rows + meta_rows, :] = jnp.concatenate(
            [two_rows(meta[k : k + 1]) for k in range(3)] + [ends, jnp.zeros((1, lanes), f32)], axis=0)
        origin_ref[side : side + 1, :] = meta[3:4] - 1.0
        chosen.append(rows_dot(moved, picked, 1).astype(bf16))
    for f in range(fields):
        data = jnp.concatenate([tile_ref[pl.ds(f * rows + h, blocks, stride=halves), :] for h in range(halves)], axis=1)
        parts = split3(data)
        for pick, out_ref in zip(chosen, (east_ref, west_ref)):
            got = rows_dot(pick, parts[0], 0) + rows_dot(pick, parts[1], 0) + rows_dot(pick, parts[2], 0)
            for h in range(halves):
                out_ref[pl.ds(f * slot_rows + h, slots, stride=halves), :] = got[:, h * lanes : (h + 1) * lanes]


def shape_of(kind):
    steps = (16, 16, 24, 32)[kind]
    return steps, -(-steps // 16), (1, 2, 2, 2)[kind]


def pair_loops(total, spare, table, src, grad, buffers):
    size = halves * lanes

    def word_at(k, at):
        place = table[11, k] + at
        return table[12 + (place >> 7), place & 127]

    def load(index, fill, parts):
        size = parts * lanes
        row_id = lax.broadcasted_iota(i32, (8, size), 0)
        lane_id = lax.broadcasted_iota(i32, (8, size), 1)
        pieces = []
        for h in range(parts):
            got = src[pl.ds(halves * index + h, fields, stride=total), :]
            pieces.append(jnp.concatenate([got, jnp.zeros((8 - fields, lanes), f32)], axis=0))
        x = jnp.concatenate(pieces, axis=1)
        return jnp.where((row_id < axes) | (lane_id < fill), x, 0.0)

    def spread(k, at, mixed, partner):
        steps, parts_a, parts_b = shape_of(k)
        word = word_at(k, at)
        ia, ib = word & 4095, word >> 12
        live = at < table[11, 8 + k]
        a = load(ia, jnp.where(live, table[ia >> 7, ia & 127], 0), parts_a)
        b = load(ib, jnp.where(live, table[ib >> 7, ib & 127], 0), parts_b)
        partner[:, : parts_b * lanes] = b
        zero = jnp.zeros((8, lanes), f32)
        row_b = lax.broadcasted_iota(i32, b.shape, 0)
        ah, am, al = split3(a)
        left = jnp.concatenate([ah, am, al, ah], axis=0).astype(bf16)
        swapped = jnp.where(row_b == 3, jnp.roll(b, -1, axis=0), jnp.where(row_b == 4, jnp.roll(b, 1, axis=0), 0.0))
        swapped = swapped * -20.0
        sh = swapped.astype(bf16).astype(f32)
        sm = swapped - sh
        right = jnp.concatenate([sh, sh, jnp.zeros_like(b), sm], axis=0).astype(bf16)
        row_id = lax.broadcasted_iota(i32, (8, lanes), 0)
        units = [(row_id == f).astype(f32) for f in range(axes)]
        pick = jnp.concatenate([jnp.concatenate([u, u, u, zero], axis=0) for u in units], axis=1).astype(bf16)
        mixed[: parts_a * lanes, : (axes + parts_b) * lanes] = lax.dot_general(
            left, jnp.concatenate([pick, right], axis=1), (((0,), (0,)), ((), ())), preferred_element_type=f32)

    def work(k, mixed, partner, own, far):
        steps, parts_a, parts_b = shape_of(k)
        b_rows = [
            [jnp.broadcast_to(partner[f : f + 1, p * lanes : (p + 1) * lanes], (8, lanes)) for f in range(axes)]
            for p in range(parts_b)
        ]
        sums = [[None] * axes for _ in range(parts_b)]
        for g in range(steps):
            rows = slice(8 * g, 8 * g + 8)
            a_cols = [mixed[rows, f * lanes : (f + 1) * lanes] for f in range(axes)]
            mine = [None] * axes
            for p in range(parts_b):
                diff = [a_cols[f] - b_rows[p][f] for f in range(axes)]
                square = diff[0] * diff[0] + diff[1] * diff[1] + diff[2] * diff[2]
                square = jnp.maximum(square, 1e-30)
                reach = jnp.maximum(1.0 - square * lax.rsqrt(square), 0.0)
                w = (reach * reach) * (reach * mixed[rows, (axes + p) * lanes : (axes + p + 1) * lanes])
                for f in range(axes):
                    push = w * diff[f]
                    mine[f] = push if p == 0 else mine[f] + push
                    sums[p][f] = push if g == 0 else sums[p][f] + push
            for f in range(axes):
                own[f * size + 8 * g : f * size + 8 * g + 8, :] = mine[f]
        for p in range(parts_b):
            for f in range(axes):
                far[8 * f : 8 * f + 8, p * lanes : (p + 1) * lanes] = sums[p][f]

    def finish(k, at, own, far):
        steps, parts_a, parts_b = shape_of(k)
        word = jnp.where(at < 0, spare | (spare << 12), word_at(k, jnp.maximum(at, 0)))
        ia, ib = word & 4095, word >> 12
        for h in range(parts_a):
            count = min(lanes, 8 * steps - h * lanes)
            rows = []
            for f in range(axes):
                part = own[f * size + h * lanes : f * size + h * lanes + count, :]
                if count < lanes:
                    part = jnp.concatenate([part, jnp.zeros((lanes - count, lanes), f32)], axis=0)
                rows.append(jnp.sum(part.T, axis=0, keepdims=True))
            place = pl.ds(halves * ia + h, axes, stride=total)
            grad[place, :] = grad[place, :] + jnp.concatenate(rows, axis=0)
        for p in range(parts_b):
            rows = [jnp.sum(far[8 * f : 8 * f + 8, p * lanes : (p + 1) * lanes], axis=0, keepdims=True) for f in range(axes)]
            place = pl.ds(halves * ib + p, axes, stride=total)
            grad[place, :] = grad[place, :] - jnp.concatenate(rows, axis=0)

    mixed0, mixed1, partner0, partner1, own0, own1, far0, far1 = buffers
    for k in range(kinds):
        turns = (table[11, 8 + k] + 1) // 2

        def turn(t, carry, k=k):
            at = 2 * t
            finish(k, at - 1, own1, far1)
            work(k, mixed0, partner0, own0, far0)
            spread(k, at + 1, mixed1, partner1)
            finish(k, at, own0, far0)
            work(k, mixed1, partner1, own1, far1)
            spread(k, at + 2, mixed0, partner0)
            return carry

        spread(k, 0, mixed0, partner0)
        lax.fori_loop(0, turns >> 1, lambda t, c, turn=turn: turn(2 * t + 1, turn(2 * t, c)), 0)
        lax.fori_loop(turns & ~1, turns, turn, 0)
        finish(k, 2 * turns - 1, own1, far1)


def sorted_pairs(entries):
    size = halves * lanes
    found = []
    for a, b, fill_a, fill_b, live in entries:
        size_a, size_b = (fill_a + 63) >> 6, (fill_b + 63) >> 6
        swap = size_a > size_b
        a, b = jnp.where(swap, b, a), jnp.where(swap, a, b)
        size_a, size_b = jnp.where(swap, size_b, size_a), jnp.where(swap, size_a, size_b)
        kind = jnp.maximum(size_a - 2, 0) + jnp.where(size_b > 2, 1, 0)
        marks = [live & (kind == k) for k in range(kinds)]
        counts = running(stacked(marks, size))
        values = stacked([a & 255, a >> 8, b & 255, b >> 8], size)
        found.append((marks, counts, values))
    firsts, totals = [], []
    at = jnp.zeros((1, 1), f32)
    for k in range(kinds):
        firsts.append(at)
        total = sum(counts[k : k + 1, size - 1 :] for _, counts, _ in found)
        totals.append(total)
        at = at + total
    length = size * len(entries)
    ordered = jnp.zeros((8, length), f32)
    before = firsts
    for marks, counts, values in found:
        place = jnp.full((1, size), -1.0, f32)
        for k in range(kinds):
            place = jnp.where(marks[k], before[k] + counts[k : k + 1] - 1.0, place)
        before = [before[k] + counts[k : k + 1, size - 1 :] for k in range(kinds)]
        ordered = ordered + rows_dot(values, equal_rows(place, length), 1)
    ordered = ordered.astype(i32)
    words = ordered[0:1] + (ordered[1:2] << 8) + (ordered[2:3] << 12) + (ordered[3:4] << 20)
    lane_id = lax.broadcasted_iota(i32, (1, lanes), 1)
    bounds = jnp.zeros((1, lanes), i32)
    firsts, totals = [f.astype(i32) for f in firsts], [t.astype(i32) for t in totals]
    for k in range(kinds - 1):
        odd = totals[k] & 1
        totals[k], firsts[k + 1], totals[k + 1] = totals[k] - odd, firsts[k + 1] - odd, totals[k + 1] + odd
    for k in range(kinds):
        bounds = jnp.where(lane_id == k, firsts[k], bounds)
        bounds = jnp.where(lane_id == 8 + k, totals[k], bounds)
    return words, bounds


def as_table(pieces, table_v, table, sem):
    at = 0
    for piece in pieces:
        table_v[at : at + piece.shape[0], :] = piece
        at += piece.shape[0]
    copy = pltpu.make_async_copy(table_v, table, sem)
    copy.start()
    return copy


def fills_of(fills, block):
    return rows_dot(stacked(fills, block.shape[1]), equal_rows(block, halves * lanes), 0).astype(i32)


def column_shares(lists, row, last_row):
    fill, own, offset, block, count = lists
    size = halves * lanes
    live = lax.broadcasted_iota(i32, (1, size), 1) < count
    dr = third(offset)
    column = live & (offset - 3 * dr == 1)
    marks = [column & (dr == k) for k in range(3)]
    rank = running(stacked(marks, size)).astype(i32)
    odd = [(rank[k : k + 1] & 1) == 1 for k in range(3)]
    spare = marks[1] & (rank[1:2] > kept)
    has_north, has_south = row > 0, row < last_row
    to_north = spare & has_north & odd[1]
    to_south = spare & has_south & jnp.logical_not(odd[1])
    inside = marks[1] & jnp.logical_not(to_north | to_south)
    return (
        (marks[0] & odd[0], inside, marks[2] & odd[2]),
        ((marks[0] & jnp.logical_not(odd[0])), to_north),
        ((marks[2] & jnp.logical_not(odd[2])), to_south),
    )


def column_entries(lists, base_row, fills):
    fill, own, offset, block, count = lists
    size = halves * lanes
    a = base_row * size + own
    target = base_row + third(offset) - 1
    b = target * size + block
    near = fills_of(fills, block)
    fill_b = jnp.where(target == 0, near[0:1], jnp.where(target == 1, near[1:2], near[2:3]))
    return a, b, fills_of([fill], own)[0:1], fill_b


def level_kernel(rows, total, last_row, tile_ref, g_tile, src, grad, table_v, table, sem, *buffers):
    blocks = rows // halves
    lists = lists_of(tile_ref, rows)
    mine, _, _ = column_shares(lists, lax.axis_index("ty"), last_row)
    fills = [jnp.zeros_like(lists[0]), lists[0], jnp.zeros_like(lists[0])]
    words, bounds = sorted_pairs([(*column_entries(lists, 1, fills), mine[1])])
    copy = as_table((*map(two_rows, fills), jnp.zeros((5, lanes), i32), bounds, two_rows(words)), table_v, table, sem)
    for f in range(fields):
        src[f * total + rows : f * total + 2 * rows, :] = tile_ref[f * rows : (f + 1) * rows, :]
    for f in range(axes):
        grad[f * total + rows : f * total + 2 * rows, :] = jnp.zeros((rows, lanes), f32)
    copy.wait()
    pair_loops(total, 3 * blocks, table, src, grad, buffers)
    for f in range(axes):
        g_tile[f * rows : (f + 1) * rows, :] = grad[f * total + rows : f * total + 2 * rows, :]


def column_kernel(rows, total, last_row, tile_ref, north_ref, south_ref, start_ref, g_tile, g_north, g_south,
                  src, grad, table_v, table, sem, *buffers):
    blocks = rows // halves
    row = lax.axis_index("ty")
    lists = [lists_of(ref, rows) for ref in (north_ref, tile_ref, south_ref)]
    fills = [l[0] for l in lists]
    shares = [column_shares(l, row + k - 1, last_row) for k, l in enumerate(lists)]
    wanted = (
        shares[0][2][0] | shares[0][2][1],
        shares[1][0][0] | shares[1][0][2],
        shares[2][1][0] | shares[2][1][1],
    )
    words, bounds = sorted_pairs([(*column_entries(l, k, fills), wanted[k]) for k, l in enumerate(lists)])
    copy = as_table((*map(two_rows, fills), jnp.zeros((5, lanes), i32), bounds, two_rows(words)), table_v, table, sem)
    for ref, base in ((north_ref, 0), (tile_ref, rows), (south_ref, 2 * rows)):
        for f in range(fields):
            src[f * total + base : f * total + base + rows, :] = ref[f * rows : (f + 1) * rows, :]
    for f in range(axes):
        grad[f * total : f * total + rows, :] = jnp.zeros((rows, lanes), f32)
        grad[f * total + rows : f * total + 2 * rows, :] = start_ref[f * rows : (f + 1) * rows, :]
        grad[f * total + 2 * rows : f * total + 3 * rows, :] = jnp.zeros((rows, lanes), f32)
    copy.wait()
    pair_loops(total, 3 * blocks, table, src, grad, buffers)
    for ref, base in ((g_north, 0), (g_tile, rows), (g_south, 2 * rows)):
        for f in range(axes):
            ref[f * rows : (f + 1) * rows, :] = grad[f * total + base : f * total + base + rows, :]


def side_kernel(slots, rows, total, tiles, east_ref, west_ref, g_tiles, o_tiles, o_east, o_west,
                src, grad, table_v, table, sem, *buffers):
    blocks = rows // halves
    slot_rows = halves * slots
    size = halves * lanes
    bases = (0, rows, 2 * rows)
    fills = [lists_of(t, rows)[0] for t in tiles]
    east_base, west_base = 6 * lanes, 8 * lanes
    slot_id = lax.broadcasted_iota(i32, (1, size), 1)
    entries, slot_fills = [], []
    for ref, base in ((east_ref, east_base), (west_ref, west_base)):
        meta = ref[fields * slot_rows : fields * slot_rows + meta_rows, :].astype(i32)
        live = slot_id < meta[6:7, 0:1]
        block, fill, dr = (jnp.where(live, one_row(meta[2 * k : 2 * k + 2]), 0) for k in range(3))
        near = fills_of(fills, block)
        fill_b = jnp.where(dr == 0, near[0:1], jnp.where(dr == 1, near[1:2], near[2:3]))
        entries.append((base + slot_id, dr * blocks + block, fill, fill_b, live))
        slot_fills.append(fill)
    words, bounds = sorted_pairs(entries)
    copy = as_table((*map(two_rows, fills), *map(two_rows, slot_fills), jnp.zeros((1, lanes), i32), bounds, two_rows(words)),
                    table_v, table, sem)
    slot_places = ((east_ref, halves * east_base), (west_ref, halves * west_base))
    for ref, base in zip(tiles, bases):
        for f in range(fields):
            src[f * total + base : f * total + base + rows, :] = ref[f * rows : (f + 1) * rows, :]
    for ref, base in slot_places:
        for f in range(fields):
            src[f * total + base : f * total + base + slot_rows, :] = ref[f * slot_rows : (f + 1) * slot_rows, :]
    for ref, base in zip(g_tiles, bases):
        for f in range(axes):
            grad[f * total + base : f * total + base + rows, :] = ref[f * rows : (f + 1) * rows, :]
    for _, base in slot_places:
        for f in range(axes):
            grad[f * total + base : f * total + base + slot_rows, :] = jnp.zeros((slot_rows, lanes), f32)
    copy.wait()
    pair_loops(total, 10 * lanes, table, src, grad, buffers)
    outs = (o_tiles[:2], o_tiles[2:3], o_tiles[3:])
    for refs, base in zip(outs, bases):
        for f in range(axes):
            ref, at = (refs[1], 0) if len(refs) > 1 and f == axes - 1 else (refs[0], f)
            ref[at * rows : (at + 1) * rows, :] = grad[f * total + base : f * total + base + rows, :]
    for ref, (_, base) in zip((o_east, o_west), slot_places):
        for f in range(axes):
            ref[f * slot_rows : (f + 1) * slot_rows, :] = grad[f * total + base : f * total + base + slot_rows, :]


def merge_kernel(slots, rows, origin_ref, g_tile, g_north, g_north_z, g_south, g_south_z, g_east, g_west, out_ref):
    blocks = rows // halves
    slot_rows = halves * slots
    placed = [equal_rows(origin_ref[side : side + 1, :][:, :slots], blocks) for side in range(2)]
    plane = (axes - 1) * rows
    out_ref[:plane, :] = g_tile[:plane, :] + g_north[...] + g_south[...]
    out_ref[plane:, :] = g_tile[plane:, :] + g_north_z[...] + g_south_z[...]
    for f in range(axes):
        got = jnp.zeros((blocks, halves * lanes), f32)
        for place, ref in zip(placed, (g_east, g_west)):
            data = jnp.concatenate([ref[pl.ds(f * slot_rows + h, slots, stride=halves), :] for h in range(halves)], axis=1)
            for part in split3(data):
                got = got + rows_dot(place, part, 0)
        for h in range(halves):
            at = pl.ds(f * rows + h, blocks, stride=halves)
            out_ref[at, :] = out_ref[at, :] + got[:, h * lanes : (h + 1) * lanes]


def shifted(x, axis, by):
    devices = lax.axis_size(axis)
    pairs = [(i, i + by) for i in range(devices) if 0 <= i + by < devices]
    return lax.ppermute(x, axis, pairs)


vmem = pl.BlockSpec(memory_space=pltpu.VMEM)
smem = pl.BlockSpec(memory_space=pltpu.SMEM)
in_hbm = pl.BlockSpec(memory_space=pltpu.HBM)


def sds(n):
    return jax.ShapeDtypeStruct((n, lanes), f32)


def params(mib):
    return pltpu.CompilerParams(vmem_limit_bytes=mib << 20)


def pair_scratch(total, sets):
    return [
        pltpu.VMEM((fields * total, lanes), f32),
        pltpu.VMEM((axes * total, lanes), f32),
        pltpu.VMEM((12 + halves * sets, lanes), i32),
        pltpu.SMEM((12 + halves * sets, lanes), i32),
        pltpu.SemaphoreType.DMA,
        pltpu.VMEM((halves * lanes, fields * lanes), f32),
        pltpu.VMEM((halves * lanes, fields * lanes), f32),
        pltpu.VMEM((8, halves * lanes), f32),
        pltpu.VMEM((8, halves * lanes), f32),
        pltpu.VMEM((axes * halves * lanes, lanes), f32),
        pltpu.VMEM((axes * halves * lanes, lanes), f32),
        pltpu.VMEM((axes * 8, halves * lanes), f32),
        pltpu.VMEM((axes * 8, halves * lanes), f32),
    ]


def level_call(rows, last_row, tile):
    total = 3 * rows + 8
    return pl.pallas_call(
        lambda *refs: level_kernel(rows, total, last_row, *refs),
        out_shape=sds(axes * rows),
        in_specs=[vmem],
        out_specs=vmem,
        scratch_shapes=pair_scratch(total, 1),
        compiler_params=params(24),
        name="pairs_inside",
    )(tile)


def column_call(rows, last_row, tile, north, south, g_tile):
    total = 3 * rows + 8
    return pl.pallas_call(
        lambda *refs: column_kernel(rows, total, last_row, *refs),
        out_shape=(sds(axes * rows),) * 3,
        in_specs=[vmem] * 4,
        out_specs=(vmem,) * 3,
        scratch_shapes=pair_scratch(total, 3),
        compiler_params=params(24),
        name="pairs_column",
    )(tile, north, south, g_tile)


def side_call(slots, rows, tiles, east, west, g_tiles):
    total = 3 * rows + 4 * halves * lanes + 8

    def run(*refs):
        side_kernel(slots, rows, total, refs[:3], *refs[3:5], refs[5:8], refs[8:13], *refs[13:])

    return pl.pallas_call(
        run,
        out_shape=(sds((axes - 1) * rows), sds(rows), sds(axes * rows), sds((axes - 1) * rows), sds(rows))
        + (sds(axes * halves * slots),) * 2,
        in_specs=[vmem] * 8,
        out_specs=(vmem,) * 7,
        scratch_shapes=pair_scratch(total, 2),
        compiler_params=params(32),
        name="pairs_side",
    )(*tiles, east, west, *g_tiles)


def body(locations, solution, cotangent, block_fill, pair_own, pair_offset, pair_block, pair_count):
    points = solution.shape[2]
    slots = pair_own.shape[2]
    rows = points // lanes
    blocks = rows // halves
    own = pair_own.reshape(1, slots)
    offset = pair_offset.reshape(1, slots)
    block = pair_block.reshape(1, slots)
    count = pair_count.reshape(1, 1)
    fill = block_fill.reshape(1, blocks)
    slot_rows = fields * halves * slots + meta_rows
    last_row = lax.axis_size("ty") - 1
    note = pl.pallas_call(
        note_kernel,
        out_shape=sds(meta_rows),
        in_specs=[in_hbm] * 5,
        out_specs=vmem,
        scratch_shapes=[pltpu.SMEM((1, 1), i32), pltpu.VMEM((1, blocks), i32), pltpu.VMEM((3, 1, slots), i32),
                        pltpu.SemaphoreType.DMA((5,))],
        compiler_params=params(60),
        name="note",
    )(count, fill, own, offset, block)
    tile = jnp.concatenate([locations.reshape(axes * rows, lanes), solution.reshape(rows, lanes),
                            cotangent.reshape(rows, lanes), note], axis=0)
    north = shifted(tile, "ty", 1)
    south = shifted(tile, "ty", -1)
    to_east, to_west, origin = pl.pallas_call(
        lambda *refs: pack_kernel(slots, rows, *refs),
        out_shape=(sds(slot_rows), sds(slot_rows), jax.ShapeDtypeStruct((8, halves * lanes), f32)),
        in_specs=[vmem],
        out_specs=(vmem,) * 3,
        compiler_params=params(16),
        name="pack",
    )(tile)
    from_west = shifted(to_east, "tx", 1)
    from_east = shifted(to_west, "tx", -1)
    g_tile = level_call(rows, last_row, tile)
    g_tile, g_north, g_south = column_call(rows, last_row, tile, north, south, g_tile)
    *g_north, g_tile, g_south, g_south_z, g_west, g_east = side_call(
        slots, rows, (north, tile, south), from_west, from_east, (g_north, g_tile, g_south))
    back_east = shifted(g_west, "tx", -1)
    back_west = shifted(g_east, "tx", 1)
    back_south = [shifted(g, "ty", -1) for g in g_north]
    back_north = [shifted(g, "ty", 1) for g in (g_south, g_south_z)]
    out = pl.pallas_call(
        lambda *refs: merge_kernel(slots, rows, *refs),
        out_shape=sds(axes * rows),
        in_specs=[vmem] * 8,
        out_specs=vmem,
        compiler_params=params(16),
        name="merge",
    )(origin, g_tile, *back_north, *back_south, back_east, back_west)
    return out.reshape(locations.shape)


def solution(mesh):
    placed = (
        P("ty", "tx", None, None),
        P("ty", "tx", None),
        P("ty", "tx", None),
        P("ty", "tx", None),
        P("ty", "tx", None),
        P("ty", "tx", None),
        P("ty", "tx", None),
        P("ty", "tx"),
    )
    return jax.shard_map(
        body, mesh=mesh, in_specs=placed, out_specs=P("ty", "tx", None, None), check_vma=False
    )
```
